32 devices in a mesh: groups: 2 (over x), seq: 16 (over z, y, core).
Axes of the slice: x: 2, y: 2, z: 4, core: 2. Of those that a mesh axis runs over, the one named last changes fastest.
Arguments:
- hidden: bfloat16 [768, 3072], P(('groups', 'seq')), parts along dimension 0, may hold values from -4 to 4
- latents: float32 [768, 64], P(('groups', 'seq')), parts along dimension 0, may hold values from -6 to 6
- base_qkv: bfloat16 [3, 768, 1536], P(None, ('groups', 'seq')), parts along dimension 1, may hold values from -8 to 8
- control_qkv: bfloat16 [3, 768, 1536], P(None, ('groups', 'seq')), parts along dimension 1, may hold values from -8 to 8
- step_index: int32 [1], replicated, may hold values from 0 to 49
- w_join: bfloat16 [3072, 3072], P(None, 'seq'), may hold values from -0.109375 to 0.109375
- w_mod: bfloat16 [512, 6144], replicated, may hold values from -0.25 to 0.25
- w_out: bfloat16 [3072, 64], replicated, may hold values from -0.109375 to 0.109375
Outputs:
- hidden_next: bfloat16 [768, 3072], P(('groups', 'seq')), parts along dimension 0
- velocity: float32 [768, 64], P(('groups', 'seq')), parts along dimension 0
- latents_next: float32 [768, 64], P(('groups', 'seq')), parts along dimension 0
The draws below stay inside these ranges and needn't reach their ends.
There are 2 independent parts, one for each index of `groups`. The reference program is written for one: setup_inputs(seed, part) draws one part's arguments, and reference() takes and returns one part's arrays. A program takes and returns all parts, laid end to end along the dimension named above; an argument that names none is the same for every part. Nothing has to cross between parts.
All inputs are finite; a program needn't handle non-finite values.
Results may differ from the reference program's by a relative error of at most 0.0065.
Values may be sent and summed in bfloat16 or wider, within the bound.
A program may use at most 128 MiB of HBM per device.

```python
import math
import jax
import jax.numpy as jnp
from jax import lax

D = 3072
HD = 64
PATCH = 64
TEMB = 512
HEADS = 24
STEPS = 50
ATT = 1536
SEQ_LEN = 384


def shared_draw(key, marker):
    base_key = jax.random.fold_in(key, marker)
    subkeys = jax.random.split(base_key, 1)
    spread = jnp.array([1.3, 1.3, 1.0], jnp.float32)[:, None, None]
    values = jnp.clip(jax.random.normal(subkeys[0], (3, SEQ_LEN, ATT), jnp.float32), -6.0, 6.0) * spread
    return values.astype(jnp.bfloat16)


def draw_base_qkv(key, part):
    return shared_draw(key, 17)


def draw_control_qkv(key, part):
    return shared_draw(key, 29)


def steps_of(stream_key, shape, cuts, low, high):
    level = 1.0
    for axis_at, shards_of in cuts:
        heights = jax.random.uniform(jax.random.fold_in(jax.random.fold_in(stream_key, 6), axis_at), (shards_of,), jnp.float32, low / len(cuts), high / len(cuts))
        level = level * jnp.repeat(jnp.exp(heights), shape[axis_at] // shards_of).reshape((-1,) + (1,) * (len(shape) - 1 - axis_at))
    return level


def normal_values(stream_key, shape, scale, most, cuts=(), dtype=jnp.bfloat16):
    drawn = jax.random.normal(stream_key, shape, jnp.float32) * scale
    if len(cuts) > 0:
        drawn = steps_of(stream_key, shape, cuts, -0.22, 0.18) * drawn
    return jnp.clip(drawn, min=-most, max=most).astype(dtype)


def setup_inputs(seed: int = 0, part: int = 0) -> dict:
    splits = jax.random.split(jax.random.key(seed), 9)
    own_keys = jax.random.split(jax.random.fold_in(splits[8], part), 9)
    return {
        "hidden": normal_values(own_keys[0], (SEQ_LEN, D), 0.5, 4.0, ((0, 16),)),
        "latents": normal_values(own_keys[1], (SEQ_LEN, PATCH), 1.0, 6.0, ((0, 16),), jnp.float32),
        "base_qkv": draw_base_qkv(jax.random.fold_in(jax.random.fold_in(splits[8], part), 71), part),
        "control_qkv": draw_control_qkv(jax.random.fold_in(jax.random.fold_in(splits[8], part), 71), part),
        "step_index": jax.random.randint(splits[4], (1,), 0, STEPS).astype(jnp.int32),
        "w_join": normal_values(splits[5], (2 * ATT, D), (2 * ATT) ** -0.5, 0.109375, ((1, 16),)),
        "w_mod": normal_values(splits[6], (TEMB, 2 * D), TEMB ** -0.5, 0.25),
        "w_out": normal_values(splits[7], (D, PATCH), D ** -0.5, 0.109375),
    }


def attention(section_qkv):
    score_scale = HD ** (-0.5)
    shaped = section_qkv.reshape(3, SEQ_LEN, HEADS, HD).transpose(0, 2, 1, 3)

    def single_head(head_data):
        queries, keys_block, values_block = head_data
        scores = jnp.dot(queries, keys_block.T, preferred_element_type=jnp.float32) * score_scale
        highest = lax.optimization_barrier(jnp.max(scores, axis=1, keepdims=True))
        exponent = jnp.exp(scores - highest)
        total = lax.optimization_barrier(jnp.sum(exponent, axis=1, keepdims=True))
        mixed = jnp.dot(exponent.astype(jnp.bfloat16), values_block, preferred_element_type=jnp.float32)
        return (mixed / total).astype(jnp.bfloat16)
    outputs = lax.map(single_head, (shaped[0], shaped[1], shaped[2]))
    return outputs.transpose(1, 0, 2).reshape(SEQ_LEN, HEADS * HD)

def time_terms(step_index):
    step_value = step_index[0].astype(jnp.float32)
    level_now = jnp.cos(0.5 * math.pi * step_value / STEPS)
    level_next = jnp.cos(0.5 * math.pi * (step_value + 1.0) / STEPS)
    half_width = TEMB // 2
    frequency = jnp.exp(-math.log(10000.0) * jnp.arange(half_width).astype(jnp.float32) / half_width)
    angles = 1000.0 * level_now * frequency
    embedding = jnp.concatenate([jnp.cos(angles), jnp.sin(angles)]).astype(jnp.bfloat16)
    return (embedding, level_next - level_now)

def reference(hidden, latents, base_qkv, control_qkv, step_index, w_join, w_mod, w_out):
    joined = jnp.concatenate([attention(base_qkv), attention(control_qkv)], axis=1)
    update = jnp.dot(joined, w_join, preferred_element_type=jnp.float32)
    summed = hidden.astype(jnp.float32) + update
    hidden_next = summed.astype(jnp.bfloat16)
    embedding, step_size = time_terms(step_index)
    modulation = jnp.dot(embedding[None, :], w_mod, preferred_element_type=jnp.float32)[0]
    shift_term = modulation[:D]
    gain_term = modulation[D:]
    average = lax.optimization_barrier(jnp.mean(summed, axis=1, keepdims=True))
    centered = summed - average
    variance = lax.optimization_barrier(jnp.mean(centered * centered, axis=1, keepdims=True))
    normed = (centered / jnp.sqrt(variance + 1e-05) * (1.0 + gain_term) + shift_term).astype(jnp.bfloat16)
    velocity = jnp.dot(normed, w_out, preferred_element_type=jnp.float32)
    latents_next = latents + step_size * velocity
    return (hidden_next, velocity, latents_next)
```

```python
import functools
import math

import jax
import jax.numpy as jnp
from jax import lax
from jax.experimental import pallas as pl
from jax.experimental.pallas import tpu as pltpu
from jax.sharding import PartitionSpec as P

D = 3072
HD = 64
TEMB = 512
HEADS = 24
STEPS = 50


def time_terms(step_index):
    step_value = step_index[0].astype(jnp.float32)
    level_now = jnp.cos(0.5 * math.pi * step_value / STEPS)
    level_next = jnp.cos(0.5 * math.pi * (step_value + 1.0) / STEPS)
    half_width = TEMB // 2
    frequency = jnp.exp(
        -math.log(10000.0) * jnp.arange(half_width).astype(jnp.float32) / half_width
    )
    angles = 1000.0 * level_now * frequency
    embedding = jnp.concatenate([jnp.cos(angles), jnp.sin(angles)]).astype(jnp.bfloat16)
    return (embedding, level_next - level_now)


def attend(state, queries, shard_rows):
    running_max, running_sum, weighted = state
    count = shard_rows.shape[1]
    keys_block = shard_rows[0].reshape(count, HEADS, HD)
    values_block = shard_rows[1].reshape(count, HEADS, HD)
    scores = jnp.einsum(
        "qhd,khd->qhk", queries, keys_block, preferred_element_type=jnp.float32
    ) * HD ** (-0.5)
    newest_max = jnp.max(scores, axis=2)
    rescale = jnp.exp(running_max - newest_max)
    exponent = jnp.exp(scores - newest_max[:, :, None])
    running_sum = running_sum * rescale + jnp.sum(exponent, axis=2)
    weighted = weighted * rescale[:, :, None] + jnp.einsum(
        "qhk,khd->qhd",
        exponent.astype(jnp.bfloat16),
        values_block,
        preferred_element_type=jnp.float32,
    )
    return (newest_max, running_sum, weighted)


def finish(state):
    running_max, running_sum, weighted = state
    outputs = (weighted / running_sum[:, :, None]).astype(jnp.bfloat16)
    return outputs.reshape(outputs.shape[0], HEADS * HD)


def gathered(hidden, latents, base_qkv, control_qkv, step_index, w_join, w_mod, w_out):
    tokens_here = hidden.shape[0]
    base_queries = base_qkv[0].reshape(tokens_here, HEADS, HD)
    control_queries = control_qkv[0].reshape(tokens_here, HEADS, HD)
    base_pairs = base_qkv[1:]
    control_pairs = control_qkv[1:]
    initial = (
        jnp.full((tokens_here, HEADS), -jnp.inf, jnp.float32),
        jnp.zeros((tokens_here, HEADS), jnp.float32),
        jnp.zeros((tokens_here, HEADS, HD), jnp.float32),
    )
    base_state = attend(
        initial, base_queries, lax.all_gather(base_pairs, "seq", axis=1, tiled=True)
    )
    control_state = attend(
        initial, control_queries, lax.all_gather(control_pairs, "seq", axis=1, tiled=True)
    )
    joined = jnp.concatenate([finish(base_state), finish(control_state)], axis=1)
    column_part = jnp.dot(
        lax.all_gather(joined, "seq", axis=0, tiled=True),
        w_join,
        preferred_element_type=jnp.float32,
    )
    update = lax.all_to_all(
        column_part.astype(jnp.bfloat16), "seq", split_axis=0, concat_axis=1, tiled=True
    ).astype(column_part.dtype)
    summed = hidden.astype(jnp.float32) + update
    hidden_next = summed.astype(jnp.bfloat16)
    embedding, step_size = time_terms(step_index)
    modulation = jnp.dot(embedding[None, :], w_mod, preferred_element_type=jnp.float32)[0]
    shift_term = modulation[:D]
    gain_term = modulation[D:]
    average = jnp.mean(summed, axis=1, keepdims=True)
    centered = summed - average
    variance = jnp.mean(centered * centered, axis=1, keepdims=True)
    normed = (centered / jnp.sqrt(variance + 1e-05) * (1.0 + gain_term) + shift_term).astype(
        jnp.bfloat16
    )
    velocity = jnp.dot(normed, w_out, preferred_element_type=jnp.float32)
    latents_next = latents + step_size * velocity
    return (hidden_next, velocity, latents_next)


LANES = 128
MESH = pl.DeviceIdType.MESH


def fused_kernel(
    plan,
    hidden_in,
    latents_in,
    base_in,
    control_in,
    step_in,
    join_in,
    mod_in,
    out_in,
    next_ref,
    velocity_ref,
    latents_ref,
    hidden,
    latents,
    w_out,
    w_mod,
    w_join,
    modulation,
    heads_own,
    heads_other,
    joined,
    total,
    update_out,
    update_in,
    summed,
    load_sem,
    own_sem,
    swap_send,
    swap_recv,
    pass_send,
    pass_recv,
    side_send,
    side_recv,
    right_send,
    left_send,
    cross_send,
    join_recv,
    back_send,
    back_recv,
):
    chips, rows, lines, width, pieces = plan
    tokens = hidden.shape[0]
    section = base_in.shape[2]
    per_section = section // width
    me = lax.axis_index("seq")
    core = lax.rem(me, 2)
    chip = me // 2
    row = lax.rem(chip, rows)
    place = chip // rows

    def device(other, other_core):
        return {"seq": other * 2 + other_core}

    def remote(src, dst, send, recv, target):
        return pltpu.make_async_remote_copy(
            src_ref=src,
            dst_ref=dst,
            send_sem=send,
            recv_sem=recv,
            device_id=target,
            device_id_type=MESH,
        )

    mod_load = pltpu.make_async_copy(mod_in, w_mod, load_sem.at[0])
    small_loads = [
        pltpu.make_async_copy(hidden_in, hidden, load_sem.at[1]),
        pltpu.make_async_copy(latents_in, latents, load_sem.at[2]),
        pltpu.make_async_copy(out_in, w_out, load_sem.at[3]),
        pltpu.make_async_copy(join_in, w_join.at[core], load_sem.at[4]),
    ]
    barrier = pltpu.get_barrier_semaphore()
    for step in range(1, chips):
        pl.semaphore_signal(
            barrier,
            inc=1,
            device_id=device(lax.rem(chip + step, chips), core),
            device_id_type=MESH,
        )
    pl.semaphore_signal(barrier, inc=1, device_id=device(chip, 1 - core), device_id_type=MESH)
    mod_load.start()
    for load in small_loads:
        load.start()
    pl.semaphore_wait(barrier, chips)

    def piece_of(ref, target, piece):
        start = lax.rem(target, per_section) * width + piece * LANES
        return ref.at[:, :, pl.ds(pl.multiple_of(start, LANES), LANES)]

    def from_section(target, act):
        @pl.when(target < per_section)
        def _():
            act(base_in)

        @pl.when(target >= per_section)
        def _():
            act(control_in)

    def columns(piece):
        return pl.ds(piece * LANES, LANES)

    def swap(ref, target, step, piece):
        return remote(
            piece_of(ref, target, piece),
            heads_own.at[chip, :, :, columns(piece)],
            swap_send.at[step, piece],
            swap_recv.at[chip, piece],
            device(target, core),
        )

    def own_copy(ref, piece):
        return pltpu.make_async_copy(
            piece_of(ref, chip, piece), heads_own.at[chip, :, :, columns(piece)], own_sem.at[piece]
        )

    def pass_on(source, piece):
        return remote(
            heads_own.at[source, 1:3, :, columns(piece)],
            heads_other.at[source, :, :, columns(piece)],
            pass_send.at[source, piece],
            pass_recv.at[source, piece],
            device(chip, 1 - core),
        )

    side = remote(join_in, w_join.at[core], side_send, side_recv, device(chip, 1 - core))
    for piece in range(pieces):
        for step in range(1, chips):
            target = lax.rem(chip + step, chips)
            from_section(
                target, lambda ref, t=target, s=step, p=piece: swap(ref, t, s, p).start()
            )
        from_section(chip, lambda ref, p=piece: own_copy(ref, p).start())
    side.start()

    step_value = jnp.full((1, TEMB), step_in[0].astype(jnp.float32))
    level_now = jnp.cos(0.5 * math.pi * step_value / STEPS)
    level_next = jnp.cos(0.5 * math.pi * (step_value + 1.0) / STEPS)
    half_width = TEMB // 2
    index = lax.broadcasted_iota(jnp.int32, (1, TEMB), 1)
    place_in_half = jnp.where(index < half_width, index, index - half_width).astype(jnp.float32)
    frequency = jnp.exp(-math.log(10000.0) * place_in_half / half_width)
    angles = 1000.0 * level_now * frequency
    embedding = jnp.where(index < half_width, jnp.cos(angles), jnp.sin(angles))
    embedding = jnp.broadcast_to(embedding, (16, TEMB)).astype(jnp.bfloat16)
    step_size = (level_next - level_now)[:, : latents.shape[1]]
    mod_load.wait()
    block = 512
    for start in range(0, w_mod.shape[1], block):
        modulation[:, start : start + block] = jnp.dot(
            embedding, w_mod[:, start : start + block], preferred_element_type=jnp.float32
        )[0:1]

    lane = lax.broadcasted_iota(jnp.int32, (chips * tokens, LANES), 1)

    def attention(piece):
        def rows_of(ref, kind):
            part = ref[:, kind, :, piece * LANES : (piece + 1) * LANES].astype(jnp.float32)
            return part.reshape(chips * tokens, LANES)

        queries = rows_of(heads_own, 0) * HD ** (-0.5)
        keys = jnp.concatenate([rows_of(heads_own, 1), rows_of(heads_other, 0)], axis=0)
        values = jnp.concatenate([rows_of(heads_own, 2), rows_of(heads_other, 1)], axis=0)
        keys = keys.astype(jnp.bfloat16)
        values = values.astype(jnp.bfloat16)
        result = None
        for head in range(LANES // HD):
            mine = (lane >= head * HD) & (lane < (head + 1) * HD)
            query = jnp.where(mine, queries, 0.0).astype(jnp.bfloat16)
            scores = lax.dot_general(
                query, keys, (((1,), (1,)), ((), ())), preferred_element_type=jnp.float32
            )
            exponent = jnp.exp(scores - jnp.max(scores, axis=1, keepdims=True))
            row_sum = jnp.sum(exponent, axis=1, keepdims=True)
            mixed = jnp.dot(
                exponent.astype(jnp.bfloat16), values, preferred_element_type=jnp.float32
            )
            mixed = mixed / row_sum
            result = mixed if result is None else jnp.where(mine, mixed, result)
        joined[chip, :, piece * LANES : (piece + 1) * LANES] = result.astype(jnp.bfloat16)

    def hop(block_chip, piece, send, target):
        view = joined.at[block_chip, :, columns(piece)]
        return remote(
            view,
            view,
            send.at[block_chip, piece],
            join_recv.at[block_chip, piece],
            device(target, core),
        )

    def other_row_step(step):
        return lax.rem(row + step, rows)

    def hand_on(origin, piece, act):
        block_chip = origin * rows + row

        @pl.when((origin <= place) & (place < lines - 1))
        def _():
            act(hop(block_chip, piece, right_send, chip + rows))

        @pl.when((origin >= place) & (place > 0))
        def _():
            act(hop(block_chip, piece, left_send, chip - rows))

        for step in range(1, rows):
            act(hop(block_chip, piece, cross_send, place * rows + other_row_step(step)))

    def at_distance(distance, act):
        @pl.when(place >= distance)
        def _():
            act(place - distance)

        @pl.when(place + distance < lines)
        def _():
            act(place + distance)

    def arrive(block_chip, piece):
        view = joined.at[block_chip, :, columns(piece)]
        remote(
            view,
            view,
            cross_send.at[block_chip, piece],
            join_recv.at[block_chip, piece],
            device(chip, 1 - core),
        ).wait_recv()

    def relay(distance, piece):
        def act(origin):
            arrive(origin * rows + row, piece)
            hand_on(origin, piece, lambda copy: copy.start())

        at_distance(distance, act)

    for piece in range(pieces):
        from_section(chip, lambda ref, p=piece: own_copy(ref, p).wait())
        pass_on(chip, piece).start()
        for step in range(1, chips):
            source = lax.rem(chip - step + chips, chips)
            remote(
                heads_own.at[source, :, :, columns(piece)],
                heads_own.at[source, :, :, columns(piece)],
                swap_send.at[step, piece],
                swap_recv.at[source, piece],
                device(source, core),
            ).wait_recv()
            pass_on(source, piece).start()
        for step in range(chips):
            pass_on(lax.rem(chip - step + chips, chips), piece).wait_recv()
        attention(piece)
        hand_on(place, piece, lambda copy: copy.start())
        for earlier in range(piece):
            distance = piece - earlier
            if distance < lines:
                relay(distance, earlier)

    small_loads[3].wait()
    side.wait_recv()

    def project(block_chip):
        block_rows = pl.ds(pl.multiple_of(block_chip * width, width), width)
        for half in range(2):
            total[half] += jnp.dot(
                joined[block_chip], w_join[half, block_rows, :], preferred_element_type=jnp.float32
            )

    total[...] = jnp.zeros_like(total)
    project(chip)
    done = {p: pieces - 1 - p for p in range(pieces)}
    for distance in range(1, lines):
        for piece in range(pieces):
            if done[piece] < distance:
                relay(distance, piece)
                done[piece] = distance
        at_distance(distance, lambda origin: project(origin * rows + row))
        for step in range(1, rows):

            def cross(origin, s=step):
                block_chip = origin * rows + other_row_step(s)
                for piece in range(pieces):
                    arrive(block_chip, piece)
                project(block_chip)

            if distance == 1:
                cross(place)
            if distance > 1:
                at_distance(distance - 1, cross)
    for step in range(1, rows):

        def last_cross(origin, s=step):
            block_chip = origin * rows + other_row_step(s)
            for piece in range(pieces):
                arrive(block_chip, piece)
            project(block_chip)

        if lines == 1:
            last_cross(place)
        else:
            at_distance(lines - 1, last_cross)

    update = jnp.concatenate([total[0], total[1]], axis=1)
    update_out[...] = update.reshape(chips, tokens, width).astype(jnp.bfloat16)

    def back(target, step):
        return remote(
            update_out.at[target],
            update_in.at[chip],
            back_send.at[step],
            back_recv.at[chip],
            device(target, core),
        )

    for step in range(1, chips):
        back(lax.rem(chip + step, chips), step).start()
    update_in[chip] = update_out[chip]
    for load in small_loads[:3]:
        load.wait()
    for step in range(1, chips):
        source = lax.rem(chip - step + chips, chips)
        remote(
            update_out.at[source],
            update_in.at[source],
            back_send.at[step],
            back_recv.at[source],
            device(source, core),
        ).wait_recv()
    for source in range(chips):
        cut = slice(source * width, (source + 1) * width)
        summed[:, cut] = hidden[:, cut].astype(jnp.float32) + update_in[source].astype(jnp.float32)
    whole = summed[...]
    next_ref[...] = whole.astype(jnp.bfloat16)
    average = jnp.mean(whole, axis=1, keepdims=True)
    centered = whole - average
    variance = jnp.mean(centered * centered, axis=1, keepdims=True)
    shift_term = modulation[:, :D]
    gain_term = modulation[:, D:]
    normed = centered / jnp.sqrt(variance + 1e-05) * (1.0 + gain_term) + shift_term
    velocity = jnp.dot(
        normed.astype(jnp.bfloat16), w_out[...], preferred_element_type=jnp.float32
    )
    velocity_ref[...] = velocity
    latents_ref[...] = latents[...] + step_size * velocity

    for piece in range(pieces):
        for step in range(1, chips):
            swap(base_in, lax.rem(chip + step, chips), step, piece).wait_send()
        for source in range(chips):
            pass_on(source, piece).wait_send()
        for distance in range(lines):
            if distance == 0:
                hand_on(place, piece, lambda copy: copy.wait_send())
            else:
                at_distance(
                    distance, lambda o, p=piece: hand_on(o, p, lambda copy: copy.wait_send())
                )
    side.wait_send()
    for step in range(1, chips):
        back(lax.rem(chip + step, chips), step).wait_send()


def fused(plan, hidden, latents, base_qkv, control_qkv, step_index, w_join, w_mod, w_out):
    chips, rows, lines, width, pieces = plan
    tokens = hidden.shape[0]
    any_spec = pl.BlockSpec(memory_space=pl.ANY)
    vmem_spec = pl.BlockSpec(memory_space=pltpu.VMEM)
    half_columns = w_join.shape[1]
    dma = pltpu.SemaphoreType.DMA
    return pl.pallas_call(
        functools.partial(fused_kernel, plan),
        out_shape=(
            jax.ShapeDtypeStruct(hidden.shape, jnp.bfloat16),
            jax.ShapeDtypeStruct(latents.shape, jnp.float32),
            jax.ShapeDtypeStruct(latents.shape, jnp.float32),
        ),
        in_specs=[any_spec] * 4
        + [pl.BlockSpec(memory_space=pltpu.SMEM)]
        + [any_spec] * 3,
        out_specs=(vmem_spec,) * 3,
        scratch_shapes=[
            pltpu.VMEM(hidden.shape, jnp.bfloat16),
            pltpu.VMEM(latents.shape, jnp.float32),
            pltpu.VMEM(w_out.shape, jnp.bfloat16),
            pltpu.VMEM(w_mod.shape, jnp.bfloat16),
            pltpu.VMEM((2,) + w_join.shape, jnp.bfloat16),
            pltpu.VMEM((1, w_mod.shape[1]), jnp.float32),
            pltpu.VMEM((chips, 3, tokens, width), jnp.bfloat16),
            pltpu.VMEM((chips, 2, tokens, width), jnp.bfloat16),
            pltpu.VMEM((chips, chips * tokens, width), jnp.bfloat16),
            pltpu.VMEM((2, chips * tokens, half_columns), jnp.float32),
            pltpu.VMEM((chips, tokens, width), jnp.bfloat16),
            pltpu.VMEM((chips, tokens, width), jnp.bfloat16),
            pltpu.VMEM(hidden.shape, jnp.float32),
            dma((5,)),
            dma((pieces,)),
            dma((chips, pieces)),
            dma((chips, pieces)),
            dma((chips, pieces)),
            dma((chips, pieces)),
            dma,
            dma,
            dma((chips, pieces)),
            dma((chips, pieces)),
            dma((chips, pieces)),
            dma((chips, pieces)),
            dma((chips,)),
            dma((chips,)),
        ],
        compiler_params=pltpu.CompilerParams(
            collective_id=0, has_side_effects=True, vmem_limit_bytes=48 * 1024 * 1024
        ),
        name="fused",
    )(hidden, latents, base_qkv, control_qkv, step_index, w_join, w_mod, w_out)


def plan_for(count, sections_width, section_width):
    if count % 4 != 0:
        return None
    chips = count // 2
    width = sections_width // chips
    if sections_width % chips or width % LANES or section_width % width:
        return None
    return (chips, 2, chips // 2, width, width // LANES)


def local(hidden, latents, base_qkv, control_qkv, step_index, w_join, w_mod, w_out, count):
    plan = plan_for(count, w_join.shape[0], base_qkv.shape[2])
    if plan is None or hidden.shape[0] % 8 or (plan[0] * hidden.shape[0]) % 16:
        return gathered(
            hidden, latents, base_qkv, control_qkv, step_index, w_join, w_mod, w_out
        )
    return fused(
        plan, hidden, latents, base_qkv, control_qkv, step_index, w_join, w_mod, w_out
    )


def solution(mesh):
    in_specs = (
        P(("groups", "seq"), None),
        P(("groups", "seq"), None),
        P(None, ("groups", "seq"), None),
        P(None, ("groups", "seq"), None),
        P(),
        P(None, "seq"),
        P(),
        P(),
    )
    out_specs = (P(("groups", "seq"), None), P(("groups", "seq"), None), P(("groups", "seq"), None))
    return jax.shard_map(
        functools.partial(local, count=mesh.shape["seq"]),
        mesh=mesh,
        in_specs=in_specs,
        out_specs=out_specs,
        check_vma=False,
    )
```

```python
import functools
import math

import jax
import jax.numpy as jnp
from jax import lax
from jax.experimental import pallas as pl
from jax.experimental.pallas import tpu as pltpu
from jax.sharding import PartitionSpec as P

D = 3072
HD = 64
TEMB = 512
HEADS = 24
STEPS = 50


def time_terms(step_index):
    step_value = step_index[0].astype(jnp.float32)
    level_now = jnp.cos(0.5 * math.pi * step_value / STEPS)
    level_next = jnp.cos(0.5 * math.pi * (step_value + 1.0) / STEPS)
    half_width = TEMB // 2
    frequency = jnp.exp(
        -math.log(10000.0) * jnp.arange(half_width).astype(jnp.float32) / half_width
    )
    angles = 1000.0 * level_now * frequency
    embedding = jnp.concatenate([jnp.cos(angles), jnp.sin(angles)]).astype(jnp.bfloat16)
    return (embedding, level_next - level_now)


def attend(state, queries, shard_rows):
    running_max, running_sum, weighted = state
    count = shard_rows.shape[1]
    keys_block = shard_rows[0].reshape(count, HEADS, HD)
    values_block = shard_rows[1].reshape(count, HEADS, HD)
    scores = jnp.einsum(
        "qhd,khd->qhk", queries, keys_block, preferred_element_type=jnp.float32
    ) * HD ** (-0.5)
    newest_max = jnp.max(scores, axis=2)
    rescale = jnp.exp(running_max - newest_max)
    exponent = jnp.exp(scores - newest_max[:, :, None])
    running_sum = running_sum * rescale + jnp.sum(exponent, axis=2)
    weighted = weighted * rescale[:, :, None] + jnp.einsum(
        "qhk,khd->qhd",
        exponent.astype(jnp.bfloat16),
        values_block,
        preferred_element_type=jnp.float32,
    )
    return (newest_max, running_sum, weighted)


def finish(state):
    running_max, running_sum, weighted = state
    outputs = (weighted / running_sum[:, :, None]).astype(jnp.bfloat16)
    return outputs.reshape(outputs.shape[0], HEADS * HD)


def gathered(hidden, latents, base_qkv, control_qkv, step_index, w_join, w_mod, w_out):
    tokens_here = hidden.shape[0]
    base_queries = base_qkv[0].reshape(tokens_here, HEADS, HD)
    control_queries = control_qkv[0].reshape(tokens_here, HEADS, HD)
    base_pairs = base_qkv[1:]
    control_pairs = control_qkv[1:]
    initial = (
        jnp.full((tokens_here, HEADS), -jnp.inf, jnp.float32),
        jnp.zeros((tokens_here, HEADS), jnp.float32),
        jnp.zeros((tokens_here, HEADS, HD), jnp.float32),
    )
    base_state = attend(
        initial, base_queries, lax.all_gather(base_pairs, "seq", axis=1, tiled=True)
    )
    control_state = attend(
        initial, control_queries, lax.all_gather(control_pairs, "seq", axis=1, tiled=True)
    )
    joined = jnp.concatenate([finish(base_state), finish(control_state)], axis=1)
    column_part = jnp.dot(
        lax.all_gather(joined, "seq", axis=0, tiled=True),
        w_join,
        preferred_element_type=jnp.float32,
    )
    update = lax.all_to_all(
        column_part.astype(jnp.bfloat16), "seq", split_axis=0, concat_axis=1, tiled=True
    ).astype(column_part.dtype)
    summed = hidden.astype(jnp.float32) + update
    hidden_next = summed.astype(jnp.bfloat16)
    embedding, step_size = time_terms(step_index)
    modulation = jnp.dot(embedding[None, :], w_mod, preferred_element_type=jnp.float32)[0]
    shift_term = modulation[:D]
    gain_term = modulation[D:]
    average = jnp.mean(summed, axis=1, keepdims=True)
    centered = summed - average
    variance = jnp.mean(centered * centered, axis=1, keepdims=True)
    normed = (centered / jnp.sqrt(variance + 1e-05) * (1.0 + gain_term) + shift_term).astype(
        jnp.bfloat16
    )
    velocity = jnp.dot(normed, w_out, preferred_element_type=jnp.float32)
    latents_next = latents + step_size * velocity
    return (hidden_next, velocity, latents_next)


LANES = 128
MESH = pl.DeviceIdType.MESH


def fused_kernel(
    plan,
    hidden_in,
    latents_in,
    base_in,
    control_in,
    step_in,
    join_in,
    mod_in,
    out_in,
    next_ref,
    velocity_ref,
    latents_ref,
    hidden,
    latents,
    w_out,
    w_mod,
    w_join,
    modulation,
    heads_own,
    heads_other,
    joined,
    total,
    update_out,
    update_in,
    summed,
    load_sem,
    own_sem,
    swap_send,
    swap_recv,
    pass_send,
    pass_recv,
    side_send,
    side_recv,
    right_send,
    left_send,
    cross_send,
    join_recv,
    back_send,
    back_recv,
):
    chips, rows, lines, width, pieces = plan
    tokens = hidden.shape[0]
    section = base_in.shape[2]
    per_section = section // width
    me = lax.axis_index("seq")
    core = lax.rem(me, 2)
    chip = me // 2
    row = lax.rem(chip, rows)
    place = chip // rows

    def device(other, other_core):
        return {"seq": other * 2 + other_core}

    def remote(src, dst, send, recv, target):
        return pltpu.make_async_remote_copy(
            src_ref=src,
            dst_ref=dst,
            send_sem=send,
            recv_sem=recv,
            device_id=target,
            device_id_type=MESH,
        )

    half_rows = join_in.shape[0]

    def join_half(which):
        return w_join.at[pl.ds(pl.multiple_of(which * half_rows, half_rows), half_rows), :]

    mod_load = pltpu.make_async_copy(mod_in, w_mod, load_sem.at[0])
    small_loads = [
        pltpu.make_async_copy(hidden_in, hidden, load_sem.at[1]),
        pltpu.make_async_copy(latents_in, latents, load_sem.at[2]),
        pltpu.make_async_copy(out_in, w_out, load_sem.at[3]),
        pltpu.make_async_copy(join_in, join_half(core), load_sem.at[4]),
    ]
    barrier = pltpu.get_barrier_semaphore()
    for step in range(1, chips):
        pl.semaphore_signal(
            barrier,
            inc=1,
            device_id=device(lax.rem(chip + step, chips), core),
            device_id_type=MESH,
        )
    pl.semaphore_signal(barrier, inc=1, device_id=device(chip, 1 - core), device_id_type=MESH)
    mod_load.start()
    for load in small_loads:
        load.start()
    step_value = jnp.full((1, TEMB), step_in[0].astype(jnp.float32))
    level_now = jnp.cos(0.5 * math.pi * step_value / STEPS)
    level_next = jnp.cos(0.5 * math.pi * (step_value + 1.0) / STEPS)
    half_width = TEMB // 2
    index = lax.broadcasted_iota(jnp.int32, (1, TEMB), 1)
    place_in_half = jnp.where(index < half_width, index, index - half_width).astype(jnp.float32)
    frequency = jnp.exp(-math.log(10000.0) * place_in_half / half_width)
    angles = 1000.0 * level_now * frequency
    embedding = jnp.where(index < half_width, jnp.cos(angles), jnp.sin(angles))
    embedding = jnp.broadcast_to(embedding, (16, TEMB)).astype(jnp.bfloat16)
    step_size = (level_next - level_now)[:, : latents.shape[1]]
    pl.semaphore_wait(barrier, chips)

    def piece_of(ref, target, piece):
        start = lax.rem(target, per_section) * width + piece * LANES
        return ref.at[:, :, pl.ds(pl.multiple_of(start, LANES), LANES)]

    def from_section(target, act):
        @pl.when(target < per_section)
        def _():
            act(base_in)

        @pl.when(target >= per_section)
        def _():
            act(control_in)

    def columns(piece):
        return pl.ds(piece * LANES, LANES)

    far_first = sorted(range(1, chips), key=lambda step: abs(2 * step - chips))

    def swap(ref, target, step, piece):
        return remote(
            piece_of(ref, target, piece),
            heads_own.at[chip, :, :, columns(piece)],
            swap_send.at[step, piece],
            swap_recv.at[chip, piece],
            device(target, core),
        )

    def own_copy(ref, piece):
        return pltpu.make_async_copy(
            piece_of(ref, chip, piece), heads_own.at[chip, :, :, columns(piece)], own_sem.at[piece]
        )

    def pass_on(source, piece):
        return remote(
            heads_own.at[source, 1:3, :, columns(piece)],
            heads_other.at[source, :, :, columns(piece)],
            pass_send.at[source, piece],
            pass_recv.at[source, piece],
            device(chip, 1 - core),
        )

    side = remote(join_in, join_half(core), side_send, side_recv, device(chip, 1 - core))
    for piece in range(pieces):
        for step in far_first:
            target = lax.rem(chip + step, chips)
            from_section(
                target, lambda ref, t=target, s=step, p=piece: swap(ref, t, s, p).start()
            )
        from_section(chip, lambda ref, p=piece: own_copy(ref, p).start())
    side.start()

    mod_load.wait()
    block = 512
    for start in range(0, w_mod.shape[1], block):
        modulation[:, start : start + block] = jnp.dot(
            embedding, w_mod[:, start : start + block], preferred_element_type=jnp.float32
        )[0:1]

    lane = lax.broadcasted_iota(jnp.int32, (chips * tokens, LANES), 1)

    def attention(piece):
        def rows_of(ref, kind):
            part = ref[:, kind, :, piece * LANES : (piece + 1) * LANES].astype(jnp.float32)
            return part.reshape(chips * tokens, LANES)

        queries = rows_of(heads_own, 0) * HD ** (-0.5)
        keys = jnp.concatenate([rows_of(heads_own, 1), rows_of(heads_other, 0)], axis=0)
        values = jnp.concatenate([rows_of(heads_own, 2), rows_of(heads_other, 1)], axis=0)
        keys = keys.astype(jnp.bfloat16)
        values = values.astype(jnp.bfloat16)
        result = None
        for head in range(LANES // HD):
            mine = (lane >= head * HD) & (lane < (head + 1) * HD)
            query = jnp.where(mine, queries, 0.0).astype(jnp.bfloat16)
            scores = lax.dot_general(
                query, keys, (((1,), (1,)), ((), ())), preferred_element_type=jnp.float32
            )
            exponent = jnp.exp(scores - jnp.max(scores, axis=1, keepdims=True))
            row_sum = jnp.sum(exponent, axis=1, keepdims=True)
            mixed = jnp.dot(
                exponent.astype(jnp.bfloat16), values, preferred_element_type=jnp.float32
            )
            mixed = mixed / row_sum
            result = mixed if result is None else jnp.where(mine, mixed, result)
        joined[chip, :, piece * LANES : (piece + 1) * LANES] = result.astype(jnp.bfloat16)

    def hop(block_chip, piece, send, target):
        view = joined.at[block_chip, :, columns(piece)]
        return remote(
            view,
            view,
            send.at[block_chip, piece],
            join_recv.at[block_chip, piece],
            device(target, core),
        )

    def other_row_step(step):
        return lax.rem(row + step, rows)

    def hand_on(origin, piece, act):
        block_chip = origin * rows + row

        @pl.when((origin <= place) & (place < lines - 1))
        def _():
            act(hop(block_chip, piece, right_send, chip + rows))

        @pl.when((origin >= place) & (place > 0))
        def _():
            act(hop(block_chip, piece, left_send, chip - rows))

        for step in range(1, rows):
            act(hop(block_chip, piece, cross_send, place * rows + other_row_step(step)))

    def at_distance(distance, act):
        @pl.when(place >= distance)
        def _():
            act(place - distance)

        @pl.when(place + distance < lines)
        def _():
            act(place + distance)

    def arrive(block_chip, piece):
        view = joined.at[block_chip, :, columns(piece)]
        remote(
            view,
            view,
            cross_send.at[block_chip, piece],
            join_recv.at[block_chip, piece],
            device(chip, 1 - core),
        ).wait_recv()

    def relay(distance, piece):
        def act(origin):
            arrive(origin * rows + row, piece)
            hand_on(origin, piece, lambda copy: copy.start())

        at_distance(distance, act)

    for piece in range(pieces):
        from_section(chip, lambda ref, p=piece: own_copy(ref, p).wait())
        pass_on(chip, piece).start()
        for step in reversed(far_first):
            source = lax.rem(chip - step + chips, chips)
            remote(
                heads_own.at[source, :, :, columns(piece)],
                heads_own.at[source, :, :, columns(piece)],
                swap_send.at[step, piece],
                swap_recv.at[source, piece],
                device(source, core),
            ).wait_recv()
            pass_on(source, piece).start()
        for step in range(chips):
            pass_on(lax.rem(chip - step + chips, chips), piece).wait_recv()
        attention(piece)
        hand_on(place, piece, lambda copy: copy.start())
        for earlier in range(piece):
            distance = piece - earlier
            if distance < lines:
                relay(distance, earlier)

    small_loads[3].wait()
    side.wait_recv()

    def project(block_chip):
        block_columns = pl.ds(pl.multiple_of(block_chip * width, LANES), width)
        total[...] += lax.dot_general(
            joined[block_chip],
            w_join[:, block_columns],
            (((1,), (1,)), ((), ())),
            preferred_element_type=jnp.float32,
        )

    total[...] = jnp.zeros_like(total)
    project(chip)
    done = {p: pieces - 1 - p for p in range(pieces)}
    for distance in range(1, lines):
        for piece in range(pieces):
            if done[piece] < distance:
                relay(distance, piece)
                done[piece] = distance
        at_distance(distance, lambda origin: project(origin * rows + row))
        for step in range(1, rows):

            def cross(origin, s=step):
                block_chip = origin * rows + other_row_step(s)
                for piece in range(pieces):
                    arrive(block_chip, piece)
                project(block_chip)

            if distance == 1:
                cross(place)
            if distance > 1:
                at_distance(distance - 1, cross)
    for step in range(1, rows):

        def last_cross(origin, s=step):
            block_chip = origin * rows + other_row_step(s)
            for piece in range(pieces):
                arrive(block_chip, piece)
            project(block_chip)

        if lines == 1:
            last_cross(place)
        else:
            at_distance(lines - 1, last_cross)

    update_out[...] = total[...].reshape(chips, tokens, width).astype(jnp.bfloat16)

    def back(target, step):
        return remote(
            update_out.at[target],
            update_in.at[chip],
            back_send.at[step],
            back_recv.at[chip],
            device(target, core),
        )

    for step in far_first:
        back(lax.rem(chip + step, chips), step).start()
    update_in[chip] = update_out[chip]
    for load in small_loads[:3]:
        load.wait()
    for step in range(1, chips):
        source = lax.rem(chip - step + chips, chips)
        remote(
            update_out.at[source],
            update_in.at[source],
            back_send.at[step],
            back_recv.at[source],
            device(source, core),
        ).wait_recv()
    for source in range(chips):
        cut = slice(source * width, (source + 1) * width)
        summed[:, cut] = hidden[:, cut].astype(jnp.float32) + update_in[source].astype(jnp.float32)
    whole = summed[...]
    next_ref[...] = whole.astype(jnp.bfloat16)
    average = jnp.mean(whole, axis=1, keepdims=True)
    centered = whole - average
    variance = jnp.mean(centered * centered, axis=1, keepdims=True)
    shift_term = modulation[:, :D]
    gain_term = modulation[:, D:]
    normed = centered / jnp.sqrt(variance + 1e-05) * (1.0 + gain_term) + shift_term
    velocity = lax.dot_general(
        normed.astype(jnp.bfloat16),
        w_out[...],
        (((1,), (1,)), ((), ())),
        preferred_element_type=jnp.float32,
    )
    velocity_ref[...] = velocity
    latents_ref[...] = latents[...] + step_size * velocity

    for piece in range(pieces):
        for step in range(1, chips):
            swap(base_in, lax.rem(chip + step, chips), step, piece).wait_send()
        for source in range(chips):
            pass_on(source, piece).wait_send()
        for distance in range(lines):
            if distance == 0:
                hand_on(place, piece, lambda copy: copy.wait_send())
            else:
                at_distance(
                    distance, lambda o, p=piece: hand_on(o, p, lambda copy: copy.wait_send())
                )
    side.wait_send()
    for step in range(1, chips):
        back(lax.rem(chip + step, chips), step).wait_send()


def fused(plan, hidden, latents, base_qkv, control_qkv, step_index, w_join, w_mod, w_out):
    chips, rows, lines, width, pieces = plan
    tokens = hidden.shape[0]
    any_spec = pl.BlockSpec(memory_space=pl.ANY)
    vmem_spec = pl.BlockSpec(memory_space=pltpu.VMEM)
    dma = pltpu.SemaphoreType.DMA
    return pl.pallas_call(
        functools.partial(fused_kernel, plan),
        out_shape=(
            jax.ShapeDtypeStruct(hidden.shape, jnp.bfloat16),
            jax.ShapeDtypeStruct(latents.shape, jnp.float32),
            jax.ShapeDtypeStruct(latents.shape, jnp.float32),
        ),
        in_specs=[any_spec] * 4
        + [pl.BlockSpec(memory_space=pltpu.SMEM)]
        + [any_spec] * 3,
        out_specs=(vmem_spec,) * 3,
        scratch_shapes=[
            pltpu.VMEM(hidden.shape, jnp.bfloat16),
            pltpu.VMEM(latents.shape, jnp.float32),
            pltpu.VMEM(w_out.shape[::-1], jnp.bfloat16),
            pltpu.VMEM(w_mod.shape, jnp.bfloat16),
            pltpu.VMEM((2 * w_join.shape[1], w_join.shape[0]), jnp.bfloat16),
            pltpu.VMEM((1, w_mod.shape[1]), jnp.float32),
            pltpu.VMEM((chips, 3, tokens, width), jnp.bfloat16),
            pltpu.VMEM((chips, 2, tokens, width), jnp.bfloat16),
            pltpu.VMEM((chips, chips * tokens, width), jnp.bfloat16),
            pltpu.VMEM((chips * tokens, width), jnp.float32),
            pltpu.VMEM((chips, tokens, width), jnp.bfloat16),
            pltpu.VMEM((chips, tokens, width), jnp.bfloat16),
            pltpu.VMEM(hidden.shape, jnp.float32),
            dma((5,)),
            dma((pieces,)),
            dma((chips, pieces)),
            dma((chips, pieces)),
            dma((chips, pieces)),
            dma((chips, pieces)),
            dma,
            dma,
            dma((chips, pieces)),
            dma((chips, pieces)),
            dma((chips, pieces)),
            dma((chips, pieces)),
            dma((chips,)),
            dma((chips,)),
        ],
        compiler_params=pltpu.CompilerParams(
            collective_id=0, has_side_effects=True, vmem_limit_bytes=48 * 1024 * 1024
        ),
        name="fused",
    )(hidden, latents, base_qkv, control_qkv, step_index, w_join.T, w_mod, w_out.T)


def plan_for(count, sections_width, section_width):
    if count % 4 != 0:
        return None
    chips = count // 2
    width = sections_width // chips
    if sections_width % chips or width % LANES or section_width % width:
        return None
    return (chips, 2, chips // 2, width, width // LANES)


def local(hidden, latents, base_qkv, control_qkv, step_index, w_join, w_mod, w_out, count):
    plan = plan_for(count, w_join.shape[0], base_qkv.shape[2])
    if plan is None or hidden.shape[0] % 8 or (plan[0] * hidden.shape[0]) % 16:
        return gathered(
            hidden, latents, base_qkv, control_qkv, step_index, w_join, w_mod, w_out
        )
    return fused(
        plan, hidden, latents, base_qkv, control_qkv, step_index, w_join, w_mod, w_out
    )


def solution(mesh):
    in_specs = (
        P(("groups", "seq"), None),
        P(("groups", "seq"), None),
        P(None, ("groups", "seq"), None),
        P(None, ("groups", "seq"), None),
        P(),
        P(None, "seq"),
        P(),
        P(),
    )
    out_specs = (P(("groups", "seq"), None), P(("groups", "seq"), None), P(("groups", "seq"), None))
    return jax.shard_map(
        functools.partial(local, count=mesh.shape["seq"]),
        mesh=mesh,
        in_specs=in_specs,
        out_specs=out_specs,
        check_vma=False,
    )
```

```python
import functools
import math

import jax
import jax.numpy as jnp
from jax import lax
from jax.experimental import pallas as pl
from jax.experimental.pallas import tpu as pltpu
from jax.sharding import PartitionSpec as P

D = 3072
HD = 64
TEMB = 512
HEADS = 24
STEPS = 50


def time_terms(step_index):
    step_value = step_index[0].astype(jnp.float32)
    level_now = jnp.cos(0.5 * math.pi * step_value / STEPS)
    level_next = jnp.cos(0.5 * math.pi * (step_value + 1.0) / STEPS)
    half_width = TEMB // 2
    frequency = jnp.exp(
        -math.log(10000.0) * jnp.arange(half_width).astype(jnp.float32) / half_width
    )
    angles = 1000.0 * level_now * frequency
    embedding = jnp.concatenate([jnp.cos(angles), jnp.sin(angles)]).astype(jnp.bfloat16)
    return (embedding, level_next - level_now)


def attend(state, queries, shard_rows):
    running_max, running_sum, weighted = state
    count = shard_rows.shape[1]
    keys_block = shard_rows[0].reshape(count, HEADS, HD)
    values_block = shard_rows[1].reshape(count, HEADS, HD)
    scores = jnp.einsum(
        "qhd,khd->qhk", queries, keys_block, preferred_element_type=jnp.float32
    ) * HD ** (-0.5)
    newest_max = jnp.max(scores, axis=2)
    rescale = jnp.exp(running_max - newest_max)
    exponent = jnp.exp(scores - newest_max[:, :, None])
    running_sum = running_sum * rescale + jnp.sum(exponent, axis=2)
    weighted = weighted * rescale[:, :, None] + jnp.einsum(
        "qhk,khd->qhd",
        exponent.astype(jnp.bfloat16),
        values_block,
        preferred_element_type=jnp.float32,
    )
    return (newest_max, running_sum, weighted)


def finish(state):
    running_max, running_sum, weighted = state
    outputs = (weighted / running_sum[:, :, None]).astype(jnp.bfloat16)
    return outputs.reshape(outputs.shape[0], HEADS * HD)


def gathered(hidden, latents, base_qkv, control_qkv, step_index, w_join, w_mod, w_out):
    tokens_here = hidden.shape[0]
    base_queries = base_qkv[0].reshape(tokens_here, HEADS, HD)
    control_queries = control_qkv[0].reshape(tokens_here, HEADS, HD)
    base_pairs = base_qkv[1:]
    control_pairs = control_qkv[1:]
    initial = (
        jnp.full((tokens_here, HEADS), -jnp.inf, jnp.float32),
        jnp.zeros((tokens_here, HEADS), jnp.float32),
        jnp.zeros((tokens_here, HEADS, HD), jnp.float32),
    )
    base_state = attend(
        initial, base_queries, lax.all_gather(base_pairs, "seq", axis=1, tiled=True)
    )
    control_state = attend(
        initial, control_queries, lax.all_gather(control_pairs, "seq", axis=1, tiled=True)
    )
    joined = jnp.concatenate([finish(base_state), finish(control_state)], axis=1)
    column_part = jnp.dot(
        lax.all_gather(joined, "seq", axis=0, tiled=True),
        w_join,
        preferred_element_type=jnp.float32,
    )
    update = lax.all_to_all(
        column_part.astype(jnp.bfloat16), "seq", split_axis=0, concat_axis=1, tiled=True
    ).astype(column_part.dtype)
    summed = hidden.astype(jnp.float32) + update
    hidden_next = summed.astype(jnp.bfloat16)
    embedding, step_size = time_terms(step_index)
    modulation = jnp.dot(embedding[None, :], w_mod, preferred_element_type=jnp.float32)[0]
    shift_term = modulation[:D]
    gain_term = modulation[D:]
    average = jnp.mean(summed, axis=1, keepdims=True)
    centered = summed - average
    variance = jnp.mean(centered * centered, axis=1, keepdims=True)
    normed = (centered / jnp.sqrt(variance + 1e-05) * (1.0 + gain_term) + shift_term).astype(
        jnp.bfloat16
    )
    velocity = jnp.dot(normed, w_out, preferred_element_type=jnp.float32)
    latents_next = latents + step_size * velocity
    return (hidden_next, velocity, latents_next)


LANES = 128
MESH = pl.DeviceIdType.MESH


def fused_kernel(
    plan,
    hidden_in,
    latents_in,
    base_in,
    control_in,
    step_in,
    join_in,
    mod_in,
    out_in,
    next_ref,
    velocity_ref,
    latents_ref,
    hidden,
    latents,
    w_out,
    w_mod,
    w_join,
    modulation,
    heads_own,
    heads_other,
    joined,
    total,
    update_out,
    update_in,
    summed,
    load_sem,
    own_sem,
    swap_send,
    swap_recv,
    pass_send,
    pass_recv,
    side_send,
    side_recv,
    right_send,
    left_send,
    cross_send,
    join_recv,
    back_send,
    back_recv,
):
    chips, rows, lines, width, pieces = plan
    tokens = hidden.shape[0]
    section = base_in.shape[2]
    per_section = section // width
    me = lax.axis_index("seq")
    core = lax.rem(me, 2)
    chip = me // 2
    row = lax.rem(chip, rows)
    place = chip // rows

    def device(other, other_core):
        return {"seq": other * 2 + other_core}

    def remote(src, dst, send, recv, target):
        return pltpu.make_async_remote_copy(
            src_ref=src,
            dst_ref=dst,
            send_sem=send,
            recv_sem=recv,
            device_id=target,
            device_id_type=MESH,
        )

    half_rows = join_in.shape[0]

    def join_half(which):
        return w_join.at[pl.ds(pl.multiple_of(which * half_rows, half_rows), half_rows), :]

    mod_load = pltpu.make_async_copy(mod_in, w_mod, load_sem.at[0])
    small_loads = [
        pltpu.make_async_copy(hidden_in, hidden, load_sem.at[1]),
        pltpu.make_async_copy(latents_in, latents, load_sem.at[2]),
        pltpu.make_async_copy(out_in, w_out, load_sem.at[3]),
        pltpu.make_async_copy(join_in, join_half(core), load_sem.at[4]),
    ]
    barrier = pltpu.get_barrier_semaphore()
    for step in range(1, chips):
        pl.semaphore_signal(
            barrier,
            inc=1,
            device_id=device(lax.rem(chip + step, chips), core),
            device_id_type=MESH,
        )
    pl.semaphore_signal(barrier, inc=1, device_id=device(chip, 1 - core), device_id_type=MESH)
    mod_load.start()
    for load in small_loads:
        load.start()
    step_value = jnp.full((1, TEMB), step_in[0].astype(jnp.float32))
    level_now = jnp.cos(0.5 * math.pi * step_value / STEPS)
    level_next = jnp.cos(0.5 * math.pi * (step_value + 1.0) / STEPS)
    half_width = TEMB // 2
    index = lax.broadcasted_iota(jnp.int32, (1, TEMB), 1)
    place_in_half = jnp.where(index < half_width, index, index - half_width).astype(jnp.float32)
    frequency = jnp.exp(-math.log(10000.0) * place_in_half / half_width)
    angles = 1000.0 * level_now * frequency
    embedding = jnp.where(index < half_width, jnp.cos(angles), jnp.sin(angles))
    embedding = jnp.broadcast_to(embedding, (16, TEMB)).astype(jnp.bfloat16)
    step_size = (level_next - level_now)[:, : latents.shape[1]]
    pl.semaphore_wait(barrier, chips)

    def piece_of(ref, target, piece):
        start = lax.rem(target, per_section) * width + piece * LANES
        return ref.at[:, :, pl.ds(pl.multiple_of(start, LANES), LANES)]

    def from_section(target, act):
        @pl.when(target < per_section)
        def _():
            act(base_in)

        @pl.when(target >= per_section)
        def _():
            act(control_in)

    far_first = sorted(range(1, chips), key=lambda step: abs(2 * step - chips))

    def swap(ref, target, step, piece):
        return remote(
            piece_of(ref, target, piece),
            heads_own.at[chip, piece],
            swap_send.at[step, piece],
            swap_recv.at[chip, piece],
            device(target, core),
        )

    def own_copy(ref, piece):
        return pltpu.make_async_copy(
            piece_of(ref, chip, piece), heads_own.at[chip, piece], own_sem.at[piece]
        )

    def pass_on(source, piece):
        return remote(
            heads_own.at[source, piece, 1:3],
            heads_other.at[source, piece],
            pass_send.at[source, piece],
            pass_recv.at[source, piece],
            device(chip, 1 - core),
        )

    side = remote(join_in, join_half(core), side_send, side_recv, device(chip, 1 - core))
    for piece in range(pieces):
        for step in far_first:
            target = lax.rem(chip + step, chips)
            from_section(
                target, lambda ref, t=target, s=step, p=piece: swap(ref, t, s, p).start()
            )
        from_section(chip, lambda ref, p=piece: own_copy(ref, p).start())
    side.start()

    mod_load.wait()
    block = 512
    for start in range(0, w_mod.shape[1], block):
        modulation[:, start : start + block] = jnp.dot(
            embedding, w_mod[:, start : start + block], preferred_element_type=jnp.float32
        )[0:1]

    lane = lax.broadcasted_iota(jnp.int32, (chips * tokens, LANES), 1)

    def attention(piece):
        def rows_of(ref, kind):
            part = ref[:, piece, kind].astype(jnp.float32)
            return part.reshape(chips * tokens, LANES)

        queries = rows_of(heads_own, 0) * HD ** (-0.5)
        keys = jnp.concatenate([rows_of(heads_own, 1), rows_of(heads_other, 0)], axis=0)
        values = jnp.concatenate([rows_of(heads_own, 2), rows_of(heads_other, 1)], axis=0)
        keys = keys.astype(jnp.bfloat16)
        values = values.astype(jnp.bfloat16)
        result = None
        for head in range(LANES // HD):
            mine = (lane >= head * HD) & (lane < (head + 1) * HD)
            query = jnp.where(mine, queries, 0.0).astype(jnp.bfloat16)
            scores = lax.dot_general(
                query, keys, (((1,), (1,)), ((), ())), preferred_element_type=jnp.float32
            )
            exponent = jnp.exp(scores - jnp.max(scores, axis=1, keepdims=True))
            row_sum = jnp.sum(exponent, axis=1, keepdims=True)
            mixed = jnp.dot(
                exponent.astype(jnp.bfloat16), values, preferred_element_type=jnp.float32
            )
            mixed = mixed / row_sum
            result = mixed if result is None else jnp.where(mine, mixed, result)
        joined[chip, piece] = result.astype(jnp.bfloat16)

    def hop(block_chip, piece, send, target):
        view = joined.at[block_chip, piece]
        return remote(
            view,
            view,
            send.at[block_chip, piece],
            join_recv.at[block_chip, piece],
            device(target, core),
        )

    def other_row_step(step):
        return lax.rem(row + step, rows)

    def hand_on(origin, piece, act):
        block_chip = origin * rows + row

        @pl.when((origin <= place) & (place < lines - 1))
        def _():
            act(hop(block_chip, piece, right_send, chip + rows))

        @pl.when((origin >= place) & (place > 0))
        def _():
            act(hop(block_chip, piece, left_send, chip - rows))

        for step in range(1, rows):
            act(hop(block_chip, piece, cross_send, place * rows + other_row_step(step)))

    def at_distance(distance, act):
        @pl.when(place >= distance)
        def _():
            act(place - distance)

        @pl.when(place + distance < lines)
        def _():
            act(place + distance)

    def arrive(block_chip, piece):
        view = joined.at[block_chip, piece]
        remote(
            view,
            view,
            cross_send.at[block_chip, piece],
            join_recv.at[block_chip, piece],
            device(chip, 1 - core),
        ).wait_recv()

    def relay(distance, piece):
        def act(origin):
            arrive(origin * rows + row, piece)
            hand_on(origin, piece, lambda copy: copy.start())

        at_distance(distance, act)

    for piece in range(pieces):
        from_section(chip, lambda ref, p=piece: own_copy(ref, p).wait())
        pass_on(chip, piece).start()
        for step in reversed(far_first):
            source = lax.rem(chip - step + chips, chips)
            remote(
                heads_own.at[source, piece],
                heads_own.at[source, piece],
                swap_send.at[step, piece],
                swap_recv.at[source, piece],
                device(source, core),
            ).wait_recv()
            pass_on(source, piece).start()
        for step in range(chips):
            pass_on(lax.rem(chip - step + chips, chips), piece).wait_recv()
        attention(piece)
        hand_on(place, piece, lambda copy: copy.start())
        for earlier in range(piece):
            distance = piece - earlier
            if distance < lines:
                relay(distance, earlier)

    small_loads[3].wait()
    side.wait_recv()

    def project(block_chip):
        block_columns = pl.ds(pl.multiple_of(block_chip * width, LANES), width)
        total[...] += lax.dot_general(
            jnp.concatenate([joined[block_chip, p] for p in range(pieces)], axis=1),
            w_join[:, block_columns],
            (((1,), (1,)), ((), ())),
            preferred_element_type=jnp.float32,
        )

    total[...] = jnp.zeros_like(total)
    project(chip)
    done = {p: pieces - 1 - p for p in range(pieces)}
    for distance in range(1, lines):
        for piece in range(pieces):
            if done[piece] < distance:
                relay(distance, piece)
                done[piece] = distance
        at_distance(distance, lambda origin: project(origin * rows + row))
        for step in range(1, rows):

            def cross(origin, s=step):
                block_chip = origin * rows + other_row_step(s)
                for piece in range(pieces):
                    arrive(block_chip, piece)
                project(block_chip)

            if distance == 1:
                cross(place)
            if distance > 1:
                at_distance(distance - 1, cross)
    for step in range(1, rows):

        def last_cross(origin, s=step):
            block_chip = origin * rows + other_row_step(s)
            for piece in range(pieces):
                arrive(block_chip, piece)
            project(block_chip)

        if lines == 1:
            last_cross(place)
        else:
            at_distance(lines - 1, last_cross)

    update_out[...] = total[...].reshape(chips, tokens, width).astype(jnp.bfloat16)

    def back(target, step):
        return remote(
            update_out.at[target],
            update_in.at[chip],
            back_send.at[step],
            back_recv.at[chip],
            device(target, core),
        )

    for step in far_first:
        back(lax.rem(chip + step, chips), step).start()
    update_in[chip] = update_out[chip]
    for load in small_loads[:3]:
        load.wait()
    for step in range(1, chips):
        source = lax.rem(chip - step + chips, chips)
        remote(
            update_out.at[source],
            update_in.at[source],
            back_send.at[step],
            back_recv.at[source],
            device(source, core),
        ).wait_recv()
    for source in range(chips):
        cut = slice(source * width, (source + 1) * width)
        summed[:, cut] = hidden[:, cut].astype(jnp.float32) + update_in[source].astype(jnp.float32)
    whole = summed[...]
    next_ref[...] = whole.astype(jnp.bfloat16)
    average = jnp.mean(whole, axis=1, keepdims=True)
    centered = whole - average
    variance = jnp.mean(centered * centered, axis=1, keepdims=True)
    shift_term = modulation[:, :D]
    gain_term = modulation[:, D:]
    normed = centered / jnp.sqrt(variance + 1e-05) * (1.0 + gain_term) + shift_term
    velocity = lax.dot_general(
        normed.astype(jnp.bfloat16),
        w_out[...],
        (((1,), (1,)), ((), ())),
        preferred_element_type=jnp.float32,
    )
    velocity_ref[...] = velocity
    latents_ref[...] = latents[...] + step_size * velocity

    for piece in range(pieces):
        for step in range(1, chips):
            swap(base_in, lax.rem(chip + step, chips), step, piece).wait_send()
        for source in range(chips):
            pass_on(source, piece).wait_send()
        for distance in range(lines):
            if distance == 0:
                hand_on(place, piece, lambda copy: copy.wait_send())
            else:
                at_distance(
                    distance, lambda o, p=piece: hand_on(o, p, lambda copy: copy.wait_send())
                )
    side.wait_send()
    for step in range(1, chips):
        back(lax.rem(chip + step, chips), step).wait_send()


def fused(plan, hidden, latents, base_qkv, control_qkv, step_index, w_join, w_mod, w_out):
    chips, rows, lines, width, pieces = plan
    tokens = hidden.shape[0]
    hbm_spec = pl.BlockSpec(memory_space=pltpu.HBM)
    vmem_spec = pl.BlockSpec(memory_space=pltpu.VMEM)
    dma = pltpu.SemaphoreType.DMA
    return pl.pallas_call(
        functools.partial(fused_kernel, plan),
        out_shape=(
            jax.ShapeDtypeStruct(hidden.shape, jnp.bfloat16),
            jax.ShapeDtypeStruct(latents.shape, jnp.float32),
            jax.ShapeDtypeStruct(latents.shape, jnp.float32),
        ),
        in_specs=[hbm_spec] * 4
        + [pl.BlockSpec(memory_space=pltpu.SMEM)]
        + [hbm_spec] * 3,
        out_specs=(vmem_spec,) * 3,
        scratch_shapes=[
            pltpu.VMEM(hidden.shape, jnp.bfloat16),
            pltpu.VMEM(latents.shape, jnp.float32),
            pltpu.VMEM(w_out.shape[::-1], jnp.bfloat16),
            pltpu.VMEM(w_mod.shape, jnp.bfloat16),
            pltpu.VMEM((2 * w_join.shape[1], w_join.shape[0]), jnp.bfloat16),
            pltpu.VMEM((1, w_mod.shape[1]), jnp.float32),
            pltpu.VMEM((chips, pieces, 3, tokens, LANES), jnp.bfloat16),
            pltpu.VMEM((chips, pieces, 2, tokens, LANES), jnp.bfloat16),
            pltpu.VMEM((chips, pieces, chips * tokens, LANES), jnp.bfloat16),
            pltpu.VMEM((chips * tokens, width), jnp.float32),
            pltpu.VMEM((chips, tokens, width), jnp.bfloat16),
            pltpu.VMEM((chips, tokens, width), jnp.bfloat16),
            pltpu.VMEM(hidden.shape, jnp.float32),
            dma((5,)),
            dma((pieces,)),
            dma((chips, pieces)),
            dma((chips, pieces)),
            dma((chips, pieces)),
            dma((chips, pieces)),
            dma,
            dma,
            dma((chips, pieces)),
            dma((chips, pieces)),
            dma((chips, pieces)),
            dma((chips, pieces)),
            dma((chips,)),
            dma((chips,)),
        ],
        compiler_params=pltpu.CompilerParams(
            collective_id=0, has_side_effects=True, vmem_limit_bytes=60 * 1024 * 1024
        ),
        name="fused",
    )(hidden, latents, base_qkv, control_qkv, step_index, w_join.T, w_mod, w_out.T)


def plan_for(count, sections_width, section_width):
    if count % 4 != 0:
        return None
    chips = count // 2
    width = sections_width // chips
    if sections_width % chips or width % LANES or section_width % width:
        return None
    return (chips, 2, chips // 2, width, width // LANES)


def local(hidden, latents, base_qkv, control_qkv, step_index, w_join, w_mod, w_out, count):
    plan = plan_for(count, w_join.shape[0], base_qkv.shape[2])
    if plan is None or hidden.shape[0] % 8 or (plan[0] * hidden.shape[0]) % 16:
        return gathered(
            hidden, latents, base_qkv, control_qkv, step_index, w_join, w_mod, w_out
        )
    return fused(
        plan, hidden, latents, base_qkv, control_qkv, step_index, w_join, w_mod, w_out
    )


def solution(mesh):
    in_specs = (
        P(("groups", "seq"), None),
        P(("groups", "seq"), None),
        P(None, ("groups", "seq"), None),
        P(None, ("groups", "seq"), None),
        P(),
        P(None, "seq"),
        P(),
        P(),
    )
    out_specs = (P(("groups", "seq"), None), P(("groups", "seq"), None), P(("groups", "seq"), None))
    return jax.shard_map(
        functools.partial(local, count=mesh.shape["seq"]),
        mesh=mesh,
        in_specs=in_specs,
        out_specs=out_specs,
        check_vma=False,
    )
```

```python
import functools
import math

import jax
import jax.numpy as jnp
from jax import lax
from jax.experimental import pallas as pl
from jax.experimental.pallas import tpu as pltpu
from jax.sharding import PartitionSpec as P

D = 3072
HD = 64
TEMB = 512
HEADS = 24
STEPS = 50


def time_terms(step_index):
    step_value = step_index[0].astype(jnp.float32)
    level_now = jnp.cos(0.5 * math.pi * step_value / STEPS)
    level_next = jnp.cos(0.5 * math.pi * (step_value + 1.0) / STEPS)
    half_width = TEMB // 2
    frequency = jnp.exp(
        -math.log(10000.0) * jnp.arange(half_width).astype(jnp.float32) / half_width
    )
    angles = 1000.0 * level_now * frequency
    embedding = jnp.concatenate([jnp.cos(angles), jnp.sin(angles)]).astype(jnp.bfloat16)
    return (embedding, level_next - level_now)


def attend(state, queries, shard_rows):
    running_max, running_sum, weighted = state
    count = shard_rows.shape[1]
    keys_block = shard_rows[0].reshape(count, HEADS, HD)
    values_block = shard_rows[1].reshape(count, HEADS, HD)
    scores = jnp.einsum(
        "qhd,khd->qhk", queries, keys_block, preferred_element_type=jnp.float32
    ) * HD ** (-0.5)
    newest_max = jnp.max(scores, axis=2)
    rescale = jnp.exp(running_max - newest_max)
    exponent = jnp.exp(scores - newest_max[:, :, None])
    running_sum = running_sum * rescale + jnp.sum(exponent, axis=2)
    weighted = weighted * rescale[:, :, None] + jnp.einsum(
        "qhk,khd->qhd",
        exponent.astype(jnp.bfloat16),
        values_block,
        preferred_element_type=jnp.float32,
    )
    return (newest_max, running_sum, weighted)


def finish(state):
    running_max, running_sum, weighted = state
    outputs = (weighted / running_sum[:, :, None]).astype(jnp.bfloat16)
    return outputs.reshape(outputs.shape[0], HEADS * HD)


def gathered(hidden, latents, base_qkv, control_qkv, step_index, w_join, w_mod, w_out):
    tokens_here = hidden.shape[0]
    base_queries = base_qkv[0].reshape(tokens_here, HEADS, HD)
    control_queries = control_qkv[0].reshape(tokens_here, HEADS, HD)
    base_pairs = base_qkv[1:]
    control_pairs = control_qkv[1:]
    initial = (
        jnp.full((tokens_here, HEADS), -jnp.inf, jnp.float32),
        jnp.zeros((tokens_here, HEADS), jnp.float32),
        jnp.zeros((tokens_here, HEADS, HD), jnp.float32),
    )
    base_state = attend(
        initial, base_queries, lax.all_gather(base_pairs, "seq", axis=1, tiled=True)
    )
    control_state = attend(
        initial, control_queries, lax.all_gather(control_pairs, "seq", axis=1, tiled=True)
    )
    joined = jnp.concatenate([finish(base_state), finish(control_state)], axis=1)
    column_part = jnp.dot(
        lax.all_gather(joined, "seq", axis=0, tiled=True),
        w_join,
        preferred_element_type=jnp.float32,
    )
    update = lax.all_to_all(
        column_part.astype(jnp.bfloat16), "seq", split_axis=0, concat_axis=1, tiled=True
    ).astype(column_part.dtype)
    summed = hidden.astype(jnp.float32) + update
    hidden_next = summed.astype(jnp.bfloat16)
    embedding, step_size = time_terms(step_index)
    modulation = jnp.dot(embedding[None, :], w_mod, preferred_element_type=jnp.float32)[0]
    shift_term = modulation[:D]
    gain_term = modulation[D:]
    average = jnp.mean(summed, axis=1, keepdims=True)
    centered = summed - average
    variance = jnp.mean(centered * centered, axis=1, keepdims=True)
    normed = (centered / jnp.sqrt(variance + 1e-05) * (1.0 + gain_term) + shift_term).astype(
        jnp.bfloat16
    )
    velocity = jnp.dot(normed, w_out, preferred_element_type=jnp.float32)
    latents_next = latents + step_size * velocity
    return (hidden_next, velocity, latents_next)


LANES = 128
MESH = pl.DeviceIdType.MESH


def fused_kernel(
    plan,
    base_in,
    control_in,
    step_in,
    join_in,
    mod_in,
    update_in,
    terms_ref,
    w_mod,
    w_join,
    modulation,
    heads_own,
    heads_other,
    joined,
    total,
    update_out,
    load_sem,
    own_sem,
    swap_send,
    swap_recv,
    pass_send,
    pass_recv,
    side_send,
    side_recv,
    right_send,
    left_send,
    cross_send,
    join_recv,
    back_send,
    back_recv,
):
    chips, rows, lines, width, pieces = plan
    tokens = base_in.shape[1]
    section = base_in.shape[2]
    per_section = section // width
    me = lax.axis_index("seq")
    core = lax.rem(me, 2)
    chip = me // 2
    row = lax.rem(chip, rows)
    place = chip // rows

    def device(other, other_core):
        return {"seq": other * 2 + other_core}

    def remote(src, dst, send, recv, target):
        return pltpu.make_async_remote_copy(
            src_ref=src,
            dst_ref=dst,
            send_sem=send,
            recv_sem=recv,
            device_id=target,
            device_id_type=MESH,
        )

    half_rows = join_in.shape[0]

    def join_half(which):
        return w_join.at[pl.ds(pl.multiple_of(which * half_rows, half_rows), half_rows), :]

    mod_load = pltpu.make_async_copy(mod_in, w_mod, load_sem.at[0])
    join_load = pltpu.make_async_copy(join_in, join_half(core), load_sem.at[1])
    barrier = pltpu.get_barrier_semaphore()
    for step in range(1, chips):
        pl.semaphore_signal(
            barrier,
            inc=1,
            device_id=device(lax.rem(chip + step, chips), core),
            device_id_type=MESH,
        )
    pl.semaphore_signal(barrier, inc=1, device_id=device(chip, 1 - core), device_id_type=MESH)
    mod_load.start()
    join_load.start()
    step_value = jnp.full((1, TEMB), step_in[0].astype(jnp.float32))
    level_now = jnp.cos(0.5 * math.pi * step_value / STEPS)
    level_next = jnp.cos(0.5 * math.pi * (step_value + 1.0) / STEPS)
    half_width = TEMB // 2
    index = lax.broadcasted_iota(jnp.int32, (1, TEMB), 1)
    place_in_half = jnp.where(index < half_width, index, index - half_width).astype(jnp.float32)
    frequency = jnp.exp(-math.log(10000.0) * place_in_half / half_width)
    angles = 1000.0 * level_now * frequency
    embedding = jnp.where(index < half_width, jnp.cos(angles), jnp.sin(angles))
    embedding = jnp.broadcast_to(embedding, (16, TEMB)).astype(jnp.bfloat16)
    step_size = level_next - level_now
    pl.semaphore_wait(barrier, chips)

    def piece_of(ref, target, piece):
        start = lax.rem(target, per_section) * width + piece * LANES
        return ref.at[:, :, pl.ds(pl.multiple_of(start, LANES), LANES)]

    def from_section(target, act):
        @pl.when(target < per_section)
        def _():
            act(base_in)

        @pl.when(target >= per_section)
        def _():
            act(control_in)

    far_first = sorted(range(1, chips), key=lambda step: abs(2 * step - chips))

    def swap(ref, target, step, piece):
        return remote(
            piece_of(ref, target, piece),
            heads_own.at[chip, piece],
            swap_send.at[step, piece],
            swap_recv.at[chip, piece],
            device(target, core),
        )

    def own_copy(ref, piece):
        return pltpu.make_async_copy(
            piece_of(ref, chip, piece), heads_own.at[chip, piece], own_sem.at[piece]
        )

    def pass_on(source, piece):
        return remote(
            heads_own.at[source, piece, 1:3],
            heads_other.at[source, piece],
            pass_send.at[source, piece],
            pass_recv.at[source, piece],
            device(chip, 1 - core),
        )

    side = remote(join_in, join_half(core), side_send, side_recv, device(chip, 1 - core))
    for piece in range(pieces):
        for step in far_first:
            target = lax.rem(chip + step, chips)
            from_section(
                target, lambda ref, t=target, s=step, p=piece: swap(ref, t, s, p).start()
            )
        from_section(chip, lambda ref, p=piece: own_copy(ref, p).start())
    side.start()

    mod_load.wait()
    for start in range(0, w_mod.shape[1], TEMB):
        modulation[0:1, start : start + TEMB] = jnp.dot(
            embedding, w_mod[:, start : start + TEMB], preferred_element_type=jnp.float32
        )[0:1]
        modulation[1:2, start : start + TEMB] = step_size
    terms_store = pltpu.make_async_copy(modulation, terms_ref, load_sem.at[2])
    terms_store.start()

    lane = lax.broadcasted_iota(jnp.int32, (chips * tokens, LANES), 1)

    def attention(piece):
        def rows_of(ref, kind):
            part = ref[:, piece, kind].astype(jnp.float32)
            return part.reshape(chips * tokens, LANES)

        queries = rows_of(heads_own, 0) * HD ** (-0.5)
        keys = jnp.concatenate([rows_of(heads_own, 1), rows_of(heads_other, 0)], axis=0)
        values = jnp.concatenate([rows_of(heads_own, 2), rows_of(heads_other, 1)], axis=0)
        keys = keys.astype(jnp.bfloat16)
        values = values.astype(jnp.bfloat16)
        result = None
        for head in range(LANES // HD):
            mine = (lane >= head * HD) & (lane < (head + 1) * HD)
            query = jnp.where(mine, queries, 0.0).astype(jnp.bfloat16)
            scores = lax.dot_general(
                query, keys, (((1,), (1,)), ((), ())), preferred_element_type=jnp.float32
            )
            exponent = jnp.exp(scores - jnp.max(scores, axis=1, keepdims=True))
            row_sum = jnp.sum(exponent, axis=1, keepdims=True)
            mixed = jnp.dot(
                exponent.astype(jnp.bfloat16), values, preferred_element_type=jnp.float32
            )
            mixed = mixed / row_sum
            result = mixed if result is None else jnp.where(mine, mixed, result)
        joined[chip, piece] = result.astype(jnp.bfloat16)

    def hop(block_chip, piece, send, target):
        view = joined.at[block_chip, piece]
        return remote(
            view,
            view,
            send.at[block_chip, piece],
            join_recv.at[block_chip, piece],
            device(target, core),
        )

    def other_row_step(step):
        return lax.rem(row + step, rows)

    def hand_on(origin, piece, act):
        block_chip = origin * rows + row

        @pl.when((origin <= place) & (place < lines - 1))
        def _():
            act(hop(block_chip, piece, right_send, chip + rows))

        @pl.when((origin >= place) & (place > 0))
        def _():
            act(hop(block_chip, piece, left_send, chip - rows))

        for step in range(1, rows):
            act(hop(block_chip, piece, cross_send, place * rows + other_row_step(step)))

    def at_distance(distance, act):
        @pl.when(place >= distance)
        def _():
            act(place - distance)

        @pl.when(place + distance < lines)
        def _():
            act(place + distance)

    def arrive(block_chip, piece):
        view = joined.at[block_chip, piece]
        remote(
            view,
            view,
            cross_send.at[block_chip, piece],
            join_recv.at[block_chip, piece],
            device(chip, 1 - core),
        ).wait_recv()

    def relay(distance, piece):
        def act(origin):
            arrive(origin * rows + row, piece)
            hand_on(origin, piece, lambda copy: copy.start())

        at_distance(distance, act)

    for piece in range(pieces):
        from_section(chip, lambda ref, p=piece: own_copy(ref, p).wait())
        pass_on(chip, piece).start()
        for step in reversed(far_first):
            source = lax.rem(chip - step + chips, chips)
            remote(
                heads_own.at[source, piece],
                heads_own.at[source, piece],
                swap_send.at[step, piece],
                swap_recv.at[source, piece],
                device(source, core),
            ).wait_recv()
            pass_on(source, piece).start()
        for step in range(chips):
            pass_on(lax.rem(chip - step + chips, chips), piece).wait_recv()
        attention(piece)
        hand_on(place, piece, lambda copy: copy.start())
        for earlier in range(piece):
            distance = piece - earlier
            if distance < lines:
                relay(distance, earlier)

    join_load.wait()
    side.wait_recv()

    def project(block_chip):
        block_columns = pl.ds(pl.multiple_of(block_chip * width, LANES), width)
        total[...] += lax.dot_general(
            jnp.concatenate([joined[block_chip, p] for p in range(pieces)], axis=1),
            w_join[:, block_columns],
            (((1,), (1,)), ((), ())),
            preferred_element_type=jnp.float32,
        )

    total[...] = jnp.zeros_like(total)
    project(chip)
    done = {p: pieces - 1 - p for p in range(pieces)}
    for distance in range(1, lines):
        for piece in range(pieces):
            if done[piece] < distance:
                relay(distance, piece)
                done[piece] = distance
        at_distance(distance, lambda origin: project(origin * rows + row))
        for step in range(1, rows):

            def cross(origin, s=step):
                block_chip = origin * rows + other_row_step(s)
                for piece in range(pieces):
                    arrive(block_chip, piece)
                project(block_chip)

            if distance == 1:
                cross(place)
            if distance > 1:
                at_distance(distance - 1, cross)
    for step in range(1, rows):

        def last_cross(origin, s=step):
            block_chip = origin * rows + other_row_step(s)
            for piece in range(pieces):
                arrive(block_chip, piece)
            project(block_chip)

        if lines == 1:
            last_cross(place)
        else:
            at_distance(lines - 1, last_cross)

    update_out[...] = total[...].reshape(chips, tokens, width).astype(jnp.bfloat16)

    def back(target, step):
        return remote(
            update_out.at[target],
            update_in.at[chip],
            back_send.at[step],
            back_recv.at[chip],
            device(target, core),
        )

    for step in far_first:
        back(lax.rem(chip + step, chips), step).start()
    own_back = pltpu.make_async_copy(update_out.at[chip], update_in.at[chip], load_sem.at[3])
    own_back.start()
    for step in range(1, chips):
        source = lax.rem(chip - step + chips, chips)
        remote(
            update_out.at[source],
            update_in.at[source],
            back_send.at[step],
            back_recv.at[source],
            device(source, core),
        ).wait_recv()
    for piece in range(pieces):
        for step in range(1, chips):
            swap(base_in, lax.rem(chip + step, chips), step, piece).wait_send()
        for source in range(chips):
            pass_on(source, piece).wait_send()
        for distance in range(lines):
            if distance == 0:
                hand_on(place, piece, lambda copy: copy.wait_send())
            else:
                at_distance(
                    distance, lambda o, p=piece: hand_on(o, p, lambda copy: copy.wait_send())
                )
    side.wait_send()
    terms_store.wait()
    own_back.wait()
    for step in range(1, chips):
        back(lax.rem(chip + step, chips), step).wait_send()


def finish_kernel(
    update_in,
    terms_in,
    hidden_in,
    latents_in,
    out_in,
    next_ref,
    velocity_ref,
    latents_ref,
    update,
    terms,
    hidden,
    latents,
    w_out,
    hidden_next,
    velocity_out,
    latents_next,
    load_sem,
    store_sem,
):
    loads = [
        pltpu.make_async_copy(source, target, load_sem.at[number])
        for number, (source, target) in enumerate(
            (
                (update_in, update),
                (hidden_in, hidden),
                (terms_in, terms),
                (out_in, w_out),
                (latents_in, latents),
            )
        )
    ]
    stores = [
        pltpu.make_async_copy(source, target, store_sem.at[number])
        for number, (source, target) in enumerate(
            (
                (hidden_next, next_ref),
                (velocity_out, velocity_ref),
                (latents_next, latents_ref),
            )
        )
    ]
    for load in loads:
        load.start()
    loads[0].wait()
    loads[1].wait()
    joined_columns = jnp.concatenate([update[p] for p in range(update.shape[0])], axis=1)
    summed = hidden[...].astype(jnp.float32) + joined_columns.astype(jnp.float32)
    hidden_next[...] = summed.astype(jnp.bfloat16)
    stores[0].start()
    average = jnp.mean(summed, axis=1, keepdims=True)
    centered = summed - average
    variance = jnp.mean(centered * centered, axis=1, keepdims=True)
    loads[2].wait()
    width = hidden.shape[1]
    shift_term = terms[0:1, :width]
    gain_term = terms[0:1, width:]
    normed = centered / jnp.sqrt(variance + 1e-05) * (1.0 + gain_term) + shift_term
    loads[3].wait()
    velocity = lax.dot_general(
        normed.astype(jnp.bfloat16),
        w_out[...],
        (((1,), (1,)), ((), ())),
        preferred_element_type=jnp.float32,
    )
    velocity_out[...] = velocity
    stores[1].start()
    loads[4].wait()
    latents_next[...] = latents[...] + terms[1:2, : latents.shape[1]] * velocity
    stores[2].start()
    for store in stores:
        store.wait()


def fused(plan, hidden, latents, base_qkv, control_qkv, step_index, w_join, w_mod, w_out):
    chips, rows, lines, width, pieces = plan
    tokens = hidden.shape[0]
    hbm_spec = pl.BlockSpec(memory_space=pltpu.HBM)
    dma = pltpu.SemaphoreType.DMA
    vmem_limit = 60 * 1024 * 1024
    per_piece = [dma((chips, pieces))] * 4
    update, terms = pl.pallas_call(
        functools.partial(fused_kernel, plan),
        out_shape=(
            jax.ShapeDtypeStruct((chips, tokens, width), jnp.bfloat16),
            jax.ShapeDtypeStruct((2, w_mod.shape[1]), jnp.float32),
        ),
        in_specs=[hbm_spec] * 2 + [pl.BlockSpec(memory_space=pltpu.SMEM)] + [hbm_spec] * 2,
        out_specs=(hbm_spec,) * 2,
        scratch_shapes=[
            pltpu.VMEM(w_mod.shape, jnp.bfloat16),
            pltpu.VMEM((2 * w_join.shape[1], w_join.shape[0]), jnp.bfloat16),
            pltpu.VMEM((2, w_mod.shape[1]), jnp.float32),
            pltpu.VMEM((chips, pieces, 3, tokens, LANES), jnp.bfloat16),
            pltpu.VMEM((chips, pieces, 2, tokens, LANES), jnp.bfloat16),
            pltpu.VMEM((chips, pieces, chips * tokens, LANES), jnp.bfloat16),
            pltpu.VMEM((chips * tokens, width), jnp.float32),
            pltpu.VMEM((chips, tokens, width), jnp.bfloat16),
            dma((4,)),
            dma((pieces,)),
            *per_piece,
            dma,
            dma,
            *per_piece,
            dma((chips,)),
            dma((chips,)),
        ],
        compiler_params=pltpu.CompilerParams(
            collective_id=0, has_side_effects=True, vmem_limit_bytes=vmem_limit
        ),
        name="fused",
    )(base_qkv, control_qkv, step_index, w_join.T, w_mod)
    return pl.pallas_call(
        finish_kernel,
        out_shape=(
            jax.ShapeDtypeStruct(hidden.shape, jnp.bfloat16),
            jax.ShapeDtypeStruct(latents.shape, jnp.float32),
            jax.ShapeDtypeStruct(latents.shape, jnp.float32),
        ),
        in_specs=[hbm_spec] * 5,
        out_specs=(hbm_spec,) * 3,
        scratch_shapes=[
            pltpu.VMEM(update.shape, jnp.bfloat16),
            pltpu.VMEM(terms.shape, jnp.float32),
            pltpu.VMEM(hidden.shape, jnp.bfloat16),
            pltpu.VMEM(latents.shape, jnp.float32),
            pltpu.VMEM(w_out.shape[::-1], jnp.bfloat16),
            pltpu.VMEM(hidden.shape, jnp.bfloat16),
            pltpu.VMEM(latents.shape, jnp.float32),
            pltpu.VMEM(latents.shape, jnp.float32),
            dma((5,)),
            dma((3,)),
        ],
        compiler_params=pltpu.CompilerParams(vmem_limit_bytes=vmem_limit),
        name="norm_and_step",
    )(update, terms, hidden, latents, w_out.T)


def plan_for(count, sections_width, section_width):
    if count % 4 != 0:
        return None
    chips = count // 2
    width = sections_width // chips
    if sections_width % chips or width % LANES or section_width % width:
        return None
    return (chips, 2, chips // 2, width, width // LANES)


def local(hidden, latents, base_qkv, control_qkv, step_index, w_join, w_mod, w_out, count):
    plan = plan_for(count, w_join.shape[0], base_qkv.shape[2])
    if plan is None or hidden.shape[0] % 8 or (plan[0] * hidden.shape[0]) % 16:
        return gathered(
            hidden, latents, base_qkv, control_qkv, step_index, w_join, w_mod, w_out
        )
    return fused(
        plan, hidden, latents, base_qkv, control_qkv, step_index, w_join, w_mod, w_out
    )


def solution(mesh):
    in_specs = (
        P(("groups", "seq"), None),
        P(("groups", "seq"), None),
        P(None, ("groups", "seq"), None),
        P(None, ("groups", "seq"), None),
        P(),
        P(None, "seq"),
        P(),
        P(),
    )
    out_specs = (P(("groups", "seq"), None), P(("groups", "seq"), None), P(("groups", "seq"), None))
    return jax.shard_map(
        functools.partial(local, count=mesh.shape["seq"]),
        mesh=mesh,
        in_specs=in_specs,
        out_specs=out_specs,
        check_vma=False,
    )
```

```python
import functools
import math

import jax
import jax.numpy as jnp
from jax import lax
from jax.experimental import pallas as pl
from jax.experimental.pallas import tpu as pltpu
from jax.sharding import PartitionSpec as P

D = 3072
HD = 64
TEMB = 512
HEADS = 24
STEPS = 50


def time_terms(step_index):
    step_value = step_index[0].astype(jnp.float32)
    level_now = jnp.cos(0.5 * math.pi * step_value / STEPS)
    level_next = jnp.cos(0.5 * math.pi * (step_value + 1.0) / STEPS)
    half_width = TEMB // 2
    frequency = jnp.exp(
        -math.log(10000.0) * jnp.arange(half_width).astype(jnp.float32) / half_width
    )
    angles = 1000.0 * level_now * frequency
    embedding = jnp.concatenate([jnp.cos(angles), jnp.sin(angles)]).astype(jnp.bfloat16)
    return (embedding, level_next - level_now)


def attend(state, queries, shard_rows):
    running_max, running_sum, weighted = state
    count = shard_rows.shape[1]
    keys_block = shard_rows[0].reshape(count, HEADS, HD)
    values_block = shard_rows[1].reshape(count, HEADS, HD)
    scores = jnp.einsum(
        "qhd,khd->qhk", queries, keys_block, preferred_element_type=jnp.float32
    ) * HD ** (-0.5)
    newest_max = jnp.max(scores, axis=2)
    rescale = jnp.exp(running_max - newest_max)
    exponent = jnp.exp(scores - newest_max[:, :, None])
    running_sum = running_sum * rescale + jnp.sum(exponent, axis=2)
    weighted = weighted * rescale[:, :, None] + jnp.einsum(
        "qhk,khd->qhd",
        exponent.astype(jnp.bfloat16),
        values_block,
        preferred_element_type=jnp.float32,
    )
    return (newest_max, running_sum, weighted)


def finish(state):
    running_max, running_sum, weighted = state
    outputs = (weighted / running_sum[:, :, None]).astype(jnp.bfloat16)
    return outputs.reshape(outputs.shape[0], HEADS * HD)


def gathered(hidden, latents, base_qkv, control_qkv, step_index, w_join, w_mod, w_out):
    tokens_here = hidden.shape[0]
    base_queries = base_qkv[0].reshape(tokens_here, HEADS, HD)
    control_queries = control_qkv[0].reshape(tokens_here, HEADS, HD)
    base_pairs = base_qkv[1:]
    control_pairs = control_qkv[1:]
    initial = (
        jnp.full((tokens_here, HEADS), -jnp.inf, jnp.float32),
        jnp.zeros((tokens_here, HEADS), jnp.float32),
        jnp.zeros((tokens_here, HEADS, HD), jnp.float32),
    )
    base_state = attend(
        initial, base_queries, lax.all_gather(base_pairs, "seq", axis=1, tiled=True)
    )
    control_state = attend(
        initial, control_queries, lax.all_gather(control_pairs, "seq", axis=1, tiled=True)
    )
    joined = jnp.concatenate([finish(base_state), finish(control_state)], axis=1)
    column_part = jnp.dot(
        lax.all_gather(joined, "seq", axis=0, tiled=True),
        w_join,
        preferred_element_type=jnp.float32,
    )
    update = lax.all_to_all(
        column_part.astype(jnp.bfloat16), "seq", split_axis=0, concat_axis=1, tiled=True
    ).astype(column_part.dtype)
    summed = hidden.astype(jnp.float32) + update
    hidden_next = summed.astype(jnp.bfloat16)
    embedding, step_size = time_terms(step_index)
    modulation = jnp.dot(embedding[None, :], w_mod, preferred_element_type=jnp.float32)[0]
    shift_term = modulation[:D]
    gain_term = modulation[D:]
    average = jnp.mean(summed, axis=1, keepdims=True)
    centered = summed - average
    variance = jnp.mean(centered * centered, axis=1, keepdims=True)
    normed = (centered / jnp.sqrt(variance + 1e-05) * (1.0 + gain_term) + shift_term).astype(
        jnp.bfloat16
    )
    velocity = jnp.dot(normed, w_out, preferred_element_type=jnp.float32)
    latents_next = latents + step_size * velocity
    return (hidden_next, velocity, latents_next)


LANES = 128
MESH = pl.DeviceIdType.MESH


def fused_kernel(
    plan,
    base_in,
    control_in,
    step_in,
    join_in,
    mod_in,
    update_in,
    terms_ref,
    w_mod,
    w_join,
    modulation,
    heads_own,
    heads_other,
    joined,
    total,
    update_out,
    load_sem,
    own_sem,
    swap_send,
    swap_recv,
    pass_send,
    pass_recv,
    side_send,
    side_recv,
    right_send,
    left_send,
    cross_send,
    join_recv,
    back_send,
    back_recv,
):
    chips, rows, lines, width, pieces = plan
    tokens = base_in.shape[1]
    section = base_in.shape[2]
    per_section = section // width
    me = lax.axis_index("seq")
    core = lax.rem(me, 2)
    chip = me // 2
    row = lax.rem(chip, rows)
    place = chip // rows

    def device(other, other_core):
        return {"seq": other * 2 + other_core}

    def remote(src, dst, send, recv, target):
        return pltpu.make_async_remote_copy(
            src_ref=src,
            dst_ref=dst,
            send_sem=send,
            recv_sem=recv,
            device_id=target,
            device_id_type=MESH,
        )

    half_rows = join_in.shape[0]

    def join_half(which):
        return w_join.at[pl.ds(pl.multiple_of(which * half_rows, half_rows), half_rows), :]

    mod_load = pltpu.make_async_copy(mod_in, w_mod, load_sem.at[0])
    join_load = pltpu.make_async_copy(join_in, join_half(core), load_sem.at[1])
    barrier = pltpu.get_barrier_semaphore()
    for step in range(1, chips):
        pl.semaphore_signal(
            barrier,
            inc=1,
            device_id=device(lax.rem(chip + step, chips), core),
            device_id_type=MESH,
        )
    pl.semaphore_signal(barrier, inc=1, device_id=device(chip, 1 - core), device_id_type=MESH)
    mod_load.start()
    join_load.start()
    step_value = jnp.full((1, TEMB), step_in[0].astype(jnp.float32))
    level_now = jnp.cos(0.5 * math.pi * step_value / STEPS)
    level_next = jnp.cos(0.5 * math.pi * (step_value + 1.0) / STEPS)
    half_width = TEMB // 2
    index = lax.broadcasted_iota(jnp.int32, (1, TEMB), 1)
    place_in_half = jnp.where(index < half_width, index, index - half_width).astype(jnp.float32)
    frequency = jnp.exp(-math.log(10000.0) * place_in_half / half_width)
    angles = 1000.0 * level_now * frequency
    embedding = jnp.where(index < half_width, jnp.cos(angles), jnp.sin(angles))
    embedding = jnp.broadcast_to(embedding, (16, TEMB)).astype(jnp.bfloat16)
    step_size = level_next - level_now
    pl.semaphore_wait(barrier, chips)

    def piece_of(ref, target, piece):
        start = lax.rem(target, per_section) * width + piece * LANES
        return ref.at[:, :, pl.ds(pl.multiple_of(start, LANES), LANES)]

    def from_section(target, act):
        @pl.when(target < per_section)
        def _():
            act(base_in)

        @pl.when(target >= per_section)
        def _():
            act(control_in)

    far_first = sorted(range(1, chips), key=lambda step: abs(2 * step - chips))

    def swap(ref, target, step, piece):
        return remote(
            piece_of(ref, target, piece),
            heads_own.at[chip, piece],
            swap_send.at[step, piece],
            swap_recv.at[chip, piece],
            device(target, core),
        )

    def own_copy(ref, piece):
        return pltpu.make_async_copy(
            piece_of(ref, chip, piece), heads_own.at[chip, piece], own_sem.at[piece]
        )

    def pass_on(source, piece):
        return remote(
            heads_own.at[source, piece, 1:3],
            heads_other.at[source, piece],
            pass_send.at[source, piece],
            pass_recv.at[source, piece],
            device(chip, 1 - core),
        )

    side = remote(join_in, join_half(core), side_send, side_recv, device(chip, 1 - core))
    for piece in range(pieces):
        for step in far_first:
            target = lax.rem(chip + step, chips)
            from_section(
                target, lambda ref, t=target, s=step, p=piece: swap(ref, t, s, p).start()
            )
        from_section(chip, lambda ref, p=piece: own_copy(ref, p).start())
    side.start()

    mod_load.wait()
    for start in range(0, w_mod.shape[1], TEMB):
        modulation[0:1, start : start + TEMB] = jnp.dot(
            embedding, w_mod[:, start : start + TEMB], preferred_element_type=jnp.float32
        )[0:1]
        modulation[1:2, start : start + TEMB] = step_size
    terms_store = pltpu.make_async_copy(modulation, terms_ref, load_sem.at[2])
    terms_store.start()

    lane = lax.broadcasted_iota(jnp.int32, (chips * tokens, LANES), 1)

    def attention(piece):
        def rows_of(ref, kind):
            part = ref[:, piece, kind].astype(jnp.float32)
            return part.reshape(chips * tokens, LANES)

        queries = rows_of(heads_own, 0) * HD ** (-0.5)
        keys = jnp.concatenate([rows_of(heads_own, 1), rows_of(heads_other, 0)], axis=0)
        values = jnp.concatenate([rows_of(heads_own, 2), rows_of(heads_other, 1)], axis=0)
        keys = keys.astype(jnp.bfloat16)
        values = values.astype(jnp.bfloat16)
        result = None
        for head in range(LANES // HD):
            mine = (lane >= head * HD) & (lane < (head + 1) * HD)
            query = jnp.where(mine, queries, 0.0).astype(jnp.bfloat16)
            scores = lax.dot_general(
                query, keys, (((1,), (1,)), ((), ())), preferred_element_type=jnp.float32
            )
            exponent = jnp.exp(scores - jnp.max(scores, axis=1, keepdims=True))
            row_sum = jnp.sum(exponent, axis=1, keepdims=True)
            mixed = jnp.dot(
                exponent.astype(jnp.bfloat16), values, preferred_element_type=jnp.float32
            )
            mixed = mixed / row_sum
            result = mixed if result is None else jnp.where(mine, mixed, result)
        joined[chip, piece] = result.astype(jnp.bfloat16)

    def hop(block_chip, piece, send, target):
        view = joined.at[block_chip, piece]
        return remote(
            view,
            view,
            send.at[block_chip, piece],
            join_recv.at[block_chip, piece],
            device(target, core),
        )

    def other_row_step(step):
        return lax.rem(row + step, rows)

    def hand_on(origin, piece, act):
        block_chip = origin * rows + row
        for step in range(1, rows):
            act(hop(block_chip, piece, cross_send, place * rows + other_row_step(step)))

        @pl.when((origin <= place) & (place < lines - 1))
        def _():
            act(hop(block_chip, piece, right_send, chip + rows))

        @pl.when((origin >= place) & (place > 0))
        def _():
            act(hop(block_chip, piece, left_send, chip - rows))

    def at_distance(distance, act):
        @pl.when(place >= distance)
        def _():
            act(place - distance)

        @pl.when(place + distance < lines)
        def _():
            act(place + distance)

    def arrive(block_chip, piece):
        view = joined.at[block_chip, piece]
        remote(
            view,
            view,
            cross_send.at[block_chip, piece],
            join_recv.at[block_chip, piece],
            device(chip, 1 - core),
        ).wait_recv()

    def relay(distance, piece):
        def act(origin):
            arrive(origin * rows + row, piece)
            hand_on(origin, piece, lambda copy: copy.start())

        at_distance(distance, act)

    for piece in range(pieces):
        from_section(chip, lambda ref, p=piece: own_copy(ref, p).wait())
        pass_on(chip, piece).start()
        for step in reversed(far_first):
            source = lax.rem(chip - step + chips, chips)
            remote(
                heads_own.at[source, piece],
                heads_own.at[source, piece],
                swap_send.at[step, piece],
                swap_recv.at[source, piece],
                device(source, core),
            ).wait_recv()
            pass_on(source, piece).start()
        for step in range(chips):
            pass_on(lax.rem(chip - step + chips, chips), piece).wait_recv()
        attention(piece)
        hand_on(place, piece, lambda copy: copy.start())
        for earlier in range(piece):
            distance = piece - earlier
            if distance < lines:
                relay(distance, earlier)

    join_load.wait()
    side.wait_recv()

    def project(block_chip):
        block_columns = pl.ds(pl.multiple_of(block_chip * width, LANES), width)
        total[...] += lax.dot_general(
            jnp.concatenate([joined[block_chip, p] for p in range(pieces)], axis=1),
            w_join[:, block_columns],
            (((1,), (1,)), ((), ())),
            preferred_element_type=jnp.float32,
        )

    total[...] = jnp.zeros_like(total)
    done = {p: pieces - 1 - p for p in range(pieces)}
    for distance in range(lines):
        for piece in range(pieces):
            if done[piece] < distance:
                relay(distance, piece)
        if distance == 0:
            project(chip)
        else:
            at_distance(distance, lambda origin: project(origin * rows + row))

    def cross(origin, step):
        block_chip = origin * rows + other_row_step(step)
        for piece in range(pieces):
            arrive(block_chip, piece)
        project(block_chip)

    for distance in range(lines):
        for step in range(1, rows):
            if distance == 0:
                cross(place, step)
            else:
                at_distance(distance, lambda origin, s=step: cross(origin, s))

    update_out[...] = total[...].reshape(chips, tokens, width).astype(jnp.bfloat16)

    def back(target, step):
        return remote(
            update_out.at[target],
            update_in.at[chip],
            back_send.at[step],
            back_recv.at[chip],
            device(target, core),
        )

    for step in far_first:
        back(lax.rem(chip + step, chips), step).start()
    own_back = pltpu.make_async_copy(update_out.at[chip], update_in.at[chip], load_sem.at[3])
    own_back.start()
    for step in range(1, chips):
        source = lax.rem(chip - step + chips, chips)
        remote(
            update_out.at[source],
            update_in.at[source],
            back_send.at[step],
            back_recv.at[source],
            device(source, core),
        ).wait_recv()
    for piece in range(pieces):
        for step in range(1, chips):
            swap(base_in, lax.rem(chip + step, chips), step, piece).wait_send()
        for source in range(chips):
            pass_on(source, piece).wait_send()
        for distance in range(lines):
            if distance == 0:
                hand_on(place, piece, lambda copy: copy.wait_send())
            else:
                at_distance(
                    distance, lambda o, p=piece: hand_on(o, p, lambda copy: copy.wait_send())
                )
    side.wait_send()
    terms_store.wait()
    own_back.wait()
    for step in range(1, chips):
        back(lax.rem(chip + step, chips), step).wait_send()


def finish_kernel(
    update_in,
    terms_in,
    hidden_in,
    latents_in,
    out_in,
    next_ref,
    velocity_ref,
    latents_ref,
    update,
    terms,
    hidden,
    latents,
    w_out,
    hidden_next,
    velocity_out,
    latents_next,
    load_sem,
    store_sem,
):
    loads = [
        pltpu.make_async_copy(source, target, load_sem.at[number])
        for number, (source, target) in enumerate(
            (
                (update_in, update),
                (hidden_in, hidden),
                (terms_in, terms),
                (out_in, w_out),
                (latents_in, latents),
            )
        )
    ]
    stores = [
        pltpu.make_async_copy(source, target, store_sem.at[number])
        for number, (source, target) in enumerate(
            (
                (hidden_next, next_ref),
                (velocity_out, velocity_ref),
                (latents_next, latents_ref),
            )
        )
    ]
    for load in loads:
        load.start()
    loads[0].wait()
    loads[1].wait()
    joined_columns = jnp.concatenate([update[p] for p in range(update.shape[0])], axis=1)
    summed = hidden[...].astype(jnp.float32) + joined_columns.astype(jnp.float32)
    hidden_next[...] = summed.astype(jnp.bfloat16)
    stores[0].start()
    average = jnp.mean(summed, axis=1, keepdims=True)
    centered = summed - average
    variance = jnp.mean(centered * centered, axis=1, keepdims=True)
    loads[2].wait()
    width = hidden.shape[1]
    shift_term = terms[0:1, :width]
    gain_term = terms[0:1, width:]
    normed = centered / jnp.sqrt(variance + 1e-05) * (1.0 + gain_term) + shift_term
    loads[3].wait()
    velocity = lax.dot_general(
        normed.astype(jnp.bfloat16),
        w_out[...],
        (((1,), (1,)), ((), ())),
        preferred_element_type=jnp.float32,
    )
    velocity_out[...] = velocity
    stores[1].start()
    loads[4].wait()
    latents_next[...] = latents[...] + terms[1:2, : latents.shape[1]] * velocity
    stores[2].start()
    for store in stores:
        store.wait()


def fused(plan, hidden, latents, base_qkv, control_qkv, step_index, w_join, w_mod, w_out):
    chips, rows, lines, width, pieces = plan
    tokens = hidden.shape[0]
    hbm_spec = pl.BlockSpec(memory_space=pltpu.HBM)
    dma = pltpu.SemaphoreType.DMA
    vmem_limit = 60 * 1024 * 1024
    per_piece = [dma((chips, pieces))] * 4
    update, terms = pl.pallas_call(
        functools.partial(fused_kernel, plan),
        out_shape=(
            jax.ShapeDtypeStruct((chips, tokens, width), jnp.bfloat16),
            jax.ShapeDtypeStruct((2, w_mod.shape[1]), jnp.float32),
        ),
        in_specs=[hbm_spec] * 2 + [pl.BlockSpec(memory_space=pltpu.SMEM)] + [hbm_spec] * 2,
        out_specs=(hbm_spec,) * 2,
        scratch_shapes=[
            pltpu.VMEM(w_mod.shape, jnp.bfloat16),
            pltpu.VMEM((2 * w_join.shape[1], w_join.shape[0]), jnp.bfloat16),
            pltpu.VMEM((2, w_mod.shape[1]), jnp.float32),
            pltpu.VMEM((chips, pieces, 3, tokens, LANES), jnp.bfloat16),
            pltpu.VMEM((chips, pieces, 2, tokens, LANES), jnp.bfloat16),
            pltpu.VMEM((chips, pieces, chips * tokens, LANES), jnp.bfloat16),
            pltpu.VMEM((chips * tokens, width), jnp.float32),
            pltpu.VMEM((chips, tokens, width), jnp.bfloat16),
            dma((4,)),
            dma((pieces,)),
            *per_piece,
            dma,
            dma,
            *per_piece,
            dma((chips,)),
            dma((chips,)),
        ],
        compiler_params=pltpu.CompilerParams(
            collective_id=0, has_side_effects=True, vmem_limit_bytes=vmem_limit
        ),
        name="fused",
    )(base_qkv, control_qkv, step_index, w_join.T, w_mod)
    return pl.pallas_call(
        finish_kernel,
        out_shape=(
            jax.ShapeDtypeStruct(hidden.shape, jnp.bfloat16),
            jax.ShapeDtypeStruct(latents.shape, jnp.float32),
            jax.ShapeDtypeStruct(latents.shape, jnp.float32),
        ),
        in_specs=[hbm_spec] * 5,
        out_specs=(hbm_spec,) * 3,
        scratch_shapes=[
            pltpu.VMEM(update.shape, jnp.bfloat16),
            pltpu.VMEM(terms.shape, jnp.float32),
            pltpu.VMEM(hidden.shape, jnp.bfloat16),
            pltpu.VMEM(latents.shape, jnp.float32),
            pltpu.VMEM(w_out.shape[::-1], jnp.bfloat16),
            pltpu.VMEM(hidden.shape, jnp.bfloat16),
            pltpu.VMEM(latents.shape, jnp.float32),
            pltpu.VMEM(latents.shape, jnp.float32),
            dma((5,)),
            dma((3,)),
        ],
        compiler_params=pltpu.CompilerParams(vmem_limit_bytes=vmem_limit),
        name="norm_and_step",
    )(update, terms, hidden, latents, w_out.T)


def plan_for(count, sections_width, section_width):
    if count % 4 != 0:
        return None
    chips = count // 2
    width = sections_width // chips
    if sections_width % chips or width % LANES or section_width % width:
        return None
    return (chips, 2, chips // 2, width, width // LANES)


def local(hidden, latents, base_qkv, control_qkv, step_index, w_join, w_mod, w_out, count):
    plan = plan_for(count, w_join.shape[0], base_qkv.shape[2])
    if plan is None or hidden.shape[0] % 8 or (plan[0] * hidden.shape[0]) % 16:
        return gathered(
            hidden, latents, base_qkv, control_qkv, step_index, w_join, w_mod, w_out
        )
    return fused(
        plan, hidden, latents, base_qkv, control_qkv, step_index, w_join, w_mod, w_out
    )


def solution(mesh):
    in_specs = (
        P(("groups", "seq"), None),
        P(("groups", "seq"), None),
        P(None, ("groups", "seq"), None),
        P(None, ("groups", "seq"), None),
        P(),
        P(None, "seq"),
        P(),
        P(),
    )
    out_specs = (P(("groups", "seq"), None), P(("groups", "seq"), None), P(("groups", "seq"), None))
    return jax.shard_map(
        functools.partial(local, count=mesh.shape["seq"]),
        mesh=mesh,
        in_specs=in_specs,
        out_specs=out_specs,
        check_vma=False,
    )
```

```python
import functools
import math

import jax
import jax.numpy as jnp
from jax import lax
from jax.experimental import pallas as pl
from jax.experimental.pallas import tpu as pltpu
from jax.sharding import PartitionSpec as P

D = 3072
HD = 64
TEMB = 512
HEADS = 24
STEPS = 50


def time_terms(step_index):
    step_value = step_index[0].astype(jnp.float32)
    level_now = jnp.cos(0.5 * math.pi * step_value / STEPS)
    level_next = jnp.cos(0.5 * math.pi * (step_value + 1.0) / STEPS)
    half_width = TEMB // 2
    frequency = jnp.exp(
        -math.log(10000.0) * jnp.arange(half_width).astype(jnp.float32) / half_width
    )
    angles = 1000.0 * level_now * frequency
    embedding = jnp.concatenate([jnp.cos(angles), jnp.sin(angles)]).astype(jnp.bfloat16)
    return (embedding, level_next - level_now)


def attend(state, queries, shard_rows):
    running_max, running_sum, weighted = state
    count = shard_rows.shape[1]
    keys_block = shard_rows[0].reshape(count, HEADS, HD)
    values_block = shard_rows[1].reshape(count, HEADS, HD)
    scores = jnp.einsum(
        "qhd,khd->qhk", queries, keys_block, preferred_element_type=jnp.float32
    ) * HD ** (-0.5)
    newest_max = jnp.max(scores, axis=2)
    rescale = jnp.exp(running_max - newest_max)
    exponent = jnp.exp(scores - newest_max[:, :, None])
    running_sum = running_sum * rescale + jnp.sum(exponent, axis=2)
    weighted = weighted * rescale[:, :, None] + jnp.einsum(
        "qhk,khd->qhd",
        exponent.astype(jnp.bfloat16),
        values_block,
        preferred_element_type=jnp.float32,
    )
    return (newest_max, running_sum, weighted)


def finish(state):
    running_max, running_sum, weighted = state
    outputs = (weighted / running_sum[:, :, None]).astype(jnp.bfloat16)
    return outputs.reshape(outputs.shape[0], HEADS * HD)


def gathered(hidden, latents, base_qkv, control_qkv, step_index, w_join, w_mod, w_out):
    tokens_here = hidden.shape[0]
    base_queries = base_qkv[0].reshape(tokens_here, HEADS, HD)
    control_queries = control_qkv[0].reshape(tokens_here, HEADS, HD)
    base_pairs = base_qkv[1:]
    control_pairs = control_qkv[1:]
    initial = (
        jnp.full((tokens_here, HEADS), -jnp.inf, jnp.float32),
        jnp.zeros((tokens_here, HEADS), jnp.float32),
        jnp.zeros((tokens_here, HEADS, HD), jnp.float32),
    )
    base_state = attend(
        initial, base_queries, lax.all_gather(base_pairs, "seq", axis=1, tiled=True)
    )
    control_state = attend(
        initial, control_queries, lax.all_gather(control_pairs, "seq", axis=1, tiled=True)
    )
    joined = jnp.concatenate([finish(base_state), finish(control_state)], axis=1)
    column_part = jnp.dot(
        lax.all_gather(joined, "seq", axis=0, tiled=True),
        w_join,
        preferred_element_type=jnp.float32,
    )
    update = lax.all_to_all(
        column_part.astype(jnp.bfloat16), "seq", split_axis=0, concat_axis=1, tiled=True
    ).astype(column_part.dtype)
    summed = hidden.astype(jnp.float32) + update
    hidden_next = summed.astype(jnp.bfloat16)
    embedding, step_size = time_terms(step_index)
    modulation = jnp.dot(embedding[None, :], w_mod, preferred_element_type=jnp.float32)[0]
    shift_term = modulation[:D]
    gain_term = modulation[D:]
    average = jnp.mean(summed, axis=1, keepdims=True)
    centered = summed - average
    variance = jnp.mean(centered * centered, axis=1, keepdims=True)
    normed = (centered / jnp.sqrt(variance + 1e-05) * (1.0 + gain_term) + shift_term).astype(
        jnp.bfloat16
    )
    velocity = jnp.dot(normed, w_out, preferred_element_type=jnp.float32)
    latents_next = latents + step_size * velocity
    return (hidden_next, velocity, latents_next)


LANES = 128
MESH = pl.DeviceIdType.MESH


def fused_kernel(
    plan,
    base_in,
    control_in,
    step_in,
    join_in,
    mod_in,
    update_in,
    terms_ref,
    w_mod,
    w_join,
    modulation,
    heads_own,
    heads_other,
    joined,
    total,
    update_out,
    load_sem,
    own_sem,
    swap_send,
    swap_recv,
    pass_send,
    pass_recv,
    side_send,
    side_recv,
    right_send,
    left_send,
    cross_send,
    join_recv,
    back_send,
    back_recv,
):
    chips, rows, lines, width, pieces = plan
    tokens = base_in.shape[1]
    section = base_in.shape[2]
    per_section = section // width
    me = lax.axis_index("seq")
    core = lax.rem(me, 2)
    chip = me // 2
    row = lax.rem(chip, rows)
    place = chip // rows

    def device(other, other_core):
        return {"seq": other * 2 + other_core}

    def remote(src, dst, send, recv, target):
        return pltpu.make_async_remote_copy(
            src_ref=src,
            dst_ref=dst,
            send_sem=send,
            recv_sem=recv,
            device_id=target,
            device_id_type=MESH,
        )

    half_rows = join_in.shape[0]

    def join_half(which):
        return w_join.at[pl.ds(pl.multiple_of(which * half_rows, half_rows), half_rows), :]

    mod_load = pltpu.make_async_copy(mod_in, w_mod, load_sem.at[0])
    join_load = pltpu.make_async_copy(join_in, join_half(core), load_sem.at[1])
    barrier = pltpu.get_barrier_semaphore()
    for step in range(1, chips):
        pl.semaphore_signal(
            barrier,
            inc=1,
            device_id=device(lax.rem(chip + step, chips), core),
            device_id_type=MESH,
        )
    pl.semaphore_signal(barrier, inc=1, device_id=device(chip, 1 - core), device_id_type=MESH)
    mod_load.start()
    join_load.start()
    step_value = jnp.full((1, TEMB), step_in[0].astype(jnp.float32))
    level_now = jnp.cos(0.5 * math.pi * step_value / STEPS)
    level_next = jnp.cos(0.5 * math.pi * (step_value + 1.0) / STEPS)
    half_width = TEMB // 2
    index = lax.broadcasted_iota(jnp.int32, (1, TEMB), 1)
    place_in_half = jnp.where(index < half_width, index, index - half_width).astype(jnp.float32)
    frequency = jnp.exp(-math.log(10000.0) * place_in_half / half_width)
    angles = 1000.0 * level_now * frequency
    embedding = jnp.where(index < half_width, jnp.cos(angles), jnp.sin(angles))
    embedding = jnp.broadcast_to(embedding, (16, TEMB)).astype(jnp.bfloat16)
    step_size = level_next - level_now
    pl.semaphore_wait(barrier, chips)

    def piece_of(ref, target, piece):
        start = lax.rem(target, per_section) * width + piece * LANES
        return ref.at[:, :, pl.ds(pl.multiple_of(start, LANES), LANES)]

    def from_section(target, act):
        @pl.when(target < per_section)
        def _():
            act(base_in)

        @pl.when(target >= per_section)
        def _():
            act(control_in)

    far_first = sorted(range(1, chips), key=lambda step: abs(2 * step - chips))

    def swap(ref, target, step, piece):
        return remote(
            piece_of(ref, target, piece),
            heads_own.at[chip, piece],
            swap_send.at[step, piece],
            swap_recv.at[chip, piece],
            device(target, core),
        )

    def own_copy(ref, piece):
        return pltpu.make_async_copy(
            piece_of(ref, chip, piece), heads_own.at[chip, piece], own_sem.at[piece]
        )

    def pass_on(source, piece):
        return remote(
            heads_own.at[source, piece, 1:3],
            heads_other.at[source, piece],
            pass_send.at[source, piece],
            pass_recv.at[source, piece],
            device(chip, 1 - core),
        )

    side = remote(join_in, join_half(core), side_send, side_recv, device(chip, 1 - core))
    def send_piece(step, piece):
        target = lax.rem(chip + step, chips)
        from_section(target, lambda ref: swap(ref, target, step, piece).start())

    for step in far_first:
        send_piece(step, 0)
    for piece in range(pieces):
        from_section(chip, lambda ref, p=piece: own_copy(ref, p).start())
    side.start()

    mod_load.wait()
    for start in range(0, w_mod.shape[1], TEMB):
        modulation[0:1, start : start + TEMB] = jnp.dot(
            embedding, w_mod[:, start : start + TEMB], preferred_element_type=jnp.float32
        )[0:1]
        modulation[1:2, start : start + TEMB] = step_size
    terms_store = pltpu.make_async_copy(modulation, terms_ref, load_sem.at[2])
    terms_store.start()

    lane = lax.broadcasted_iota(jnp.int32, (chips * tokens, LANES), 1)

    def attention(piece):
        def rows_of(ref, kind):
            part = ref[:, piece, kind].astype(jnp.float32)
            return part.reshape(chips * tokens, LANES)

        queries = rows_of(heads_own, 0) * HD ** (-0.5)
        keys = jnp.concatenate([rows_of(heads_own, 1), rows_of(heads_other, 0)], axis=0)
        values = jnp.concatenate([rows_of(heads_own, 2), rows_of(heads_other, 1)], axis=0)
        keys = keys.astype(jnp.bfloat16)
        values = values.astype(jnp.bfloat16)
        result = None
        for head in range(LANES // HD):
            mine = (lane >= head * HD) & (lane < (head + 1) * HD)
            query = jnp.where(mine, queries, 0.0).astype(jnp.bfloat16)
            scores = lax.dot_general(
                query, keys, (((1,), (1,)), ((), ())), preferred_element_type=jnp.float32
            )
            exponent = jnp.exp(scores - jnp.max(scores, axis=1, keepdims=True))
            row_sum = jnp.sum(exponent, axis=1, keepdims=True)
            mixed = jnp.dot(
                exponent.astype(jnp.bfloat16), values, preferred_element_type=jnp.float32
            )
            mixed = mixed / row_sum
            result = mixed if result is None else jnp.where(mine, mixed, result)
        joined[chip, piece] = result.astype(jnp.bfloat16)

    def hop(block_chip, piece, send, target):
        view = joined.at[block_chip, piece]
        return remote(
            view,
            view,
            send.at[block_chip, piece],
            join_recv.at[block_chip, piece],
            device(target, core),
        )

    def other_row_step(step):
        return lax.rem(row + step, rows)

    def hand_on(origin, piece, act):
        block_chip = origin * rows + row
        for step in range(1, rows):
            act(hop(block_chip, piece, cross_send, place * rows + other_row_step(step)))

        @pl.when((origin <= place) & (place < lines - 1))
        def _():
            act(hop(block_chip, piece, right_send, chip + rows))

        @pl.when((origin >= place) & (place > 0))
        def _():
            act(hop(block_chip, piece, left_send, chip - rows))

    def at_distance(distance, act):
        @pl.when(place >= distance)
        def _():
            act(place - distance)

        @pl.when(place + distance < lines)
        def _():
            act(place + distance)

    def arrive(block_chip, piece):
        view = joined.at[block_chip, piece]
        remote(
            view,
            view,
            cross_send.at[block_chip, piece],
            join_recv.at[block_chip, piece],
            device(chip, 1 - core),
        ).wait_recv()

    def relay(distance, piece):
        def act(origin):
            arrive(origin * rows + row, piece)
            hand_on(origin, piece, lambda copy: copy.start())

        at_distance(distance, act)

    for piece in range(pieces):
        from_section(chip, lambda ref, p=piece: own_copy(ref, p).wait())
        pass_on(chip, piece).start()
        for sent, step in enumerate(reversed(far_first)):
            source = lax.rem(chip - step + chips, chips)
            remote(
                heads_own.at[source, piece],
                heads_own.at[source, piece],
                swap_send.at[step, piece],
                swap_recv.at[source, piece],
                device(source, core),
            ).wait_recv()
            pass_on(source, piece).start()
            if piece + 1 < pieces:
                send_piece(far_first[sent], piece + 1)
        for step in range(chips):
            pass_on(lax.rem(chip - step + chips, chips), piece).wait_recv()
        attention(piece)
        hand_on(place, piece, lambda copy: copy.start())
        for earlier in range(piece):
            distance = piece - earlier
            if distance < lines:
                relay(distance, earlier)

    join_load.wait()
    side.wait_recv()

    def project(block_chip):
        block_columns = pl.ds(pl.multiple_of(block_chip * width, LANES), width)
        total[...] += lax.dot_general(
            jnp.concatenate([joined[block_chip, p] for p in range(pieces)], axis=1),
            w_join[:, block_columns],
            (((1,), (1,)), ((), ())),
            preferred_element_type=jnp.float32,
        )

    total[...] = jnp.zeros_like(total)
    done = {p: pieces - 1 - p for p in range(pieces)}
    for distance in range(lines):
        for piece in range(pieces):
            if done[piece] < distance:
                relay(distance, piece)
        if distance == 0:
            project(chip)
        else:
            at_distance(distance, lambda origin: project(origin * rows + row))

    def cross(origin, step):
        block_chip = origin * rows + other_row_step(step)
        for piece in range(pieces):
            arrive(block_chip, piece)
        project(block_chip)

    for distance in range(lines):
        for step in range(1, rows):
            if distance == 0:
                cross(place, step)
            else:
                at_distance(distance, lambda origin, s=step: cross(origin, s))

    update_out[...] = total[...].reshape(chips, tokens, width).astype(jnp.bfloat16)

    def back(target, step):
        return remote(
            update_out.at[target],
            update_in.at[chip],
            back_send.at[step],
            back_recv.at[chip],
            device(target, core),
        )

    for step in far_first:
        back(lax.rem(chip + step, chips), step).start()
    own_back = pltpu.make_async_copy(update_out.at[chip], update_in.at[chip], load_sem.at[3])
    own_back.start()
    for step in range(1, chips):
        source = lax.rem(chip - step + chips, chips)
        remote(
            update_out.at[source],
            update_in.at[source],
            back_send.at[step],
            back_recv.at[source],
            device(source, core),
        ).wait_recv()
    for piece in range(pieces):
        for step in range(1, chips):
            swap(base_in, lax.rem(chip + step, chips), step, piece).wait_send()
        for source in range(chips):
            pass_on(source, piece).wait_send()
        for distance in range(lines):
            if distance == 0:
                hand_on(place, piece, lambda copy: copy.wait_send())
            else:
                at_distance(
                    distance, lambda o, p=piece: hand_on(o, p, lambda copy: copy.wait_send())
                )
    side.wait_send()
    terms_store.wait()
    own_back.wait()
    for step in range(1, chips):
        back(lax.rem(chip + step, chips), step).wait_send()


def finish_kernel(
    update_in,
    terms_in,
    hidden_in,
    latents_in,
    out_in,
    next_ref,
    velocity_ref,
    latents_ref,
    update,
    terms,
    hidden,
    latents,
    w_out,
    hidden_next,
    velocity_out,
    latents_next,
    load_sem,
    store_sem,
):
    loads = [
        pltpu.make_async_copy(source, target, load_sem.at[number])
        for number, (source, target) in enumerate(
            (
                (update_in, update),
                (hidden_in, hidden),
                (terms_in, terms),
                (out_in, w_out),
                (latents_in, latents),
            )
        )
    ]
    stores = [
        pltpu.make_async_copy(source, target, store_sem.at[number])
        for number, (source, target) in enumerate(
            (
                (hidden_next, next_ref),
                (velocity_out, velocity_ref),
                (latents_next, latents_ref),
            )
        )
    ]
    for load in loads:
        load.start()
    loads[0].wait()
    loads[1].wait()
    joined_columns = jnp.concatenate([update[p] for p in range(update.shape[0])], axis=1)
    summed = hidden[...].astype(jnp.float32) + joined_columns.astype(jnp.float32)
    hidden_next[...] = summed.astype(jnp.bfloat16)
    stores[0].start()
    average = jnp.mean(summed, axis=1, keepdims=True)
    centered = summed - average
    variance = jnp.mean(centered * centered, axis=1, keepdims=True)
    loads[2].wait()
    width = hidden.shape[1]
    shift_term = terms[0:1, :width]
    gain_term = terms[0:1, width:]
    normed = centered / jnp.sqrt(variance + 1e-05) * (1.0 + gain_term) + shift_term
    loads[3].wait()
    velocity = lax.dot_general(
        normed.astype(jnp.bfloat16),
        w_out[...],
        (((1,), (1,)), ((), ())),
        preferred_element_type=jnp.float32,
    )
    velocity_out[...] = velocity
    stores[1].start()
    loads[4].wait()
    latents_next[...] = latents[...] + terms[1:2, : latents.shape[1]] * velocity
    stores[2].start()
    for store in stores:
        store.wait()


def fused(plan, hidden, latents, base_qkv, control_qkv, step_index, w_join, w_mod, w_out):
    chips, rows, lines, width, pieces = plan
    tokens = hidden.shape[0]
    hbm_spec = pl.BlockSpec(memory_space=pltpu.HBM)
    dma = pltpu.SemaphoreType.DMA
    vmem_limit = 60 * 1024 * 1024
    per_piece = [dma((chips, pieces))] * 4
    update, terms = pl.pallas_call(
        functools.partial(fused_kernel, plan),
        out_shape=(
            jax.ShapeDtypeStruct((chips, tokens, width), jnp.bfloat16),
            jax.ShapeDtypeStruct((2, w_mod.shape[1]), jnp.float32),
        ),
        in_specs=[hbm_spec] * 2 + [pl.BlockSpec(memory_space=pltpu.SMEM)] + [hbm_spec] * 2,
        out_specs=(hbm_spec,) * 2,
        scratch_shapes=[
            pltpu.VMEM(w_mod.shape, jnp.bfloat16),
            pltpu.VMEM((2 * w_join.shape[1], w_join.shape[0]), jnp.bfloat16),
            pltpu.VMEM((2, w_mod.shape[1]), jnp.float32),
            pltpu.VMEM((chips, pieces, 3, tokens, LANES), jnp.bfloat16),
            pltpu.VMEM((chips, pieces, 2, tokens, LANES), jnp.bfloat16),
            pltpu.VMEM((chips, pieces, chips * tokens, LANES), jnp.bfloat16),
            pltpu.VMEM((chips * tokens, width), jnp.float32),
            pltpu.VMEM((chips, tokens, width), jnp.bfloat16),
            dma((4,)),
            dma((pieces,)),
            *per_piece,
            dma,
            dma,
            *per_piece,
            dma((chips,)),
            dma((chips,)),
        ],
        compiler_params=pltpu.CompilerParams(
            collective_id=0, has_side_effects=True, vmem_limit_bytes=vmem_limit
        ),
        name="fused",
    )(base_qkv, control_qkv, step_index, w_join.T, w_mod)
    return pl.pallas_call(
        finish_kernel,
        out_shape=(
            jax.ShapeDtypeStruct(hidden.shape, jnp.bfloat16),
            jax.ShapeDtypeStruct(latents.shape, jnp.float32),
            jax.ShapeDtypeStruct(latents.shape, jnp.float32),
        ),
        in_specs=[hbm_spec] * 5,
        out_specs=(hbm_spec,) * 3,
        scratch_shapes=[
            pltpu.VMEM(update.shape, jnp.bfloat16),
            pltpu.VMEM(terms.shape, jnp.float32),
            pltpu.VMEM(hidden.shape, jnp.bfloat16),
            pltpu.VMEM(latents.shape, jnp.float32),
            pltpu.VMEM(w_out.shape[::-1], jnp.bfloat16),
            pltpu.VMEM(hidden.shape, jnp.bfloat16),
            pltpu.VMEM(latents.shape, jnp.float32),
            pltpu.VMEM(latents.shape, jnp.float32),
            dma((5,)),
            dma((3,)),
        ],
        compiler_params=pltpu.CompilerParams(vmem_limit_bytes=vmem_limit),
        name="norm_and_step",
    )(update, terms, hidden, latents, w_out.T)


def plan_for(count, sections_width, section_width):
    if count % 4 != 0:
        return None
    chips = count // 2
    width = sections_width // chips
    if sections_width % chips or width % LANES or section_width % width:
        return None
    return (chips, 2, chips // 2, width, width // LANES)


def local(hidden, latents, base_qkv, control_qkv, step_index, w_join, w_mod, w_out, count):
    plan = plan_for(count, w_join.shape[0], base_qkv.shape[2])
    if plan is None or hidden.shape[0] % 8 or (plan[0] * hidden.shape[0]) % 16:
        return gathered(
            hidden, latents, base_qkv, control_qkv, step_index, w_join, w_mod, w_out
        )
    return fused(
        plan, hidden, latents, base_qkv, control_qkv, step_index, w_join, w_mod, w_out
    )


def solution(mesh):
    in_specs = (
        P(("groups", "seq"), None),
        P(("groups", "seq"), None),
        P(None, ("groups", "seq"), None),
        P(None, ("groups", "seq"), None),
        P(),
        P(None, "seq"),
        P(),
        P(),
    )
    out_specs = (P(("groups", "seq"), None), P(("groups", "seq"), None), P(("groups", "seq"), None))
    return jax.shard_map(
        functools.partial(local, count=mesh.shape["seq"]),
        mesh=mesh,
        in_specs=in_specs,
        out_specs=out_specs,
        check_vma=False,
    )
```

```python
import functools
import math

import jax
import jax.numpy as jnp
from jax import lax
from jax.experimental import pallas as pl
from jax.experimental.pallas import tpu as pltpu
from jax.sharding import PartitionSpec as P

D = 3072
HD = 64
TEMB = 512
HEADS = 24
STEPS = 50


def time_terms(step_index):
    step_value = step_index[0].astype(jnp.float32)
    level_now = jnp.cos(0.5 * math.pi * step_value / STEPS)
    level_next = jnp.cos(0.5 * math.pi * (step_value + 1.0) / STEPS)
    half_width = TEMB // 2
    frequency = jnp.exp(
        -math.log(10000.0) * jnp.arange(half_width).astype(jnp.float32) / half_width
    )
    angles = 1000.0 * level_now * frequency
    embedding = jnp.concatenate([jnp.cos(angles), jnp.sin(angles)]).astype(jnp.bfloat16)
    return (embedding, level_next - level_now)


def attend(state, queries, shard_rows):
    running_max, running_sum, weighted = state
    count = shard_rows.shape[1]
    keys_block = shard_rows[0].reshape(count, HEADS, HD)
    values_block = shard_rows[1].reshape(count, HEADS, HD)
    scores = jnp.einsum(
        "qhd,khd->qhk", queries, keys_block, preferred_element_type=jnp.float32
    ) * HD ** (-0.5)
    newest_max = jnp.max(scores, axis=2)
    rescale = jnp.exp(running_max - newest_max)
    exponent = jnp.exp(scores - newest_max[:, :, None])
    running_sum = running_sum * rescale + jnp.sum(exponent, axis=2)
    weighted = weighted * rescale[:, :, None] + jnp.einsum(
        "qhk,khd->qhd",
        exponent.astype(jnp.bfloat16),
        values_block,
        preferred_element_type=jnp.float32,
    )
    return (newest_max, running_sum, weighted)


def finish(state):
    running_max, running_sum, weighted = state
    outputs = (weighted / running_sum[:, :, None]).astype(jnp.bfloat16)
    return outputs.reshape(outputs.shape[0], HEADS * HD)


def gathered(hidden, latents, base_qkv, control_qkv, step_index, w_join, w_mod, w_out):
    tokens_here = hidden.shape[0]
    base_queries = base_qkv[0].reshape(tokens_here, HEADS, HD)
    control_queries = control_qkv[0].reshape(tokens_here, HEADS, HD)
    base_pairs = base_qkv[1:]
    control_pairs = control_qkv[1:]
    initial = (
        jnp.full((tokens_here, HEADS), -jnp.inf, jnp.float32),
        jnp.zeros((tokens_here, HEADS), jnp.float32),
        jnp.zeros((tokens_here, HEADS, HD), jnp.float32),
    )
    base_state = attend(
        initial, base_queries, lax.all_gather(base_pairs, "seq", axis=1, tiled=True)
    )
    control_state = attend(
        initial, control_queries, lax.all_gather(control_pairs, "seq", axis=1, tiled=True)
    )
    joined = jnp.concatenate([finish(base_state), finish(control_state)], axis=1)
    column_part = jnp.dot(
        lax.all_gather(joined, "seq", axis=0, tiled=True),
        w_join,
        preferred_element_type=jnp.float32,
    )
    update = lax.all_to_all(
        column_part.astype(jnp.bfloat16), "seq", split_axis=0, concat_axis=1, tiled=True
    ).astype(column_part.dtype)
    summed = hidden.astype(jnp.float32) + update
    hidden_next = summed.astype(jnp.bfloat16)
    embedding, step_size = time_terms(step_index)
    modulation = jnp.dot(embedding[None, :], w_mod, preferred_element_type=jnp.float32)[0]
    shift_term = modulation[:D]
    gain_term = modulation[D:]
    average = jnp.mean(summed, axis=1, keepdims=True)
    centered = summed - average
    variance = jnp.mean(centered * centered, axis=1, keepdims=True)
    normed = (centered / jnp.sqrt(variance + 1e-05) * (1.0 + gain_term) + shift_term).astype(
        jnp.bfloat16
    )
    velocity = jnp.dot(normed, w_out, preferred_element_type=jnp.float32)
    latents_next = latents + step_size * velocity
    return (hidden_next, velocity, latents_next)


LANES = 128
MESH = pl.DeviceIdType.MESH


def fused_kernel(
    plan,
    base_in,
    control_in,
    step_in,
    join_in,
    mod_in,
    update_in,
    terms_ref,
    w_mod,
    w_join,
    modulation,
    heads_own,
    heads_other,
    joined,
    total,
    update_out,
    load_sem,
    own_sem,
    swap_send,
    swap_recv,
    pass_send,
    pass_recv,
    side_send,
    side_recv,
    right_send,
    left_send,
    far_right_send,
    far_left_send,
    cross_send,
    join_recv,
    back_send,
    back_recv,
):
    chips, rows, lines, width, pieces = plan
    tokens = base_in.shape[1]
    section = base_in.shape[2]
    per_section = section // width
    me = lax.axis_index("seq")
    core = lax.rem(me, 2)
    chip = me // 2
    row = lax.rem(chip, rows)
    place = chip // rows

    def device(other, other_core):
        return {"seq": other * 2 + other_core}

    def remote(src, dst, send, recv, target):
        return pltpu.make_async_remote_copy(
            src_ref=src,
            dst_ref=dst,
            send_sem=send,
            recv_sem=recv,
            device_id=target,
            device_id_type=MESH,
        )

    half_rows = join_in.shape[0]

    def join_half(which):
        return w_join.at[pl.ds(pl.multiple_of(which * half_rows, half_rows), half_rows), :]

    mod_load = pltpu.make_async_copy(mod_in, w_mod, load_sem.at[0])
    join_load = pltpu.make_async_copy(join_in, join_half(core), load_sem.at[1])
    barrier = pltpu.get_barrier_semaphore()
    for step in range(1, chips):
        pl.semaphore_signal(
            barrier,
            inc=1,
            device_id=device(lax.rem(chip + step, chips), core),
            device_id_type=MESH,
        )
    pl.semaphore_signal(barrier, inc=1, device_id=device(chip, 1 - core), device_id_type=MESH)
    mod_load.start()
    join_load.start()
    step_value = jnp.full((1, TEMB), step_in[0].astype(jnp.float32))
    level_now = jnp.cos(0.5 * math.pi * step_value / STEPS)
    level_next = jnp.cos(0.5 * math.pi * (step_value + 1.0) / STEPS)
    half_width = TEMB // 2
    index = lax.broadcasted_iota(jnp.int32, (1, TEMB), 1)
    place_in_half = jnp.where(index < half_width, index, index - half_width).astype(jnp.float32)
    frequency = jnp.exp(-math.log(10000.0) * place_in_half / half_width)
    angles = 1000.0 * level_now * frequency
    embedding = jnp.where(index < half_width, jnp.cos(angles), jnp.sin(angles))
    embedding = jnp.broadcast_to(embedding, (16, TEMB)).astype(jnp.bfloat16)
    step_size = level_next - level_now
    pl.semaphore_wait(barrier, chips)

    def piece_of(ref, target, piece):
        start = lax.rem(target, per_section) * width + piece * LANES
        return ref.at[:, :, pl.ds(pl.multiple_of(start, LANES), LANES)]

    def from_section(target, act):
        @pl.when(target < per_section)
        def _():
            act(base_in)

        @pl.when(target >= per_section)
        def _():
            act(control_in)

    far_first = sorted(range(1, chips), key=lambda step: abs(2 * step - chips))

    def swap(ref, target, step, piece):
        return remote(
            piece_of(ref, target, piece),
            heads_own.at[chip, piece],
            swap_send.at[step, piece],
            swap_recv.at[chip, piece],
            device(target, core),
        )

    def own_copy(ref, piece):
        return pltpu.make_async_copy(
            piece_of(ref, chip, piece), heads_own.at[chip, piece], own_sem.at[piece]
        )

    def pass_on(source, piece):
        return remote(
            heads_own.at[source, piece, 1:3],
            heads_other.at[source, piece],
            pass_send.at[source, piece],
            pass_recv.at[source, piece],
            device(chip, 1 - core),
        )

    side = remote(join_in, join_half(core), side_send, side_recv, device(chip, 1 - core))
    for piece in range(pieces):
        for step in far_first:
            target = lax.rem(chip + step, chips)
            from_section(
                target, lambda ref, t=target, s=step, p=piece: swap(ref, t, s, p).start()
            )
        from_section(chip, lambda ref, p=piece: own_copy(ref, p).start())
    side.start()

    mod_blocks = w_mod.shape[1] // TEMB

    def modulate(first, last):
        for block in range(first, last):
            cut = slice(block * TEMB, (block + 1) * TEMB)
            modulation[0:1, cut] = jnp.dot(
                embedding, w_mod[:, cut], preferred_element_type=jnp.float32
            )[0:1]
            modulation[1:2, cut] = step_size

    lane = lax.broadcasted_iota(jnp.int32, (chips * tokens, LANES), 1)

    def attention(piece):
        def rows_of(ref, kind):
            part = ref[:, piece, kind].astype(jnp.float32)
            return part.reshape(chips * tokens, LANES)

        queries = rows_of(heads_own, 0) * HD ** (-0.5)
        keys = jnp.concatenate([rows_of(heads_own, 1), rows_of(heads_other, 0)], axis=0)
        values = jnp.concatenate([rows_of(heads_own, 2), rows_of(heads_other, 1)], axis=0)
        keys = keys.astype(jnp.bfloat16)
        values = values.astype(jnp.bfloat16)
        result = None
        for head in range(LANES // HD):
            mine = (lane >= head * HD) & (lane < (head + 1) * HD)
            query = jnp.where(mine, queries, 0.0).astype(jnp.bfloat16)
            scores = lax.dot_general(
                query, keys, (((1,), (1,)), ((), ())), preferred_element_type=jnp.float32
            )
            exponent = jnp.exp(scores - jnp.max(scores, axis=1, keepdims=True))
            row_sum = jnp.sum(exponent, axis=1, keepdims=True)
            mixed = jnp.dot(
                exponent.astype(jnp.bfloat16), values, preferred_element_type=jnp.float32
            )
            mixed = mixed / row_sum
            result = mixed if result is None else jnp.where(mine, mixed, result)
        joined[chip, piece] = result.astype(jnp.bfloat16)

    def hop(block_chip, piece, send, target):
        view = joined.at[block_chip, piece]
        return remote(
            view,
            view,
            send.at[block_chip, piece],
            join_recv.at[block_chip, piece],
            device(target, core),
        )

    def other_row_step(step):
        return lax.rem(row + step, rows)

    def to_other_rows(origin, piece, act):
        for step in range(1, rows):
            target = place * rows + other_row_step(step)
            act(hop(origin * rows + row, piece, cross_send, target))

    def hand_out(piece, act):
        to_other_rows(place, piece, act)

        @pl.when(place < lines - 2)
        def _():
            act(hop(chip, piece, far_right_send, chip + 2 * rows))

        @pl.when(place > 1)
        def _():
            act(hop(chip, piece, far_left_send, chip - 2 * rows))

        @pl.when(place < lines - 1)
        def _():
            act(hop(chip, piece, right_send, chip + rows))

        @pl.when(place > 0)
        def _():
            act(hop(chip, piece, left_send, chip - rows))

    def hand_on(origin, piece, act):
        block_chip = origin * rows + row

        @pl.when((origin <= place - 2) & (place < lines - 1))
        def _():
            act(hop(block_chip, piece, right_send, chip + rows))

        @pl.when((origin >= place + 2) & (place > 0))
        def _():
            act(hop(block_chip, piece, left_send, chip - rows))

        to_other_rows(origin, piece, act)

    def at_distance(distance, act):
        @pl.when(place >= distance)
        def _():
            act(place - distance)

        @pl.when(place + distance < lines)
        def _():
            act(place + distance)

    def arrive(block_chip, piece):
        view = joined.at[block_chip, piece]
        remote(
            view,
            view,
            cross_send.at[block_chip, piece],
            join_recv.at[block_chip, piece],
            device(chip, 1 - core),
        ).wait_recv()

    def relay(distance, piece):
        def act(origin):
            arrive(origin * rows + row, piece)
            hand_on(origin, piece, lambda copy: copy.start())

        at_distance(distance, act)

    for piece in range(pieces):
        from_section(chip, lambda ref, p=piece: own_copy(ref, p).wait())
        pass_on(chip, piece).start()
        for step in reversed(far_first):
            source = lax.rem(chip - step + chips, chips)
            remote(
                heads_own.at[source, piece],
                heads_own.at[source, piece],
                swap_send.at[step, piece],
                swap_recv.at[source, piece],
                device(source, core),
            ).wait_recv()
            pass_on(source, piece).start()
        for step in range(chips):
            pass_on(lax.rem(chip - step + chips, chips), piece).wait_recv()
        attention(piece)
        hand_out(piece, lambda copy: copy.start())

    join_load.wait()
    side.wait_recv()

    def project(block_chip):
        block_columns = pl.ds(pl.multiple_of(block_chip * width, LANES), width)
        total[...] += lax.dot_general(
            jnp.concatenate([joined[block_chip, p] for p in range(pieces)], axis=1),
            w_join[:, block_columns],
            (((1,), (1,)), ((), ())),
            preferred_element_type=jnp.float32,
        )

    total[...] = jnp.zeros_like(total)
    mod_load.wait()
    for distance in range(lines):
        if distance == 0:
            project(chip)
        else:
            for piece in range(pieces):
                relay(distance, piece)
            at_distance(distance, lambda origin: project(origin * rows + row))
        modulate(distance * mod_blocks // lines, (distance + 1) * mod_blocks // lines)
    terms_store = pltpu.make_async_copy(modulation, terms_ref, load_sem.at[2])
    terms_store.start()

    def cross(origin, step):
        block_chip = origin * rows + other_row_step(step)
        for piece in range(pieces):
            arrive(block_chip, piece)
        project(block_chip)

    for distance in range(lines):
        for step in range(1, rows):
            if distance == 0:
                cross(place, step)
            else:
                at_distance(distance, lambda origin, s=step: cross(origin, s))

    update_out[...] = total[...].reshape(chips, tokens, width).astype(jnp.bfloat16)

    def back(target, step):
        return remote(
            update_out.at[target],
            update_in.at[chip],
            back_send.at[step],
            back_recv.at[chip],
            device(target, core),
        )

    for step in far_first:
        back(lax.rem(chip + step, chips), step).start()
    own_back = pltpu.make_async_copy(update_out.at[chip], update_in.at[chip], load_sem.at[3])
    own_back.start()
    for step in range(1, chips):
        source = lax.rem(chip - step + chips, chips)
        remote(
            update_out.at[source],
            update_in.at[source],
            back_send.at[step],
            back_recv.at[source],
            device(source, core),
        ).wait_recv()
    for piece in range(pieces):
        for step in range(1, chips):
            swap(base_in, lax.rem(chip + step, chips), step, piece).wait_send()
        for source in range(chips):
            pass_on(source, piece).wait_send()
        for distance in range(lines):
            if distance == 0:
                hand_out(piece, lambda copy: copy.wait_send())
            else:
                at_distance(
                    distance, lambda o, p=piece: hand_on(o, p, lambda copy: copy.wait_send())
                )
    side.wait_send()
    terms_store.wait()
    own_back.wait()
    for step in range(1, chips):
        back(lax.rem(chip + step, chips), step).wait_send()


def finish_kernel(
    update_in,
    terms_in,
    hidden_in,
    latents_in,
    out_in,
    next_ref,
    velocity_ref,
    latents_ref,
    update,
    terms,
    hidden,
    latents,
    w_out,
    hidden_next,
    velocity_out,
    latents_next,
    load_sem,
    store_sem,
):
    loads = [
        pltpu.make_async_copy(source, target, load_sem.at[number])
        for number, (source, target) in enumerate(
            (
                (update_in, update),
                (hidden_in, hidden),
                (terms_in, terms),
                (out_in, w_out),
                (latents_in, latents),
            )
        )
    ]
    stores = [
        pltpu.make_async_copy(source, target, store_sem.at[number])
        for number, (source, target) in enumerate(
            (
                (hidden_next, next_ref),
                (velocity_out, velocity_ref),
                (latents_next, latents_ref),
            )
        )
    ]
    for load in loads:
        load.start()
    loads[0].wait()
    loads[1].wait()
    joined_columns = jnp.concatenate([update[p] for p in range(update.shape[0])], axis=1)
    summed = hidden[...].astype(jnp.float32) + joined_columns.astype(jnp.float32)
    hidden_next[...] = summed.astype(jnp.bfloat16)
    stores[0].start()
    average = jnp.mean(summed, axis=1, keepdims=True)
    centered = summed - average
    variance = jnp.mean(centered * centered, axis=1, keepdims=True)
    loads[2].wait()
    width = hidden.shape[1]
    shift_term = terms[0:1, :width]
    gain_term = terms[0:1, width:]
    normed = centered / jnp.sqrt(variance + 1e-05) * (1.0 + gain_term) + shift_term
    loads[3].wait()
    velocity = lax.dot_general(
        normed.astype(jnp.bfloat16),
        w_out[...],
        (((1,), (1,)), ((), ())),
        preferred_element_type=jnp.float32,
    )
    velocity_out[...] = velocity
    stores[1].start()
    loads[4].wait()
    latents_next[...] = latents[...] + terms[1:2, : latents.shape[1]] * velocity
    stores[2].start()
    for store in stores:
        store.wait()


def fused(plan, hidden, latents, base_qkv, control_qkv, step_index, w_join, w_mod, w_out):
    chips, rows, lines, width, pieces = plan
    tokens = hidden.shape[0]
    hbm_spec = pl.BlockSpec(memory_space=pltpu.HBM)
    dma = pltpu.SemaphoreType.DMA
    vmem_limit = 60 * 1024 * 1024
    per_piece = [dma((chips, pieces))] * 4
    update, terms = pl.pallas_call(
        functools.partial(fused_kernel, plan),
        out_shape=(
            jax.ShapeDtypeStruct((chips, tokens, width), jnp.bfloat16),
            jax.ShapeDtypeStruct((2, w_mod.shape[1]), jnp.float32),
        ),
        in_specs=[hbm_spec] * 2 + [pl.BlockSpec(memory_space=pltpu.SMEM)] + [hbm_spec] * 2,
        out_specs=(hbm_spec,) * 2,
        scratch_shapes=[
            pltpu.VMEM(w_mod.shape, jnp.bfloat16),
            pltpu.VMEM((2 * w_join.shape[1], w_join.shape[0]), jnp.bfloat16),
            pltpu.VMEM((2, w_mod.shape[1]), jnp.float32),
            pltpu.VMEM((chips, pieces, 3, tokens, LANES), jnp.bfloat16),
            pltpu.VMEM((chips, pieces, 2, tokens, LANES), jnp.bfloat16),
            pltpu.VMEM((chips, pieces, chips * tokens, LANES), jnp.bfloat16),
            pltpu.VMEM((chips * tokens, width), jnp.float32),
            pltpu.VMEM((chips, tokens, width), jnp.bfloat16),
            dma((4,)),
            dma((pieces,)),
            *per_piece,
            dma,
            dma,
            *per_piece,
            *per_piece[:2],
            dma((chips,)),
            dma((chips,)),
        ],
        compiler_params=pltpu.CompilerParams(
            collective_id=0, has_side_effects=True, vmem_limit_bytes=vmem_limit
        ),
        name="fused",
    )(base_qkv, control_qkv, step_index, w_join.T, w_mod)
    return pl.pallas_call(
        finish_kernel,
        out_shape=(
            jax.ShapeDtypeStruct(hidden.shape, jnp.bfloat16),
            jax.ShapeDtypeStruct(latents.shape, jnp.float32),
            jax.ShapeDtypeStruct(latents.shape, jnp.float32),
        ),
        in_specs=[hbm_spec] * 5,
        out_specs=(hbm_spec,) * 3,
        scratch_shapes=[
            pltpu.VMEM(update.shape, jnp.bfloat16),
            pltpu.VMEM(terms.shape, jnp.float32),
            pltpu.VMEM(hidden.shape, jnp.bfloat16),
            pltpu.VMEM(latents.shape, jnp.float32),
            pltpu.VMEM(w_out.shape[::-1], jnp.bfloat16),
            pltpu.VMEM(hidden.shape, jnp.bfloat16),
            pltpu.VMEM(latents.shape, jnp.float32),
            pltpu.VMEM(latents.shape, jnp.float32),
            dma((5,)),
            dma((3,)),
        ],
        compiler_params=pltpu.CompilerParams(vmem_limit_bytes=vmem_limit),
        name="norm_and_step",
    )(update, terms, hidden, latents, w_out.T)


def plan_for(count, sections_width, section_width):
    if count % 4 != 0:
        return None
    chips = count // 2
    width = sections_width // chips
    if sections_width % chips or width % LANES or section_width % width:
        return None
    return (chips, 2, chips // 2, width, width // LANES)


def local(hidden, latents, base_qkv, control_qkv, step_index, w_join, w_mod, w_out, count):
    plan = plan_for(count, w_join.shape[0], base_qkv.shape[2])
    if plan is None or hidden.shape[0] % 8 or (plan[0] * hidden.shape[0]) % 16:
        return gathered(
            hidden, latents, base_qkv, control_qkv, step_index, w_join, w_mod, w_out
        )
    return fused(
        plan, hidden, latents, base_qkv, control_qkv, step_index, w_join, w_mod, w_out
    )


def solution(mesh):
    in_specs = (
        P(("groups", "seq"), None),
        P(("groups", "seq"), None),
        P(None, ("groups", "seq"), None),
        P(None, ("groups", "seq"), None),
        P(),
        P(None, "seq"),
        P(),
        P(),
    )
    out_specs = (P(("groups", "seq"), None), P(("groups", "seq"), None), P(("groups", "seq"), None))
    return jax.shard_map(
        functools.partial(local, count=mesh.shape["seq"]),
        mesh=mesh,
        in_specs=in_specs,
        out_specs=out_specs,
        check_vma=False,
    )
```

```python
import functools
import math

import jax
import jax.numpy as jnp
from jax import lax
from jax.experimental import pallas as pl
from jax.experimental.pallas import tpu as pltpu
from jax.sharding import PartitionSpec as P

D = 3072
HD = 64
TEMB = 512
HEADS = 24
STEPS = 50


def time_terms(step_index):
    step_value = step_index[0].astype(jnp.float32)
    level_now = jnp.cos(0.5 * math.pi * step_value / STEPS)
    level_next = jnp.cos(0.5 * math.pi * (step_value + 1.0) / STEPS)
    half_width = TEMB // 2
    frequency = jnp.exp(
        -math.log(10000.0) * jnp.arange(half_width).astype(jnp.float32) / half_width
    )
    angles = 1000.0 * level_now * frequency
    embedding = jnp.concatenate([jnp.cos(angles), jnp.sin(angles)]).astype(jnp.bfloat16)
    return (embedding, level_next - level_now)


def attend(state, queries, shard_rows):
    running_max, running_sum, weighted = state
    count = shard_rows.shape[1]
    keys_block = shard_rows[0].reshape(count, HEADS, HD)
    values_block = shard_rows[1].reshape(count, HEADS, HD)
    scores = jnp.einsum(
        "qhd,khd->qhk", queries, keys_block, preferred_element_type=jnp.float32
    ) * HD ** (-0.5)
    newest_max = jnp.max(scores, axis=2)
    rescale = jnp.exp(running_max - newest_max)
    exponent = jnp.exp(scores - newest_max[:, :, None])
    running_sum = running_sum * rescale + jnp.sum(exponent, axis=2)
    weighted = weighted * rescale[:, :, None] + jnp.einsum(
        "qhk,khd->qhd",
        exponent.astype(jnp.bfloat16),
        values_block,
        preferred_element_type=jnp.float32,
    )
    return (newest_max, running_sum, weighted)


def finish(state):
    running_max, running_sum, weighted = state
    outputs = (weighted / running_sum[:, :, None]).astype(jnp.bfloat16)
    return outputs.reshape(outputs.shape[0], HEADS * HD)


def gathered(hidden, latents, base_qkv, control_qkv, step_index, w_join, w_mod, w_out):
    tokens_here = hidden.shape[0]
    base_queries = base_qkv[0].reshape(tokens_here, HEADS, HD)
    control_queries = control_qkv[0].reshape(tokens_here, HEADS, HD)
    base_pairs = base_qkv[1:]
    control_pairs = control_qkv[1:]
    initial = (
        jnp.full((tokens_here, HEADS), -jnp.inf, jnp.float32),
        jnp.zeros((tokens_here, HEADS), jnp.float32),
        jnp.zeros((tokens_here, HEADS, HD), jnp.float32),
    )
    base_state = attend(
        initial, base_queries, lax.all_gather(base_pairs, "seq", axis=1, tiled=True)
    )
    control_state = attend(
        initial, control_queries, lax.all_gather(control_pairs, "seq", axis=1, tiled=True)
    )
    joined = jnp.concatenate([finish(base_state), finish(control_state)], axis=1)
    column_part = jnp.dot(
        lax.all_gather(joined, "seq", axis=0, tiled=True),
        w_join,
        preferred_element_type=jnp.float32,
    )
    update = lax.all_to_all(
        column_part.astype(jnp.bfloat16), "seq", split_axis=0, concat_axis=1, tiled=True
    ).astype(column_part.dtype)
    summed = hidden.astype(jnp.float32) + update
    hidden_next = summed.astype(jnp.bfloat16)
    embedding, step_size = time_terms(step_index)
    modulation = jnp.dot(embedding[None, :], w_mod, preferred_element_type=jnp.float32)[0]
    shift_term = modulation[:D]
    gain_term = modulation[D:]
    average = jnp.mean(summed, axis=1, keepdims=True)
    centered = summed - average
    variance = jnp.mean(centered * centered, axis=1, keepdims=True)
    normed = (centered / jnp.sqrt(variance + 1e-05) * (1.0 + gain_term) + shift_term).astype(
        jnp.bfloat16
    )
    velocity = jnp.dot(normed, w_out, preferred_element_type=jnp.float32)
    latents_next = latents + step_size * velocity
    return (hidden_next, velocity, latents_next)


LANES = 128
MESH = pl.DeviceIdType.MESH


def fused_kernel(
    plan,
    base_in,
    control_in,
    step_in,
    join_in,
    mod_in,
    update_in,
    terms_ref,
    w_mod,
    w_join,
    modulation,
    heads_own,
    heads_other,
    joined,
    total,
    update_out,
    load_sem,
    own_sem,
    swap_send,
    swap_recv,
    pass_send,
    pass_recv,
    side_send,
    side_recv,
    right_send,
    left_send,
    cross_send,
    join_recv,
    back_send,
    back_recv,
):
    chips, rows, lines, width, pieces = plan
    tokens = base_in.shape[1]
    section = base_in.shape[2]
    per_section = section // width
    me = lax.axis_index("seq")
    core = lax.rem(me, 2)
    chip = me // 2
    row = lax.rem(chip, rows)
    place = chip // rows

    def device(other, other_core):
        return {"seq": other * 2 + other_core}

    def remote(src, dst, send, recv, target):
        return pltpu.make_async_remote_copy(
            src_ref=src,
            dst_ref=dst,
            send_sem=send,
            recv_sem=recv,
            device_id=target,
            device_id_type=MESH,
        )

    half_rows = join_in.shape[0]

    def join_half(which):
        return w_join.at[pl.ds(pl.multiple_of(which * half_rows, half_rows), half_rows), :]

    mod_load = pltpu.make_async_copy(mod_in, w_mod, load_sem.at[0])
    join_load = pltpu.make_async_copy(join_in, join_half(core), load_sem.at[1])
    barrier = pltpu.get_barrier_semaphore()
    for step in range(1, chips):
        pl.semaphore_signal(
            barrier,
            inc=1,
            device_id=device(lax.rem(chip + step, chips), core),
            device_id_type=MESH,
        )
    pl.semaphore_signal(barrier, inc=1, device_id=device(chip, 1 - core), device_id_type=MESH)
    mod_load.start()
    join_load.start()
    step_value = jnp.full((1, TEMB), step_in[0].astype(jnp.float32))
    level_now = jnp.cos(0.5 * math.pi * step_value / STEPS)
    level_next = jnp.cos(0.5 * math.pi * (step_value + 1.0) / STEPS)
    half_width = TEMB // 2
    index = lax.broadcasted_iota(jnp.int32, (1, TEMB), 1)
    place_in_half = jnp.where(index < half_width, index, index - half_width).astype(jnp.float32)
    frequency = jnp.exp(-math.log(10000.0) * place_in_half / half_width)
    angles = 1000.0 * level_now * frequency
    embedding = jnp.where(index < half_width, jnp.cos(angles), jnp.sin(angles))
    embedding = jnp.broadcast_to(embedding, (16, TEMB)).astype(jnp.bfloat16)
    step_size = level_next - level_now
    pl.semaphore_wait(barrier, chips)

    def piece_of(ref, target, piece):
        start = lax.rem(target, per_section) * width + piece * LANES
        return ref.at[:, :, pl.ds(pl.multiple_of(start, LANES), LANES)]

    def from_section(target, act):
        @pl.when(target < per_section)
        def _():
            act(base_in)

        @pl.when(target >= per_section)
        def _():
            act(control_in)

    far_first = sorted(range(1, chips), key=lambda step: abs(2 * step - chips))

    def swap(ref, target, step, piece):
        return remote(
            piece_of(ref, target, piece),
            heads_own.at[chip, piece],
            swap_send.at[step, piece],
            swap_recv.at[chip, piece],
            device(target, core),
        )

    def own_copy(ref, piece):
        return pltpu.make_async_copy(
            piece_of(ref, chip, piece), heads_own.at[chip, piece], own_sem.at[piece]
        )

    def pass_on(source, piece):
        return remote(
            heads_own.at[source, piece, 1:3],
            heads_other.at[source, piece],
            pass_send.at[source, piece],
            pass_recv.at[source, piece],
            device(chip, 1 - core),
        )

    side = remote(join_in, join_half(core), side_send, side_recv, device(chip, 1 - core))
    for piece in range(pieces):
        for step in far_first:
            target = lax.rem(chip + step, chips)
            from_section(
                target, lambda ref, t=target, s=step, p=piece: swap(ref, t, s, p).start()
            )
        from_section(chip, lambda ref, p=piece: own_copy(ref, p).start())
    side.start()

    mod_load.wait()
    for start in range(0, w_mod.shape[1], TEMB):
        modulation[0:1, start : start + TEMB] = jnp.dot(
            embedding, w_mod[:, start : start + TEMB], preferred_element_type=jnp.float32
        )[0:1]
        modulation[1:2, start : start + TEMB] = step_size
    terms_store = pltpu.make_async_copy(modulation, terms_ref, load_sem.at[2])
    terms_store.start()

    lane = lax.broadcasted_iota(jnp.int32, (chips * tokens, LANES), 1)

    def attention(piece):
        def rows_of(ref, kind):
            part = ref[:, piece, kind].astype(jnp.float32)
            return part.reshape(chips * tokens, LANES)

        queries = rows_of(heads_own, 0) * HD ** (-0.5)
        keys = jnp.concatenate([rows_of(heads_own, 1), rows_of(heads_other, 0)], axis=0)
        values = jnp.concatenate([rows_of(heads_own, 2), rows_of(heads_other, 1)], axis=0)
        keys = keys.astype(jnp.bfloat16)
        values = values.astype(jnp.bfloat16)
        result = None
        for head in range(LANES // HD):
            mine = (lane >= head * HD) & (lane < (head + 1) * HD)
            query = jnp.where(mine, queries, 0.0).astype(jnp.bfloat16)
            scores = lax.dot_general(
                query, keys, (((1,), (1,)), ((), ())), preferred_element_type=jnp.float32
            )
            exponent = jnp.exp(scores - jnp.max(scores, axis=1, keepdims=True))
            row_sum = jnp.sum(exponent, axis=1, keepdims=True)
            mixed = jnp.dot(
                exponent.astype(jnp.bfloat16), values, preferred_element_type=jnp.float32
            )
            mixed = mixed / row_sum
            result = mixed if result is None else jnp.where(mine, mixed, result)
        joined[chip, piece] = result.astype(jnp.bfloat16)

    def hop(block_chip, piece, send, target):
        view = joined.at[block_chip, piece]
        return remote(
            view,
            view,
            send.at[block_chip, piece],
            join_recv.at[block_chip, piece],
            device(target, core),
        )

    other_row = rows - 1 - row

    def along_line(origin, target, piece):
        near = (origin == target - 1) | (origin == target + 1)
        origin_end = (origin == 0) | (origin == lines - 1)
        target_end = (target == 0) | (target == lines - 1)
        chosen = jnp.logical_not(target_end) & origin_end
        if piece == 0:
            chosen = chosen | target_end
        return near & chosen

    def share_other_row(piece, act):
        block_chip = place * rows + other_row

        @pl.when((place < lines - 1) & along_line(place, place + 1, piece))
        def _():
            act(hop(block_chip, piece, right_send, chip + rows))

        @pl.when((place > 0) & along_line(place, place - 1, piece))
        def _():
            act(hop(block_chip, piece, left_send, chip - rows))

    def hand_on(origin, piece, act):
        block_chip = origin * rows + row

        @pl.when(jnp.logical_not(along_line(origin, place, piece)))
        def _():
            act(hop(block_chip, piece, cross_send, place * rows + other_row))

        @pl.when((origin <= place) & (place < lines - 1))
        def _():
            act(hop(block_chip, piece, right_send, chip + rows))

        @pl.when((origin >= place) & (place > 0))
        def _():
            act(hop(block_chip, piece, left_send, chip - rows))

    def at_distance(distance, act):
        @pl.when(place >= distance)
        def _():
            act(place - distance)

        @pl.when(place + distance < lines)
        def _():
            act(place + distance)

    def arrive(block_chip, piece):
        view = joined.at[block_chip, piece]
        remote(
            view,
            view,
            cross_send.at[block_chip, piece],
            join_recv.at[block_chip, piece],
            device(chip, 1 - core),
        ).wait_recv()

    def relay(distance, piece):
        if distance == 1:
            arrive(place * rows + other_row, piece)
            share_other_row(piece, lambda copy: copy.start())

        def act(origin):
            arrive(origin * rows + row, piece)
            hand_on(origin, piece, lambda copy: copy.start())

        at_distance(distance, act)

    for piece in range(pieces):
        from_section(chip, lambda ref, p=piece: own_copy(ref, p).wait())
        pass_on(chip, piece).start()
        for step in reversed(far_first):
            source = lax.rem(chip - step + chips, chips)
            remote(
                heads_own.at[source, piece],
                heads_own.at[source, piece],
                swap_send.at[step, piece],
                swap_recv.at[source, piece],
                device(source, core),
            ).wait_recv()
            pass_on(source, piece).start()
        for step in range(chips):
            pass_on(lax.rem(chip - step + chips, chips), piece).wait_recv()
        attention(piece)
        hand_on(place, piece, lambda copy: copy.start())
        for earlier in range(piece):
            distance = piece - earlier
            if distance < lines:
                relay(distance, earlier)

    join_load.wait()
    side.wait_recv()

    def project(block_chip):
        block_columns = pl.ds(pl.multiple_of(block_chip * width, LANES), width)
        total[...] += lax.dot_general(
            jnp.concatenate([joined[block_chip, p] for p in range(pieces)], axis=1),
            w_join[:, block_columns],
            (((1,), (1,)), ((), ())),
            preferred_element_type=jnp.float32,
        )

    total[...] = jnp.zeros_like(total)
    done = {p: pieces - 1 - p for p in range(pieces)}
    for distance in range(lines):
        for piece in range(pieces):
            if done[piece] < distance:
                relay(distance, piece)
        if distance == 0:
            project(chip)
        else:
            at_distance(distance, lambda origin: project(origin * rows + row))

    def cross(origin):
        block_chip = origin * rows + other_row
        for piece in range(pieces):
            arrive(block_chip, piece)
        project(block_chip)

    project(place * rows + other_row)
    for distance in range(1, lines):
        at_distance(distance, cross)

    update_out[...] = total[...].reshape(chips, tokens, width).astype(jnp.bfloat16)

    def back(target, step):
        return remote(
            update_out.at[target],
            update_in.at[chip],
            back_send.at[step],
            back_recv.at[chip],
            device(target, core),
        )

    for step in far_first:
        back(lax.rem(chip + step, chips), step).start()
    own_back = pltpu.make_async_copy(update_out.at[chip], update_in.at[chip], load_sem.at[3])
    own_back.start()
    for step in range(1, chips):
        source = lax.rem(chip - step + chips, chips)
        remote(
            update_out.at[source],
            update_in.at[source],
            back_send.at[step],
            back_recv.at[source],
            device(source, core),
        ).wait_recv()
    for piece in range(pieces):
        for step in range(1, chips):
            swap(base_in, lax.rem(chip + step, chips), step, piece).wait_send()
        for source in range(chips):
            pass_on(source, piece).wait_send()
        for distance in range(lines):
            if distance == 0:
                share_other_row(piece, lambda copy: copy.wait_send())
                hand_on(place, piece, lambda copy: copy.wait_send())
            else:
                at_distance(
                    distance, lambda o, p=piece: hand_on(o, p, lambda copy: copy.wait_send())
                )
    side.wait_send()
    terms_store.wait()
    own_back.wait()
    for step in range(1, chips):
        back(lax.rem(chip + step, chips), step).wait_send()


def finish_kernel(
    update_in,
    terms_in,
    hidden_in,
    latents_in,
    out_in,
    next_ref,
    velocity_ref,
    latents_ref,
    update,
    terms,
    hidden,
    latents,
    w_out,
    hidden_next,
    velocity_out,
    latents_next,
    load_sem,
    store_sem,
):
    loads = [
        pltpu.make_async_copy(source, target, load_sem.at[number])
        for number, (source, target) in enumerate(
            (
                (update_in, update),
                (hidden_in, hidden),
                (terms_in, terms),
                (out_in, w_out),
                (latents_in, latents),
            )
        )
    ]
    stores = [
        pltpu.make_async_copy(source, target, store_sem.at[number])
        for number, (source, target) in enumerate(
            (
                (hidden_next, next_ref),
                (velocity_out, velocity_ref),
                (latents_next, latents_ref),
            )
        )
    ]
    for load in loads:
        load.start()
    loads[0].wait()
    loads[1].wait()
    joined_columns = jnp.concatenate([update[p] for p in range(update.shape[0])], axis=1)
    summed = hidden[...].astype(jnp.float32) + joined_columns.astype(jnp.float32)
    hidden_next[...] = summed.astype(jnp.bfloat16)
    stores[0].start()
    average = jnp.mean(summed, axis=1, keepdims=True)
    centered = summed - average
    variance = jnp.mean(centered * centered, axis=1, keepdims=True)
    loads[2].wait()
    width = hidden.shape[1]
    shift_term = terms[0:1, :width]
    gain_term = terms[0:1, width:]
    normed = centered / jnp.sqrt(variance + 1e-05) * (1.0 + gain_term) + shift_term
    loads[3].wait()
    velocity = lax.dot_general(
        normed.astype(jnp.bfloat16),
        w_out[...],
        (((1,), (1,)), ((), ())),
        preferred_element_type=jnp.float32,
    )
    velocity_out[...] = velocity
    stores[1].start()
    loads[4].wait()
    latents_next[...] = latents[...] + terms[1:2, : latents.shape[1]] * velocity
    stores[2].start()
    for store in stores:
        store.wait()


def fused(plan, hidden, latents, base_qkv, control_qkv, step_index, w_join, w_mod, w_out):
    chips, rows, lines, width, pieces = plan
    tokens = hidden.shape[0]
    hbm_spec = pl.BlockSpec(memory_space=pltpu.HBM)
    dma = pltpu.SemaphoreType.DMA
    vmem_limit = 60 * 1024 * 1024
    per_piece = [dma((chips, pieces))] * 4
    update, terms = pl.pallas_call(
        functools.partial(fused_kernel, plan),
        out_shape=(
            jax.ShapeDtypeStruct((chips, tokens, width), jnp.bfloat16),
            jax.ShapeDtypeStruct((2, w_mod.shape[1]), jnp.float32),
        ),
        in_specs=[hbm_spec] * 2 + [pl.BlockSpec(memory_space=pltpu.SMEM)] + [hbm_spec] * 2,
        out_specs=(hbm_spec,) * 2,
        scratch_shapes=[
            pltpu.VMEM(w_mod.shape, jnp.bfloat16),
            pltpu.VMEM((2 * w_join.shape[1], w_join.shape[0]), jnp.bfloat16),
            pltpu.VMEM((2, w_mod.shape[1]), jnp.float32),
            pltpu.VMEM((chips, pieces, 3, tokens, LANES), jnp.bfloat16),
            pltpu.VMEM((chips, pieces, 2, tokens, LANES), jnp.bfloat16),
            pltpu.VMEM((chips, pieces, chips * tokens, LANES), jnp.bfloat16),
            pltpu.VMEM((chips * tokens, width), jnp.float32),
            pltpu.VMEM((chips, tokens, width), jnp.bfloat16),
            dma((4,)),
            dma((pieces,)),
            *per_piece,
            dma,
            dma,
            *per_piece,
            dma((chips,)),
            dma((chips,)),
        ],
        compiler_params=pltpu.CompilerParams(
            collective_id=0, has_side_effects=True, vmem_limit_bytes=vmem_limit
        ),
        name="fused",
    )(base_qkv, control_qkv, step_index, w_join.T, w_mod)
    return pl.pallas_call(
        finish_kernel,
        out_shape=(
            jax.ShapeDtypeStruct(hidden.shape, jnp.bfloat16),
            jax.ShapeDtypeStruct(latents.shape, jnp.float32),
            jax.ShapeDtypeStruct(latents.shape, jnp.float32),
        ),
        in_specs=[hbm_spec] * 5,
        out_specs=(hbm_spec,) * 3,
        scratch_shapes=[
            pltpu.VMEM(update.shape, jnp.bfloat16),
            pltpu.VMEM(terms.shape, jnp.float32),
            pltpu.VMEM(hidden.shape, jnp.bfloat16),
            pltpu.VMEM(latents.shape, jnp.float32),
            pltpu.VMEM(w_out.shape[::-1], jnp.bfloat16),
            pltpu.VMEM(hidden.shape, jnp.bfloat16),
            pltpu.VMEM(latents.shape, jnp.float32),
            pltpu.VMEM(latents.shape, jnp.float32),
            dma((5,)),
            dma((3,)),
        ],
        compiler_params=pltpu.CompilerParams(vmem_limit_bytes=vmem_limit),
        name="norm_and_step",
    )(update, terms, hidden, latents, w_out.T)


def plan_for(count, sections_width, section_width):
    if count % 4 != 0 or count < 8:
        return None
    chips = count // 2
    width = sections_width // chips
    if sections_width % chips or width % LANES or section_width % width:
        return None
    return (chips, 2, chips // 2, width, width // LANES)


def local(hidden, latents, base_qkv, control_qkv, step_index, w_join, w_mod, w_out, count):
    plan = plan_for(count, w_join.shape[0], base_qkv.shape[2])
    if plan is None or hidden.shape[0] % 8 or (plan[0] * hidden.shape[0]) % 16:
        return gathered(
            hidden, latents, base_qkv, control_qkv, step_index, w_join, w_mod, w_out
        )
    return fused(
        plan, hidden, latents, base_qkv, control_qkv, step_index, w_join, w_mod, w_out
    )


def solution(mesh):
    in_specs = (
        P(("groups", "seq"), None),
        P(("groups", "seq"), None),
        P(None, ("groups", "seq"), None),
        P(None, ("groups", "seq"), None),
        P(),
        P(None, "seq"),
        P(),
        P(),
    )
    out_specs = (P(("groups", "seq"), None), P(("groups", "seq"), None), P(("groups", "seq"), None))
    return jax.shard_map(
        functools.partial(local, count=mesh.shape["seq"]),
        mesh=mesh,
        in_specs=in_specs,
        out_specs=out_specs,
        check_vma=False,
    )
```

```python
import functools
import math

import jax
import jax.numpy as jnp
from jax import lax
from jax.experimental import pallas as pl
from jax.experimental.pallas import tpu as pltpu
from jax.sharding import PartitionSpec as P

D = 3072
HD = 64
TEMB = 512
HEADS = 24
STEPS = 50


def time_terms(step_index):
    step_value = step_index[0].astype(jnp.float32)
    level_now = jnp.cos(0.5 * math.pi * step_value / STEPS)
    level_next = jnp.cos(0.5 * math.pi * (step_value + 1.0) / STEPS)
    half_width = TEMB // 2
    frequency = jnp.exp(
        -math.log(10000.0) * jnp.arange(half_width).astype(jnp.float32) / half_width
    )
    angles = 1000.0 * level_now * frequency
    embedding = jnp.concatenate([jnp.cos(angles), jnp.sin(angles)]).astype(jnp.bfloat16)
    return (embedding, level_next - level_now)


def attend(state, queries, shard_rows):
    running_max, running_sum, weighted = state
    count = shard_rows.shape[1]
    keys_block = shard_rows[0].reshape(count, HEADS, HD)
    values_block = shard_rows[1].reshape(count, HEADS, HD)
    scores = jnp.einsum(
        "qhd,khd->qhk", queries, keys_block, preferred_element_type=jnp.float32
    ) * HD ** (-0.5)
    newest_max = jnp.max(scores, axis=2)
    rescale = jnp.exp(running_max - newest_max)
    exponent = jnp.exp(scores - newest_max[:, :, None])
    running_sum = running_sum * rescale + jnp.sum(exponent, axis=2)
    weighted = weighted * rescale[:, :, None] + jnp.einsum(
        "qhk,khd->qhd",
        exponent.astype(jnp.bfloat16),
        values_block,
        preferred_element_type=jnp.float32,
    )
    return (newest_max, running_sum, weighted)


def finish(state):
    running_max, running_sum, weighted = state
    outputs = (weighted / running_sum[:, :, None]).astype(jnp.bfloat16)
    return outputs.reshape(outputs.shape[0], HEADS * HD)


def gathered(hidden, latents, base_qkv, control_qkv, step_index, w_join, w_mod, w_out):
    tokens_here = hidden.shape[0]
    base_queries = base_qkv[0].reshape(tokens_here, HEADS, HD)
    control_queries = control_qkv[0].reshape(tokens_here, HEADS, HD)
    base_pairs = base_qkv[1:]
    control_pairs = control_qkv[1:]
    initial = (
        jnp.full((tokens_here, HEADS), -jnp.inf, jnp.float32),
        jnp.zeros((tokens_here, HEADS), jnp.float32),
        jnp.zeros((tokens_here, HEADS, HD), jnp.float32),
    )
    base_state = attend(
        initial, base_queries, lax.all_gather(base_pairs, "seq", axis=1, tiled=True)
    )
    control_state = attend(
        initial, control_queries, lax.all_gather(control_pairs, "seq", axis=1, tiled=True)
    )
    joined = jnp.concatenate([finish(base_state), finish(control_state)], axis=1)
    column_part = jnp.dot(
        lax.all_gather(joined, "seq", axis=0, tiled=True),
        w_join,
        preferred_element_type=jnp.float32,
    )
    update = lax.all_to_all(
        column_part.astype(jnp.bfloat16), "seq", split_axis=0, concat_axis=1, tiled=True
    ).astype(column_part.dtype)
    summed = hidden.astype(jnp.float32) + update
    hidden_next = summed.astype(jnp.bfloat16)
    embedding, step_size = time_terms(step_index)
    modulation = jnp.dot(embedding[None, :], w_mod, preferred_element_type=jnp.float32)[0]
    shift_term = modulation[:D]
    gain_term = modulation[D:]
    average = jnp.mean(summed, axis=1, keepdims=True)
    centered = summed - average
    variance = jnp.mean(centered * centered, axis=1, keepdims=True)
    normed = (centered / jnp.sqrt(variance + 1e-05) * (1.0 + gain_term) + shift_term).astype(
        jnp.bfloat16
    )
    velocity = jnp.dot(normed, w_out, preferred_element_type=jnp.float32)
    latents_next = latents + step_size * velocity
    return (hidden_next, velocity, latents_next)


LANES = 128
MESH = pl.DeviceIdType.MESH


def fused_kernel(
    plan,
    base_in,
    control_in,
    step_in,
    join_in,
    mod_in,
    update_in,
    terms_ref,
    w_mod,
    w_join,
    modulation,
    heads_own,
    heads_other,
    joined,
    total,
    update_out,
    load_sem,
    own_sem,
    swap_send,
    swap_recv,
    pass_send,
    pass_recv,
    side_send,
    side_recv,
    right_send,
    left_send,
    far_right_send,
    far_left_send,
    cross_send,
    join_recv,
    back_send,
    back_recv,
):
    chips, rows, lines, width, pieces = plan
    tokens = base_in.shape[1]
    section = base_in.shape[2]
    per_section = section // width
    me = lax.axis_index("seq")
    core = lax.rem(me, 2)
    chip = me // 2
    row = lax.rem(chip, rows)
    place = chip // rows

    def device(other, other_core):
        return {"seq": other * 2 + other_core}

    def remote(src, dst, send, recv, target):
        return pltpu.make_async_remote_copy(
            src_ref=src,
            dst_ref=dst,
            send_sem=send,
            recv_sem=recv,
            device_id=target,
            device_id_type=MESH,
        )

    half_rows = join_in.shape[0]

    def join_half(which):
        return w_join.at[pl.ds(pl.multiple_of(which * half_rows, half_rows), half_rows), :]

    mod_load = pltpu.make_async_copy(mod_in, w_mod, load_sem.at[0])
    join_load = pltpu.make_async_copy(join_in, join_half(core), load_sem.at[1])
    barrier = pltpu.get_barrier_semaphore()
    for step in range(1, chips):
        pl.semaphore_signal(
            barrier,
            inc=1,
            device_id=device(lax.rem(chip + step, chips), core),
            device_id_type=MESH,
        )
    pl.semaphore_signal(barrier, inc=1, device_id=device(chip, 1 - core), device_id_type=MESH)
    mod_load.start()
    join_load.start()
    step_value = jnp.full((1, TEMB), step_in[0].astype(jnp.float32))
    level_now = jnp.cos(0.5 * math.pi * step_value / STEPS)
    level_next = jnp.cos(0.5 * math.pi * (step_value + 1.0) / STEPS)
    half_width = TEMB // 2
    index = lax.broadcasted_iota(jnp.int32, (1, TEMB), 1)
    place_in_half = jnp.where(index < half_width, index, index - half_width).astype(jnp.float32)
    frequency = jnp.exp(-math.log(10000.0) * place_in_half / half_width)
    angles = 1000.0 * level_now * frequency
    embedding = jnp.where(index < half_width, jnp.cos(angles), jnp.sin(angles))
    embedding = jnp.broadcast_to(embedding, (16, TEMB)).astype(jnp.bfloat16)
    step_size = level_next - level_now
    pl.semaphore_wait(barrier, chips)

    def piece_of(ref, target, piece):
        start = lax.rem(target, per_section) * width + piece * LANES
        return ref.at[:, :, pl.ds(pl.multiple_of(start, LANES), LANES)]

    def from_section(target, act):
        @pl.when(target < per_section)
        def _():
            act(base_in)

        @pl.when(target >= per_section)
        def _():
            act(control_in)

    far_first = sorted(range(1, chips), key=lambda step: abs(2 * step - chips))

    def swap(ref, target, step, piece):
        return remote(
            piece_of(ref, target, piece),
            heads_own.at[chip, piece],
            swap_send.at[step, piece],
            swap_recv.at[chip, piece],
            device(target, core),
        )

    def own_copy(ref, piece):
        return pltpu.make_async_copy(
            piece_of(ref, chip, piece), heads_own.at[chip, piece], own_sem.at[piece]
        )

    def pass_on(source, piece):
        return remote(
            heads_own.at[source, piece, 1:3],
            heads_other.at[source, piece],
            pass_send.at[source, piece],
            pass_recv.at[source, piece],
            device(chip, 1 - core),
        )

    side = remote(join_in, join_half(core), side_send, side_recv, device(chip, 1 - core))
    for piece in range(pieces):
        for step in far_first:
            target = lax.rem(chip + step, chips)
            from_section(
                target, lambda ref, t=target, s=step, p=piece: swap(ref, t, s, p).start()
            )
        from_section(chip, lambda ref, p=piece: own_copy(ref, p).start())
    side.start()

    mod_load.wait()
    for start in range(0, w_mod.shape[1], TEMB):
        modulation[0:1, start : start + TEMB] = jnp.dot(
            embedding, w_mod[:, start : start + TEMB], preferred_element_type=jnp.float32
        )[0:1]
        modulation[1:2, start : start + TEMB] = step_size
    terms_store = pltpu.make_async_copy(modulation, terms_ref, load_sem.at[2])
    terms_store.start()

    lane = lax.broadcasted_iota(jnp.int32, (chips * tokens, LANES), 1)

    def attention(piece):
        def rows_of(ref, kind):
            part = ref[:, piece, kind].astype(jnp.float32)
            return part.reshape(chips * tokens, LANES)

        queries = rows_of(heads_own, 0) * HD ** (-0.5)
        keys = jnp.concatenate([rows_of(heads_own, 1), rows_of(heads_other, 0)], axis=0)
        values = jnp.concatenate([rows_of(heads_own, 2), rows_of(heads_other, 1)], axis=0)
        keys = keys.astype(jnp.bfloat16)
        values = values.astype(jnp.bfloat16)
        result = None
        for head in range(LANES // HD):
            mine = (lane >= head * HD) & (lane < (head + 1) * HD)
            query = jnp.where(mine, queries, 0.0).astype(jnp.bfloat16)
            scores = lax.dot_general(
                query, keys, (((1,), (1,)), ((), ())), preferred_element_type=jnp.float32
            )
            exponent = jnp.exp(scores - jnp.max(scores, axis=1, keepdims=True))
            row_sum = jnp.sum(exponent, axis=1, keepdims=True)
            mixed = jnp.dot(
                exponent.astype(jnp.bfloat16), values, preferred_element_type=jnp.float32
            )
            mixed = mixed / row_sum
            result = mixed if result is None else jnp.where(mine, mixed, result)
        joined[chip, piece] = result.astype(jnp.bfloat16)

    def hop(block_chip, piece, send, target):
        view = joined.at[block_chip, piece]
        return remote(
            view,
            view,
            send.at[block_chip, piece],
            join_recv.at[block_chip, piece],
            device(target, core),
        )

    def other_row_step(step):
        return lax.rem(row + step, rows)

    def to_other_rows(origin, piece, act):
        for step in range(1, rows):
            target = place * rows + other_row_step(step)
            act(hop(origin * rows + row, piece, cross_send, target))

    def hand_out(piece, act):
        to_other_rows(place, piece, act)

        @pl.when(place < lines - 2)
        def _():
            act(hop(chip, piece, far_right_send, chip + 2 * rows))

        @pl.when(place > 1)
        def _():
            act(hop(chip, piece, far_left_send, chip - 2 * rows))

        @pl.when(place < lines - 1)
        def _():
            act(hop(chip, piece, right_send, chip + rows))

        @pl.when(place > 0)
        def _():
            act(hop(chip, piece, left_send, chip - rows))

    def hand_on(origin, piece, act):
        block_chip = origin * rows + row

        @pl.when((origin <= place - 2) & (place < lines - 1))
        def _():
            act(hop(block_chip, piece, right_send, chip + rows))

        @pl.when((origin >= place + 2) & (place > 0))
        def _():
            act(hop(block_chip, piece, left_send, chip - rows))

        to_other_rows(origin, piece, act)

    def at_distance(distance, act):
        @pl.when(place >= distance)
        def _():
            act(place - distance)

        @pl.when(place + distance < lines)
        def _():
            act(place + distance)

    def arrive(block_chip, piece):
        view = joined.at[block_chip, piece]
        remote(
            view,
            view,
            cross_send.at[block_chip, piece],
            join_recv.at[block_chip, piece],
            device(chip, 1 - core),
        ).wait_recv()

    def relay(distance, piece):
        def act(origin):
            arrive(origin * rows + row, piece)
            hand_on(origin, piece, lambda copy: copy.start())

        at_distance(distance, act)

    for piece in range(pieces):
        from_section(chip, lambda ref, p=piece: own_copy(ref, p).wait())
        pass_on(chip, piece).start()
        for step in reversed(far_first):
            source = lax.rem(chip - step + chips, chips)
            remote(
                heads_own.at[source, piece],
                heads_own.at[source, piece],
                swap_send.at[step, piece],
                swap_recv.at[source, piece],
                device(source, core),
            ).wait_recv()
            pass_on(source, piece).start()
        for step in range(chips):
            pass_on(lax.rem(chip - step + chips, chips), piece).wait_recv()
        attention(piece)
        hand_out(piece, lambda copy: copy.start())

    join_load.wait()
    side.wait_recv()

    def project(block_chip):
        block_columns = pl.ds(pl.multiple_of(block_chip * width, LANES), width)
        total[...] += lax.dot_general(
            jnp.concatenate([joined[block_chip, p] for p in range(pieces)], axis=1),
            w_join[:, block_columns],
            (((1,), (1,)), ((), ())),
            preferred_element_type=jnp.float32,
        )

    total[...] = jnp.zeros_like(total)
    for distance in range(lines):
        if distance == 0:
            project(chip)
        else:
            for piece in range(pieces):
                relay(distance, piece)
            at_distance(distance, lambda origin: project(origin * rows + row))

    def cross(origin, step):
        block_chip = origin * rows + other_row_step(step)
        for piece in range(pieces):
            arrive(block_chip, piece)
        project(block_chip)

    for distance in range(lines):
        for step in range(1, rows):
            if distance == 0:
                cross(place, step)
            else:
                at_distance(distance, lambda origin, s=step: cross(origin, s))

    update_out[...] = total[...].reshape(chips, tokens, width).astype(jnp.bfloat16)

    def back(target, step):
        return remote(
            update_out.at[target],
            update_in.at[chip],
            back_send.at[step],
            back_recv.at[chip],
            device(target, core),
        )

    for step in far_first:
        back(lax.rem(chip + step, chips), step).start()
    own_back = pltpu.make_async_copy(update_out.at[chip], update_in.at[chip], load_sem.at[3])
    own_back.start()
    for step in range(1, chips):
        source = lax.rem(chip - step + chips, chips)
        remote(
            update_out.at[source],
            update_in.at[source],
            back_send.at[step],
            back_recv.at[source],
            device(source, core),
        ).wait_recv()
    for piece in range(pieces):
        for step in range(1, chips):
            swap(base_in, lax.rem(chip + step, chips), step, piece).wait_send()
        for source in range(chips):
            pass_on(source, piece).wait_send()
        for distance in range(lines):
            if distance == 0:
                hand_out(piece, lambda copy: copy.wait_send())
            else:
                at_distance(
                    distance, lambda o, p=piece: hand_on(o, p, lambda copy: copy.wait_send())
                )
    side.wait_send()
    terms_store.wait()
    own_back.wait()
    for step in range(1, chips):
        back(lax.rem(chip + step, chips), step).wait_send()


def finish_kernel(
    update_in,
    terms_in,
    hidden_in,
    latents_in,
    out_in,
    next_ref,
    velocity_ref,
    latents_ref,
    update,
    terms,
    hidden,
    latents,
    w_out,
    hidden_next,
    velocity_out,
    latents_next,
    load_sem,
    store_sem,
):
    loads = [
        pltpu.make_async_copy(source, target, load_sem.at[number])
        for number, (source, target) in enumerate(
            (
                (update_in, update),
                (hidden_in, hidden),
                (terms_in, terms),
                (out_in, w_out),
                (latents_in, latents),
            )
        )
    ]
    stores = [
        pltpu.make_async_copy(source, target, store_sem.at[number])
        for number, (source, target) in enumerate(
            (
                (hidden_next, next_ref),
                (velocity_out, velocity_ref),
                (latents_next, latents_ref),
            )
        )
    ]
    for load in loads:
        load.start()
    loads[0].wait()
    loads[1].wait()
    joined_columns = jnp.concatenate([update[p] for p in range(update.shape[0])], axis=1)
    summed = hidden[...].astype(jnp.float32) + joined_columns.astype(jnp.float32)
    hidden_next[...] = summed.astype(jnp.bfloat16)
    stores[0].start()
    average = jnp.mean(summed, axis=1, keepdims=True)
    centered = summed - average
    variance = jnp.mean(centered * centered, axis=1, keepdims=True)
    loads[2].wait()
    width = hidden.shape[1]
    shift_term = terms[0:1, :width]
    gain_term = terms[0:1, width:]
    normed = centered / jnp.sqrt(variance + 1e-05) * (1.0 + gain_term) + shift_term
    loads[3].wait()
    velocity = lax.dot_general(
        normed.astype(jnp.bfloat16),
        w_out[...],
        (((1,), (1,)), ((), ())),
        preferred_element_type=jnp.float32,
    )
    velocity_out[...] = velocity
    stores[1].start()
    loads[4].wait()
    latents_next[...] = latents[...] + terms[1:2, : latents.shape[1]] * velocity
    stores[2].start()
    for store in stores:
        store.wait()


def fused(plan, hidden, latents, base_qkv, control_qkv, step_index, w_join, w_mod, w_out):
    chips, rows, lines, width, pieces = plan
    tokens = hidden.shape[0]
    hbm_spec = pl.BlockSpec(memory_space=pltpu.HBM)
    dma = pltpu.SemaphoreType.DMA
    vmem_limit = 60 * 1024 * 1024
    per_piece = [dma((chips, pieces))] * 4
    update, terms = pl.pallas_call(
        functools.partial(fused_kernel, plan),
        out_shape=(
            jax.ShapeDtypeStruct((chips, tokens, width), jnp.bfloat16),
            jax.ShapeDtypeStruct((2, w_mod.shape[1]), jnp.float32),
        ),
        in_specs=[hbm_spec] * 2 + [pl.BlockSpec(memory_space=pltpu.SMEM)] + [hbm_spec] * 2,
        out_specs=(hbm_spec,) * 2,
        scratch_shapes=[
            pltpu.VMEM(w_mod.shape, jnp.bfloat16),
            pltpu.VMEM((2 * w_join.shape[1], w_join.shape[0]), jnp.bfloat16),
            pltpu.VMEM((2, w_mod.shape[1]), jnp.float32),
            pltpu.VMEM((chips, pieces, 3, tokens, LANES), jnp.bfloat16),
            pltpu.VMEM((chips, pieces, 2, tokens, LANES), jnp.bfloat16),
            pltpu.VMEM((chips, pieces, chips * tokens, LANES), jnp.bfloat16),
            pltpu.VMEM((chips * tokens, width), jnp.float32),
            pltpu.VMEM((chips, tokens, width), jnp.bfloat16),
            dma((4,)),
            dma((pieces,)),
            *per_piece,
            dma,
            dma,
            *per_piece,
            *per_piece[:2],
            dma((chips,)),
            dma((chips,)),
        ],
        compiler_params=pltpu.CompilerParams(
            collective_id=0, has_side_effects=True, vmem_limit_bytes=vmem_limit
        ),
        name="fused",
    )(base_qkv, control_qkv, step_index, w_join.T, w_mod)
    return pl.pallas_call(
        finish_kernel,
        out_shape=(
            jax.ShapeDtypeStruct(hidden.shape, jnp.bfloat16),
            jax.ShapeDtypeStruct(latents.shape, jnp.float32),
            jax.ShapeDtypeStruct(latents.shape, jnp.float32),
        ),
        in_specs=[hbm_spec] * 5,
        out_specs=(hbm_spec,) * 3,
        scratch_shapes=[
            pltpu.VMEM(update.shape, jnp.bfloat16),
            pltpu.VMEM(terms.shape, jnp.float32),
            pltpu.VMEM(hidden.shape, jnp.bfloat16),
            pltpu.VMEM(latents.shape, jnp.float32),
            pltpu.VMEM(w_out.shape[::-1], jnp.bfloat16),
            pltpu.VMEM(hidden.shape, jnp.bfloat16),
            pltpu.VMEM(latents.shape, jnp.float32),
            pltpu.VMEM(latents.shape, jnp.float32),
            dma((5,)),
            dma((3,)),
        ],
        compiler_params=pltpu.CompilerParams(vmem_limit_bytes=vmem_limit),
        name="norm_and_step",
    )(update, terms, hidden, latents, w_out.T)


def plan_for(count, sections_width, section_width):
    if count % 4 != 0:
        return None
    chips = count // 2
    width = sections_width // chips
    if sections_width % chips or width % LANES or section_width % width:
        return None
    return (chips, 2, chips // 2, width, width // LANES)


def local(hidden, latents, base_qkv, control_qkv, step_index, w_join, w_mod, w_out, count):
    plan = plan_for(count, w_join.shape[0], base_qkv.shape[2])
    if plan is None or hidden.shape[0] % 8 or (plan[0] * hidden.shape[0]) % 16:
        return gathered(
            hidden, latents, base_qkv, control_qkv, step_index, w_join, w_mod, w_out
        )
    return fused(
        plan, hidden, latents, base_qkv, control_qkv, step_index, w_join, w_mod, w_out
    )


def solution(mesh):
    in_specs = (
        P(("groups", "seq"), None),
        P(("groups", "seq"), None),
        P(None, ("groups", "seq"), None),
        P(None, ("groups", "seq"), None),
        P(),
        P(None, "seq"),
        P(),
        P(),
    )
    out_specs = (P(("groups", "seq"), None), P(("groups", "seq"), None), P(("groups", "seq"), None))
    return jax.shard_map(
        functools.partial(local, count=mesh.shape["seq"]),
        mesh=mesh,
        in_specs=in_specs,
        out_specs=out_specs,
        check_vma=False,
    )
```

```python
import functools
import math

import jax
import jax.numpy as jnp
from jax import lax
from jax.experimental import pallas as pl
from jax.experimental.pallas import tpu as pltpu
from jax.sharding import PartitionSpec as P

D = 3072
HD = 64
TEMB = 512
HEADS = 24
STEPS = 50


def time_terms(step_index):
    step_value = step_index[0].astype(jnp.float32)
    level_now = jnp.cos(0.5 * math.pi * step_value / STEPS)
    level_next = jnp.cos(0.5 * math.pi * (step_value + 1.0) / STEPS)
    half_width = TEMB // 2
    frequency = jnp.exp(
        -math.log(10000.0) * jnp.arange(half_width).astype(jnp.float32) / half_width
    )
    angles = 1000.0 * level_now * frequency
    embedding = jnp.concatenate([jnp.cos(angles), jnp.sin(angles)]).astype(jnp.bfloat16)
    return (embedding, level_next - level_now)


def attend(state, queries, shard_rows):
    running_max, running_sum, weighted = state
    count = shard_rows.shape[1]
    keys_block = shard_rows[0].reshape(count, HEADS, HD)
    values_block = shard_rows[1].reshape(count, HEADS, HD)
    scores = jnp.einsum(
        "qhd,khd->qhk", queries, keys_block, preferred_element_type=jnp.float32
    ) * HD ** (-0.5)
    newest_max = jnp.max(scores, axis=2)
    rescale = jnp.exp(running_max - newest_max)
    exponent = jnp.exp(scores - newest_max[:, :, None])
    running_sum = running_sum * rescale + jnp.sum(exponent, axis=2)
    weighted = weighted * rescale[:, :, None] + jnp.einsum(
        "qhk,khd->qhd",
        exponent.astype(jnp.bfloat16),
        values_block,
        preferred_element_type=jnp.float32,
    )
    return (newest_max, running_sum, weighted)


def finish(state):
    running_max, running_sum, weighted = state
    outputs = (weighted / running_sum[:, :, None]).astype(jnp.bfloat16)
    return outputs.reshape(outputs.shape[0], HEADS * HD)


def gathered(hidden, latents, base_qkv, control_qkv, step_index, w_join, w_mod, w_out):
    tokens_here = hidden.shape[0]
    base_queries = base_qkv[0].reshape(tokens_here, HEADS, HD)
    control_queries = control_qkv[0].reshape(tokens_here, HEADS, HD)
    base_pairs = base_qkv[1:]
    control_pairs = control_qkv[1:]
    initial = (
        jnp.full((tokens_here, HEADS), -jnp.inf, jnp.float32),
        jnp.zeros((tokens_here, HEADS), jnp.float32),
        jnp.zeros((tokens_here, HEADS, HD), jnp.float32),
    )
    base_state = attend(
        initial, base_queries, lax.all_gather(base_pairs, "seq", axis=1, tiled=True)
    )
    control_state = attend(
        initial, control_queries, lax.all_gather(control_pairs, "seq", axis=1, tiled=True)
    )
    joined = jnp.concatenate([finish(base_state), finish(control_state)], axis=1)
    column_part = jnp.dot(
        lax.all_gather(joined, "seq", axis=0, tiled=True),
        w_join,
        preferred_element_type=jnp.float32,
    )
    update = lax.all_to_all(
        column_part.astype(jnp.bfloat16), "seq", split_axis=0, concat_axis=1, tiled=True
    ).astype(column_part.dtype)
    summed = hidden.astype(jnp.float32) + update
    hidden_next = summed.astype(jnp.bfloat16)
    embedding, step_size = time_terms(step_index)
    modulation = jnp.dot(embedding[None, :], w_mod, preferred_element_type=jnp.float32)[0]
    shift_term = modulation[:D]
    gain_term = modulation[D:]
    average = jnp.mean(summed, axis=1, keepdims=True)
    centered = summed - average
    variance = jnp.mean(centered * centered, axis=1, keepdims=True)
    normed = (centered / jnp.sqrt(variance + 1e-05) * (1.0 + gain_term) + shift_term).astype(
        jnp.bfloat16
    )
    velocity = jnp.dot(normed, w_out, preferred_element_type=jnp.float32)
    latents_next = latents + step_size * velocity
    return (hidden_next, velocity, latents_next)


LANES = 128
MESH = pl.DeviceIdType.MESH


def fused_kernel(
    plan,
    base_in,
    control_in,
    step_in,
    join_in,
    mod_in,
    update_in,
    terms_ref,
    w_mod,
    w_join,
    modulation,
    heads_own,
    heads_other,
    joined,
    total,
    update_out,
    load_sem,
    own_sem,
    swap_send,
    swap_recv,
    pass_send,
    pass_recv,
    side_send,
    side_recv,
    right_send,
    left_send,
    cross_send,
    join_recv,
    back_send,
    back_recv,
):
    chips, rows, lines, width, pieces = plan
    tokens = base_in.shape[1]
    section = base_in.shape[2]
    per_section = section // width
    me = lax.axis_index("seq")
    core = lax.rem(me, 2)
    chip = me // 2
    row = lax.rem(chip, rows)
    place = chip // rows

    def device(other, other_core):
        return {"seq": other * 2 + other_core}

    def remote(src, dst, send, recv, target):
        return pltpu.make_async_remote_copy(
            src_ref=src,
            dst_ref=dst,
            send_sem=send,
            recv_sem=recv,
            device_id=target,
            device_id_type=MESH,
        )

    half_rows = join_in.shape[0]

    def join_half(which):
        return w_join.at[pl.ds(pl.multiple_of(which * half_rows, half_rows), half_rows), :]

    mod_load = pltpu.make_async_copy(mod_in, w_mod, load_sem.at[0])
    join_load = pltpu.make_async_copy(join_in, join_half(core), load_sem.at[1])
    barrier = pltpu.get_barrier_semaphore()
    for step in range(1, chips):
        pl.semaphore_signal(
            barrier,
            inc=1,
            device_id=device(lax.rem(chip + step, chips), core),
            device_id_type=MESH,
        )
    pl.semaphore_signal(barrier, inc=1, device_id=device(chip, 1 - core), device_id_type=MESH)
    mod_load.start()
    join_load.start()
    step_value = jnp.full((1, TEMB), step_in[0].astype(jnp.float32))
    level_now = jnp.cos(0.5 * math.pi * step_value / STEPS)
    level_next = jnp.cos(0.5 * math.pi * (step_value + 1.0) / STEPS)
    half_width = TEMB // 2
    index = lax.broadcasted_iota(jnp.int32, (1, TEMB), 1)
    place_in_half = jnp.where(index < half_width, index, index - half_width).astype(jnp.float32)
    frequency = jnp.exp(-math.log(10000.0) * place_in_half / half_width)
    angles = 1000.0 * level_now * frequency
    embedding = jnp.where(index < half_width, jnp.cos(angles), jnp.sin(angles))
    embedding = jnp.broadcast_to(embedding, (16, TEMB)).astype(jnp.bfloat16)
    step_size = level_next - level_now
    pl.semaphore_wait(barrier, chips)

    def part_of(ref, target):
        start = lax.rem(target, per_section) * width
        return ref.at[:, :, pl.ds(pl.multiple_of(start, LANES), width)]

    def from_section(target, act):
        @pl.when(target < per_section)
        def _():
            act(base_in)

        @pl.when(target >= per_section)
        def _():
            act(control_in)

    far_first = sorted(range(1, chips), key=lambda step: abs(2 * step - chips))

    def swap(ref, target, step):
        return remote(
            part_of(ref, target),
            heads_own.at[chip],
            swap_send.at[step],
            swap_recv.at[chip],
            device(target, core),
        )

    def own_copy(ref):
        return pltpu.make_async_copy(part_of(ref, chip), heads_own.at[chip], own_sem)

    def pass_on(source):
        return remote(
            heads_own.at[source, 1:3],
            heads_other.at[source],
            pass_send.at[source],
            pass_recv.at[source],
            device(chip, 1 - core),
        )

    side = remote(join_in, join_half(core), side_send, side_recv, device(chip, 1 - core))
    for step in far_first:
        target = lax.rem(chip + step, chips)
        from_section(target, lambda ref, t=target, s=step: swap(ref, t, s).start())
    from_section(chip, lambda ref: own_copy(ref).start())
    side.start()

    mod_load.wait()
    for start in range(0, w_mod.shape[1], TEMB):
        modulation[0:1, start : start + TEMB] = jnp.dot(
            embedding, w_mod[:, start : start + TEMB], preferred_element_type=jnp.float32
        )[0:1]
        modulation[1:2, start : start + TEMB] = step_size
    terms_store = pltpu.make_async_copy(modulation, terms_ref, load_sem.at[2])
    terms_store.start()

    lane = lax.broadcasted_iota(jnp.int32, (chips * tokens, LANES), 1)

    def attention(piece):
        def rows_of(ref, kind):
            part = ref[:, kind, :, piece * LANES : (piece + 1) * LANES].astype(jnp.float32)
            return part.reshape(chips * tokens, LANES)

        queries = rows_of(heads_own, 0) * HD ** (-0.5)
        keys = jnp.concatenate([rows_of(heads_own, 1), rows_of(heads_other, 0)], axis=0)
        values = jnp.concatenate([rows_of(heads_own, 2), rows_of(heads_other, 1)], axis=0)
        keys = keys.astype(jnp.bfloat16)
        values = values.astype(jnp.bfloat16)
        result = None
        for head in range(LANES // HD):
            mine = (lane >= head * HD) & (lane < (head + 1) * HD)
            query = jnp.where(mine, queries, 0.0).astype(jnp.bfloat16)
            scores = lax.dot_general(
                query, keys, (((1,), (1,)), ((), ())), preferred_element_type=jnp.float32
            )
            exponent = jnp.exp(scores - jnp.max(scores, axis=1, keepdims=True))
            row_sum = jnp.sum(exponent, axis=1, keepdims=True)
            mixed = jnp.dot(
                exponent.astype(jnp.bfloat16), values, preferred_element_type=jnp.float32
            )
            mixed = mixed / row_sum
            result = mixed if result is None else jnp.where(mine, mixed, result)
        joined[chip, piece] = result.astype(jnp.bfloat16)

    def hop(block_chip, piece, send, target):
        view = joined.at[block_chip, piece]
        return remote(
            view,
            view,
            send.at[block_chip, piece],
            join_recv.at[block_chip, piece],
            device(target, core),
        )

    def other_row_step(step):
        return lax.rem(row + step, rows)

    def hand_on(origin, piece, act):
        block_chip = origin * rows + row
        for step in range(1, rows):
            act(hop(block_chip, piece, cross_send, place * rows + other_row_step(step)))

        @pl.when((origin <= place) & (place < lines - 1))
        def _():
            act(hop(block_chip, piece, right_send, chip + rows))

        @pl.when((origin >= place) & (place > 0))
        def _():
            act(hop(block_chip, piece, left_send, chip - rows))

    def at_distance(distance, act):
        @pl.when(place >= distance)
        def _():
            act(place - distance)

        @pl.when(place + distance < lines)
        def _():
            act(place + distance)

    def arrive(block_chip, piece):
        view = joined.at[block_chip, piece]
        remote(
            view,
            view,
            cross_send.at[block_chip, piece],
            join_recv.at[block_chip, piece],
            device(chip, 1 - core),
        ).wait_recv()

    def relay(distance, piece):
        def act(origin):
            arrive(origin * rows + row, piece)
            hand_on(origin, piece, lambda copy: copy.start())

        at_distance(distance, act)

    from_section(chip, lambda ref: own_copy(ref).wait())
    pass_on(chip).start()
    for step in reversed(far_first):
        source = lax.rem(chip - step + chips, chips)
        remote(
            heads_own.at[source],
            heads_own.at[source],
            swap_send.at[step],
            swap_recv.at[source],
            device(source, core),
        ).wait_recv()
        pass_on(source).start()
    for step in range(chips):
        pass_on(lax.rem(chip - step + chips, chips)).wait_recv()
    for piece in range(pieces):
        attention(piece)
        hand_on(place, piece, lambda copy: copy.start())
        for earlier in range(piece):
            distance = piece - earlier
            if distance < lines:
                relay(distance, earlier)

    join_load.wait()
    side.wait_recv()

    def project(block_chip):
        block_columns = pl.ds(pl.multiple_of(block_chip * width, LANES), width)
        total[...] += lax.dot_general(
            jnp.concatenate([joined[block_chip, p] for p in range(pieces)], axis=1),
            w_join[:, block_columns],
            (((1,), (1,)), ((), ())),
            preferred_element_type=jnp.float32,
        )

    total[...] = jnp.zeros_like(total)
    done = {p: pieces - 1 - p for p in range(pieces)}
    for distance in range(lines):
        for piece in range(pieces):
            if done[piece] < distance:
                relay(distance, piece)
        if distance == 0:
            project(chip)
        else:
            at_distance(distance, lambda origin: project(origin * rows + row))

    def cross(origin, step):
        block_chip = origin * rows + other_row_step(step)
        for piece in range(pieces):
            arrive(block_chip, piece)
        project(block_chip)

    for distance in range(lines):
        for step in range(1, rows):
            if distance == 0:
                cross(place, step)
            else:
                at_distance(distance, lambda origin, s=step: cross(origin, s))

    update_out[...] = total[...].reshape(chips, tokens, width).astype(jnp.bfloat16)

    def back(target, step):
        return remote(
            update_out.at[target],
            update_in.at[chip],
            back_send.at[step],
            back_recv.at[chip],
            device(target, core),
        )

    for step in far_first:
        back(lax.rem(chip + step, chips), step).start()
    own_back = pltpu.make_async_copy(update_out.at[chip], update_in.at[chip], load_sem.at[3])
    own_back.start()
    for step in range(1, chips):
        source = lax.rem(chip - step + chips, chips)
        remote(
            update_out.at[source],
            update_in.at[source],
            back_send.at[step],
            back_recv.at[source],
            device(source, core),
        ).wait_recv()
    for step in range(1, chips):
        swap(base_in, lax.rem(chip + step, chips), step).wait_send()
    for source in range(chips):
        pass_on(source).wait_send()
    for piece in range(pieces):
        for distance in range(lines):
            if distance == 0:
                hand_on(place, piece, lambda copy: copy.wait_send())
            else:
                at_distance(
                    distance, lambda o, p=piece: hand_on(o, p, lambda copy: copy.wait_send())
                )
    side.wait_send()
    terms_store.wait()
    own_back.wait()
    for step in range(1, chips):
        back(lax.rem(chip + step, chips), step).wait_send()


def finish_kernel(
    update_in,
    terms_in,
    hidden_in,
    latents_in,
    out_in,
    next_ref,
    velocity_ref,
    latents_ref,
    update,
    terms,
    hidden,
    latents,
    w_out,
    hidden_next,
    velocity_out,
    latents_next,
    load_sem,
    store_sem,
):
    loads = [
        pltpu.make_async_copy(source, target, load_sem.at[number])
        for number, (source, target) in enumerate(
            (
                (update_in, update),
                (hidden_in, hidden),
                (terms_in, terms),
                (out_in, w_out),
                (latents_in, latents),
            )
        )
    ]
    stores = [
        pltpu.make_async_copy(source, target, store_sem.at[number])
        for number, (source, target) in enumerate(
            (
                (hidden_next, next_ref),
                (velocity_out, velocity_ref),
                (latents_next, latents_ref),
            )
        )
    ]
    for load in loads:
        load.start()
    loads[0].wait()
    loads[1].wait()
    joined_columns = jnp.concatenate([update[p] for p in range(update.shape[0])], axis=1)
    summed = hidden[...].astype(jnp.float32) + joined_columns.astype(jnp.float32)
    hidden_next[...] = summed.astype(jnp.bfloat16)
    stores[0].start()
    average = jnp.mean(summed, axis=1, keepdims=True)
    centered = summed - average
    variance = jnp.mean(centered * centered, axis=1, keepdims=True)
    loads[2].wait()
    width = hidden.shape[1]
    shift_term = terms[0:1, :width]
    gain_term = terms[0:1, width:]
    normed = centered / jnp.sqrt(variance + 1e-05) * (1.0 + gain_term) + shift_term
    loads[3].wait()
    velocity = lax.dot_general(
        normed.astype(jnp.bfloat16),
        w_out[...],
        (((1,), (1,)), ((), ())),
        preferred_element_type=jnp.float32,
    )
    velocity_out[...] = velocity
    stores[1].start()
    loads[4].wait()
    latents_next[...] = latents[...] + terms[1:2, : latents.shape[1]] * velocity
    stores[2].start()
    for store in stores:
        store.wait()


def fused(plan, hidden, latents, base_qkv, control_qkv, step_index, w_join, w_mod, w_out):
    chips, rows, lines, width, pieces = plan
    tokens = hidden.shape[0]
    hbm_spec = pl.BlockSpec(memory_space=pltpu.HBM)
    dma = pltpu.SemaphoreType.DMA
    vmem_limit = 60 * 1024 * 1024
    per_piece = [dma((chips, pieces))] * 4
    update, terms = pl.pallas_call(
        functools.partial(fused_kernel, plan),
        out_shape=(
            jax.ShapeDtypeStruct((chips, tokens, width), jnp.bfloat16),
            jax.ShapeDtypeStruct((2, w_mod.shape[1]), jnp.float32),
        ),
        in_specs=[hbm_spec] * 2 + [pl.BlockSpec(memory_space=pltpu.SMEM)] + [hbm_spec] * 2,
        out_specs=(hbm_spec,) * 2,
        scratch_shapes=[
            pltpu.VMEM(w_mod.shape, jnp.bfloat16),
            pltpu.VMEM((2 * w_join.shape[1], w_join.shape[0]), jnp.bfloat16),
            pltpu.VMEM((2, w_mod.shape[1]), jnp.float32),
            pltpu.VMEM((chips, 3, tokens, width), jnp.bfloat16),
            pltpu.VMEM((chips, 2, tokens, width), jnp.bfloat16),
            pltpu.VMEM((chips, pieces, chips * tokens, LANES), jnp.bfloat16),
            pltpu.VMEM((chips * tokens, width), jnp.float32),
            pltpu.VMEM((chips, tokens, width), jnp.bfloat16),
            dma((4,)),
            dma,
            *[dma((chips,))] * 4,
            dma,
            dma,
            *per_piece,
            dma((chips,)),
            dma((chips,)),
        ],
        compiler_params=pltpu.CompilerParams(
            collective_id=0, has_side_effects=True, vmem_limit_bytes=vmem_limit
        ),
        name="fused",
    )(base_qkv, control_qkv, step_index, w_join.T, w_mod)
    return pl.pallas_call(
        finish_kernel,
        out_shape=(
            jax.ShapeDtypeStruct(hidden.shape, jnp.bfloat16),
            jax.ShapeDtypeStruct(latents.shape, jnp.float32),
            jax.ShapeDtypeStruct(latents.shape, jnp.float32),
        ),
        in_specs=[hbm_spec] * 5,
        out_specs=(hbm_spec,) * 3,
        scratch_shapes=[
            pltpu.VMEM(update.shape, jnp.bfloat16),
            pltpu.VMEM(terms.shape, jnp.float32),
            pltpu.VMEM(hidden.shape, jnp.bfloat16),
            pltpu.VMEM(latents.shape, jnp.float32),
            pltpu.VMEM(w_out.shape[::-1], jnp.bfloat16),
            pltpu.VMEM(hidden.shape, jnp.bfloat16),
            pltpu.VMEM(latents.shape, jnp.float32),
            pltpu.VMEM(latents.shape, jnp.float32),
            dma((5,)),
            dma((3,)),
        ],
        compiler_params=pltpu.CompilerParams(vmem_limit_bytes=vmem_limit),
        name="norm_and_step",
    )(update, terms, hidden, latents, w_out.T)


def plan_for(count, sections_width, section_width):
    if count % 4 != 0:
        return None
    chips = count // 2
    width = sections_width // chips
    if sections_width % chips or width % LANES or section_width % width:
        return None
    return (chips, 2, chips // 2, width, width // LANES)


def local(hidden, latents, base_qkv, control_qkv, step_index, w_join, w_mod, w_out, count):
    plan = plan_for(count, w_join.shape[0], base_qkv.shape[2])
    if plan is None or hidden.shape[0] % 8 or (plan[0] * hidden.shape[0]) % 16:
        return gathered(
            hidden, latents, base_qkv, control_qkv, step_index, w_join, w_mod, w_out
        )
    return fused(
        plan, hidden, latents, base_qkv, control_qkv, step_index, w_join, w_mod, w_out
    )


def solution(mesh):
    in_specs = (
        P(("groups", "seq"), None),
        P(("groups", "seq"), None),
        P(None, ("groups", "seq"), None),
        P(None, ("groups", "seq"), None),
        P(),
        P(None, "seq"),
        P(),
        P(),
    )
    out_specs = (P(("groups", "seq"), None), P(("groups", "seq"), None), P(("groups", "seq"), None))
    return jax.shard_map(
        functools.partial(local, count=mesh.shape["seq"]),
        mesh=mesh,
        in_specs=in_specs,
        out_specs=out_specs,
        check_vma=False,
    )
```

```python
import functools
import math

import jax
import jax.numpy as jnp
from jax import lax
from jax.experimental import pallas as pl
from jax.experimental.pallas import tpu as pltpu
from jax.sharding import PartitionSpec as P

D = 3072
HD = 64
TEMB = 512
HEADS = 24
STEPS = 50


def time_terms(step_index):
    step_value = step_index[0].astype(jnp.float32)
    level_now = jnp.cos(0.5 * math.pi * step_value / STEPS)
    level_next = jnp.cos(0.5 * math.pi * (step_value + 1.0) / STEPS)
    half_width = TEMB // 2
    frequency = jnp.exp(
        -math.log(10000.0) * jnp.arange(half_width).astype(jnp.float32) / half_width
    )
    angles = 1000.0 * level_now * frequency
    embedding = jnp.concatenate([jnp.cos(angles), jnp.sin(angles)]).astype(jnp.bfloat16)
    return (embedding, level_next - level_now)


def attend(state, queries, shard_rows):
    running_max, running_sum, weighted = state
    count = shard_rows.shape[1]
    keys_block = shard_rows[0].reshape(count, HEADS, HD)
    values_block = shard_rows[1].reshape(count, HEADS, HD)
    scores = jnp.einsum(
        "qhd,khd->qhk", queries, keys_block, preferred_element_type=jnp.float32
    ) * HD ** (-0.5)
    newest_max = jnp.max(scores, axis=2)
    rescale = jnp.exp(running_max - newest_max)
    exponent = jnp.exp(scores - newest_max[:, :, None])
    running_sum = running_sum * rescale + jnp.sum(exponent, axis=2)
    weighted = weighted * rescale[:, :, None] + jnp.einsum(
        "qhk,khd->qhd",
        exponent.astype(jnp.bfloat16),
        values_block,
        preferred_element_type=jnp.float32,
    )
    return (newest_max, running_sum, weighted)


def finish(state):
    running_max, running_sum, weighted = state
    outputs = (weighted / running_sum[:, :, None]).astype(jnp.bfloat16)
    return outputs.reshape(outputs.shape[0], HEADS * HD)


def gathered(hidden, latents, base_qkv, control_qkv, step_index, w_join, w_mod, w_out):
    tokens_here = hidden.shape[0]
    base_queries = base_qkv[0].reshape(tokens_here, HEADS, HD)
    control_queries = control_qkv[0].reshape(tokens_here, HEADS, HD)
    base_pairs = base_qkv[1:]
    control_pairs = control_qkv[1:]
    initial = (
        jnp.full((tokens_here, HEADS), -jnp.inf, jnp.float32),
        jnp.zeros((tokens_here, HEADS), jnp.float32),
        jnp.zeros((tokens_here, HEADS, HD), jnp.float32),
    )
    base_state = attend(
        initial, base_queries, lax.all_gather(base_pairs, "seq", axis=1, tiled=True)
    )
    control_state = attend(
        initial, control_queries, lax.all_gather(control_pairs, "seq", axis=1, tiled=True)
    )
    joined = jnp.concatenate([finish(base_state), finish(control_state)], axis=1)
    column_part = jnp.dot(
        lax.all_gather(joined, "seq", axis=0, tiled=True),
        w_join,
        preferred_element_type=jnp.float32,
    )
    update = lax.all_to_all(
        column_part.astype(jnp.bfloat16), "seq", split_axis=0, concat_axis=1, tiled=True
    ).astype(column_part.dtype)
    summed = hidden.astype(jnp.float32) + update
    hidden_next = summed.astype(jnp.bfloat16)
    embedding, step_size = time_terms(step_index)
    modulation = jnp.dot(embedding[None, :], w_mod, preferred_element_type=jnp.float32)[0]
    shift_term = modulation[:D]
    gain_term = modulation[D:]
    average = jnp.mean(summed, axis=1, keepdims=True)
    centered = summed - average
    variance = jnp.mean(centered * centered, axis=1, keepdims=True)
    normed = (centered / jnp.sqrt(variance + 1e-05) * (1.0 + gain_term) + shift_term).astype(
        jnp.bfloat16
    )
    velocity = jnp.dot(normed, w_out, preferred_element_type=jnp.float32)
    latents_next = latents + step_size * velocity
    return (hidden_next, velocity, latents_next)


LANES = 128
MESH = pl.DeviceIdType.MESH


def fused_kernel(
    plan,
    base_in,
    control_in,
    step_in,
    join_in,
    mod_in,
    update_in,
    terms_ref,
    w_mod,
    w_join,
    modulation,
    heads_own,
    heads_other,
    joined,
    total,
    update_out,
    load_sem,
    own_sem,
    swap_send,
    swap_recv,
    pass_send,
    pass_recv,
    side_send,
    side_recv,
    right_send,
    left_send,
    cross_send,
    join_recv,
    back_send,
    back_recv,
):
    chips, rows, lines, width, pieces = plan
    tokens = base_in.shape[1]
    section = base_in.shape[2]
    per_section = section // width
    me = lax.axis_index("seq")
    core = lax.rem(me, 2)
    chip = me // 2
    row = lax.rem(chip, rows)
    place = chip // rows

    def device(other, other_core):
        return {"seq": other * 2 + other_core}

    def remote(src, dst, send, recv, target):
        return pltpu.make_async_remote_copy(
            src_ref=src,
            dst_ref=dst,
            send_sem=send,
            recv_sem=recv,
            device_id=target,
            device_id_type=MESH,
        )

    half_rows = join_in.shape[0]

    def join_half(which):
        return w_join.at[pl.ds(pl.multiple_of(which * half_rows, half_rows), half_rows), :]

    mod_load = pltpu.make_async_copy(mod_in, w_mod, load_sem.at[0])
    join_load = pltpu.make_async_copy(join_in, join_half(core), load_sem.at[1])
    barrier = pltpu.get_barrier_semaphore()
    for step in range(1, chips):
        pl.semaphore_signal(
            barrier,
            inc=1,
            device_id=device(lax.rem(chip + step, chips), core),
            device_id_type=MESH,
        )
    pl.semaphore_signal(barrier, inc=1, device_id=device(chip, 1 - core), device_id_type=MESH)
    mod_load.start()
    join_load.start()
    step_value = jnp.full((1, TEMB), step_in[0].astype(jnp.float32))
    level_now = jnp.cos(0.5 * math.pi * step_value / STEPS)
    level_next = jnp.cos(0.5 * math.pi * (step_value + 1.0) / STEPS)
    half_width = TEMB // 2
    index = lax.broadcasted_iota(jnp.int32, (1, TEMB), 1)
    place_in_half = jnp.where(index < half_width, index, index - half_width).astype(jnp.float32)
    frequency = jnp.exp(-math.log(10000.0) * place_in_half / half_width)
    angles = 1000.0 * level_now * frequency
    embedding = jnp.where(index < half_width, jnp.cos(angles), jnp.sin(angles))
    embedding = jnp.broadcast_to(embedding, (16, TEMB)).astype(jnp.bfloat16)
    step_size = level_next - level_now
    pl.semaphore_wait(barrier, chips)

    def piece_of(ref, target, piece):
        start = lax.rem(target, per_section) * width + piece * LANES
        return ref.at[:, :, pl.ds(pl.multiple_of(start, LANES), LANES)]

    def from_section(target, act):
        @pl.when(target < per_section)
        def _():
            act(base_in)

        @pl.when(target >= per_section)
        def _():
            act(control_in)

    far_first = sorted(range(1, chips), key=lambda step: abs(2 * step - chips))

    def swap(ref, target, step, piece):
        return remote(
            piece_of(ref, target, piece),
            heads_own.at[chip, piece],
            swap_send.at[step, piece],
            swap_recv.at[chip, piece],
            device(target, core),
        )

    def own_copy(ref, piece):
        return pltpu.make_async_copy(
            piece_of(ref, chip, piece), heads_own.at[chip, piece], own_sem.at[piece]
        )

    def pass_on(source, piece):
        return remote(
            heads_own.at[source, piece, 1:3],
            heads_other.at[source, piece],
            pass_send.at[source, piece],
            pass_recv.at[source, piece],
            device(chip, 1 - core),
        )

    side = remote(join_in, join_half(core), side_send, side_recv, device(chip, 1 - core))
    for piece in range(pieces):
        for step in far_first:
            target = lax.rem(chip + step, chips)
            from_section(
                target, lambda ref, t=target, s=step, p=piece: swap(ref, t, s, p).start()
            )
        from_section(chip, lambda ref, p=piece: own_copy(ref, p).start())
    side.start()

    mod_load.wait()
    for start in range(0, w_mod.shape[1], TEMB):
        modulation[0:1, start : start + TEMB] = jnp.dot(
            embedding, w_mod[:, start : start + TEMB], preferred_element_type=jnp.float32
        )[0:1]
        modulation[1:2, start : start + TEMB] = step_size
    terms_store = pltpu.make_async_copy(modulation, terms_ref, load_sem.at[2])
    terms_store.start()

    lane = lax.broadcasted_iota(jnp.int32, (chips * tokens, LANES), 1)

    def attention(piece):
        def rows_of(ref, kind):
            part = ref[:, piece, kind].astype(jnp.float32)
            return part.reshape(chips * tokens, LANES)

        queries = rows_of(heads_own, 0) * HD ** (-0.5)
        keys = jnp.concatenate([rows_of(heads_own, 1), rows_of(heads_other, 0)], axis=0)
        values = jnp.concatenate([rows_of(heads_own, 2), rows_of(heads_other, 1)], axis=0)
        keys = keys.astype(jnp.bfloat16)
        values = values.astype(jnp.bfloat16)
        result = None
        for head in range(LANES // HD):
            mine = (lane >= head * HD) & (lane < (head + 1) * HD)
            query = jnp.where(mine, queries, 0.0).astype(jnp.bfloat16)
            scores = lax.dot_general(
                query, keys, (((1,), (1,)), ((), ())), preferred_element_type=jnp.float32
            )
            exponent = jnp.exp(scores - jnp.max(scores, axis=1, keepdims=True))
            row_sum = jnp.sum(exponent, axis=1, keepdims=True)
            mixed = jnp.dot(
                exponent.astype(jnp.bfloat16), values, preferred_element_type=jnp.float32
            )
            mixed = mixed / row_sum
            result = mixed if result is None else jnp.where(mine, mixed, result)
        joined[chip, piece] = result.astype(jnp.bfloat16)

    def hop(block_chip, piece, send, target):
        view = joined.at[block_chip, piece]
        return remote(
            view,
            view,
            send.at[block_chip, piece],
            join_recv.at[block_chip, piece],
            device(target, core),
        )

    def other_row_step(step):
        return lax.rem(row + step, rows)

    def hand_on(origin, piece, act):
        block_chip = origin * rows + row
        for step in range(1, rows):
            act(hop(block_chip, piece, cross_send, place * rows + other_row_step(step)))

        @pl.when((origin <= place) & (place < lines - 1))
        def _():
            act(hop(block_chip, piece, right_send, chip + rows))

        @pl.when((origin >= place) & (place > 0))
        def _():
            act(hop(block_chip, piece, left_send, chip - rows))

    def at_distance(distance, act):
        @pl.when(place >= distance)
        def _():
            act(place - distance)

        @pl.when(place + distance < lines)
        def _():
            act(place + distance)

    def arrive(block_chip, piece):
        view = joined.at[block_chip, piece]
        remote(
            view,
            view,
            cross_send.at[block_chip, piece],
            join_recv.at[block_chip, piece],
            device(chip, 1 - core),
        ).wait_recv()

    def relay(distance, piece):
        def act(origin):
            arrive(origin * rows + row, piece)
            hand_on(origin, piece, lambda copy: copy.start())

        at_distance(distance, act)

    for piece in range(pieces):
        from_section(chip, lambda ref, p=piece: own_copy(ref, p).wait())
        pass_on(chip, piece).start()
        for step in far_first:
            source = lax.rem(chip - step + chips, chips)
            remote(
                heads_own.at[source, piece],
                heads_own.at[source, piece],
                swap_send.at[step, piece],
                swap_recv.at[source, piece],
                device(source, core),
            ).wait_recv()
            pass_on(source, piece).start()
        for step in range(chips):
            pass_on(lax.rem(chip - step + chips, chips), piece).wait_recv()
        attention(piece)
        hand_on(place, piece, lambda copy: copy.start())
        for earlier in range(piece):
            distance = piece - earlier
            if distance < lines:
                relay(distance, earlier)

    join_load.wait()
    side.wait_recv()

    def project(block_chip):
        block_columns = pl.ds(pl.multiple_of(block_chip * width, LANES), width)
        total[...] += lax.dot_general(
            jnp.concatenate([joined[block_chip, p] for p in range(pieces)], axis=1),
            w_join[:, block_columns],
            (((1,), (1,)), ((), ())),
            preferred_element_type=jnp.float32,
        )

    total[...] = jnp.zeros_like(total)
    done = {p: pieces - 1 - p for p in range(pieces)}
    for distance in range(lines):
        for piece in range(pieces):
            if done[piece] < distance:
                relay(distance, piece)
        if distance == 0:
            project(chip)
        else:
            at_distance(distance, lambda origin: project(origin * rows + row))

    def cross(origin, step):
        block_chip = origin * rows + other_row_step(step)
        for piece in range(pieces):
            arrive(block_chip, piece)
        project(block_chip)

    for distance in range(lines):
        for step in range(1, rows):
            if distance == 0:
                cross(place, step)
            else:
                at_distance(distance, lambda origin, s=step: cross(origin, s))

    update_out[...] = total[...].reshape(chips, tokens, width).astype(jnp.bfloat16)

    def back(target, step):
        return remote(
            update_out.at[target],
            update_in.at[chip],
            back_send.at[step],
            back_recv.at[chip],
            device(target, core),
        )

    for step in far_first:
        back(lax.rem(chip + step, chips), step).start()
    own_back = pltpu.make_async_copy(update_out.at[chip], update_in.at[chip], load_sem.at[3])
    own_back.start()
    for step in range(1, chips):
        source = lax.rem(chip - step + chips, chips)
        remote(
            update_out.at[source],
            update_in.at[source],
            back_send.at[step],
            back_recv.at[source],
            device(source, core),
        ).wait_recv()
    for piece in range(pieces):
        for step in range(1, chips):
            swap(base_in, lax.rem(chip + step, chips), step, piece).wait_send()
        for source in range(chips):
            pass_on(source, piece).wait_send()
        for distance in range(lines):
            if distance == 0:
                hand_on(place, piece, lambda copy: copy.wait_send())
            else:
                at_distance(
                    distance, lambda o, p=piece: hand_on(o, p, lambda copy: copy.wait_send())
                )
    side.wait_send()
    terms_store.wait()
    own_back.wait()
    for step in range(1, chips):
        back(lax.rem(chip + step, chips), step).wait_send()


def finish_kernel(
    update_in,
    terms_in,
    hidden_in,
    latents_in,
    out_in,
    next_ref,
    velocity_ref,
    latents_ref,
    update,
    terms,
    hidden,
    latents,
    w_out,
    hidden_next,
    velocity_out,
    latents_next,
    load_sem,
    store_sem,
):
    loads = [
        pltpu.make_async_copy(source, target, load_sem.at[number])
        for number, (source, target) in enumerate(
            (
                (update_in, update),
                (hidden_in, hidden),
                (terms_in, terms),
                (out_in, w_out),
                (latents_in, latents),
            )
        )
    ]
    stores = [
        pltpu.make_async_copy(source, target, store_sem.at[number])
        for number, (source, target) in enumerate(
            (
                (hidden_next, next_ref),
                (velocity_out, velocity_ref),
                (latents_next, latents_ref),
            )
        )
    ]
    for load in loads:
        load.start()
    loads[0].wait()
    loads[1].wait()
    joined_columns = jnp.concatenate([update[p] for p in range(update.shape[0])], axis=1)
    summed = hidden[...].astype(jnp.float32) + joined_columns.astype(jnp.float32)
    hidden_next[...] = summed.astype(jnp.bfloat16)
    stores[0].start()
    average = jnp.mean(summed, axis=1, keepdims=True)
    centered = summed - average
    variance = jnp.mean(centered * centered, axis=1, keepdims=True)
    loads[2].wait()
    width = hidden.shape[1]
    shift_term = terms[0:1, :width]
    gain_term = terms[0:1, width:]
    normed = centered / jnp.sqrt(variance + 1e-05) * (1.0 + gain_term) + shift_term
    loads[3].wait()
    velocity = lax.dot_general(
        normed.astype(jnp.bfloat16),
        w_out[...],
        (((1,), (1,)), ((), ())),
        preferred_element_type=jnp.float32,
    )
    velocity_out[...] = velocity
    stores[1].start()
    loads[4].wait()
    latents_next[...] = latents[...] + terms[1:2, : latents.shape[1]] * velocity
    stores[2].start()
    for store in stores:
        store.wait()


def fused(plan, hidden, latents, base_qkv, control_qkv, step_index, w_join, w_mod, w_out):
    chips, rows, lines, width, pieces = plan
    tokens = hidden.shape[0]
    hbm_spec = pl.BlockSpec(memory_space=pltpu.HBM)
    dma = pltpu.SemaphoreType.DMA
    vmem_limit = 60 * 1024 * 1024
    per_piece = [dma((chips, pieces))] * 4
    update, terms = pl.pallas_call(
        functools.partial(fused_kernel, plan),
        out_shape=(
            jax.ShapeDtypeStruct((chips, tokens, width), jnp.bfloat16),
            jax.ShapeDtypeStruct((2, w_mod.shape[1]), jnp.float32),
        ),
        in_specs=[hbm_spec] * 2 + [pl.BlockSpec(memory_space=pltpu.SMEM)] + [hbm_spec] * 2,
        out_specs=(hbm_spec,) * 2,
        scratch_shapes=[
            pltpu.VMEM(w_mod.shape, jnp.bfloat16),
            pltpu.VMEM((2 * w_join.shape[1], w_join.shape[0]), jnp.bfloat16),
            pltpu.VMEM((2, w_mod.shape[1]), jnp.float32),
            pltpu.VMEM((chips, pieces, 3, tokens, LANES), jnp.bfloat16),
            pltpu.VMEM((chips, pieces, 2, tokens, LANES), jnp.bfloat16),
            pltpu.VMEM((chips, pieces, chips * tokens, LANES), jnp.bfloat16),
            pltpu.VMEM((chips * tokens, width), jnp.float32),
            pltpu.VMEM((chips, tokens, width), jnp.bfloat16),
            dma((4,)),
            dma((pieces,)),
            *per_piece,
            dma,
            dma,
            *per_piece,
            dma((chips,)),
            dma((chips,)),
        ],
        compiler_params=pltpu.CompilerParams(
            collective_id=0, has_side_effects=True, vmem_limit_bytes=vmem_limit
        ),
        name="fused",
    )(base_qkv, control_qkv, step_index, w_join.T, w_mod)
    return pl.pallas_call(
        finish_kernel,
        out_shape=(
            jax.ShapeDtypeStruct(hidden.shape, jnp.bfloat16),
            jax.ShapeDtypeStruct(latents.shape, jnp.float32),
            jax.ShapeDtypeStruct(latents.shape, jnp.float32),
        ),
        in_specs=[hbm_spec] * 5,
        out_specs=(hbm_spec,) * 3,
        scratch_shapes=[
            pltpu.VMEM(update.shape, jnp.bfloat16),
            pltpu.VMEM(terms.shape, jnp.float32),
            pltpu.VMEM(hidden.shape, jnp.bfloat16),
            pltpu.VMEM(latents.shape, jnp.float32),
            pltpu.VMEM(w_out.shape[::-1], jnp.bfloat16),
            pltpu.VMEM(hidden.shape, jnp.bfloat16),
            pltpu.VMEM(latents.shape, jnp.float32),
            pltpu.VMEM(latents.shape, jnp.float32),
            dma((5,)),
            dma((3,)),
        ],
        compiler_params=pltpu.CompilerParams(vmem_limit_bytes=vmem_limit),
        name="norm_and_step",
    )(update, terms, hidden, latents, w_out.T)


def plan_for(count, sections_width, section_width):
    if count % 4 != 0:
        return None
    chips = count // 2
    width = sections_width // chips
    if sections_width % chips or width % LANES or section_width % width:
        return None
    return (chips, 2, chips // 2, width, width // LANES)


def local(hidden, latents, base_qkv, control_qkv, step_index, w_join, w_mod, w_out, count):
    plan = plan_for(count, w_join.shape[0], base_qkv.shape[2])
    if plan is None or hidden.shape[0] % 8 or (plan[0] * hidden.shape[0]) % 16:
        return gathered(
            hidden, latents, base_qkv, control_qkv, step_index, w_join, w_mod, w_out
        )
    return fused(
        plan, hidden, latents, base_qkv, control_qkv, step_index, w_join, w_mod, w_out
    )


def solution(mesh):
    in_specs = (
        P(("groups", "seq"), None),
        P(("groups", "seq"), None),
        P(None, ("groups", "seq"), None),
        P(None, ("groups", "seq"), None),
        P(),
        P(None, "seq"),
        P(),
        P(),
    )
    out_specs = (P(("groups", "seq"), None), P(("groups", "seq"), None), P(("groups", "seq"), None))
    return jax.shard_map(
        functools.partial(local, count=mesh.shape["seq"]),
        mesh=mesh,
        in_specs=in_specs,
        out_specs=out_specs,
        check_vma=False,
    )
```
